128 devices in a mesh: dp: 8 (over x, core), seq: 16 (over z, y).
Axes of the slice: x: 4, y: 4, z: 4, core: 2. Of those that a mesh axis runs over, the one named last changes fastest.
Arguments:
- queries: bfloat16 [8, 16384, 768], P('dp', 'seq'), may hold values from -6 to 6
- latents: bfloat16 [8, 256, 1280], P('dp', 'seq'), may hold values from -6 to 6
- query_lengths: int32 [8, 68], P('dp'), may hold values from 1 to 2048, as said below
- q_weight: bfloat16 [768, 1280], replicated, may hold values from -0.3125 to 0.3125
- k_weight: bfloat16 [1280, 1280], replicated, may hold values from -0.15625 to 0.15625
- v_weight: bfloat16 [1280, 1280], replicated, may hold values from -0.15625 to 0.15625
- out_weight: bfloat16 [1280, 768], replicated, may hold values from -1.25 to 1.25
- up_weight: bfloat16 [768, 768], replicated, may hold values from -0.21875 to 0.21875
- down_weight: bfloat16 [768, 768], replicated, may hold values from -0.3125 to 0.3125
- gain_attn: float32 [768], replicated, may hold values from 0.1 to 1.9
- gain_mlp: float32 [768], replicated, may hold values from 0.1 to 1.9
- cotangent: bfloat16 [8, 16384, 768], P('dp', 'seq'), may hold values from -6 to 6
Outputs:
- block_out: bfloat16 [8, 16384, 768], P('dp', 'seq')
- query_grad: float32 [8, 16384, 768], P('dp', 'seq')
- latent_grad: float32 [8, 256, 1280], P('dp', 'seq')
- q_weight_grad: float32 [768, 1280], replicated
- k_weight_grad: float32 [1280, 1280], replicated
- v_weight_grad: float32 [1280, 1280], replicated
- out_weight_grad: float32 [1280, 768], replicated
- up_weight_grad: float32 [768, 768], replicated
- down_weight_grad: float32 [768, 768], replicated
- gain_attn_grad: float32 [768], replicated
- gain_mlp_grad: float32 [768], replicated
The draws below stay inside these ranges and needn't reach their ends.
Inputs may be any that keep to these rules, and one draw needn't show every extreme that they name: `query_lengths`: row e holds example e's item lengths: columns 0 to 3 the long items, from 256 to 2048, one of them equal to 2048 in every example; the other columns the short items, 1 to 128, one of them equal to 128 in every example.
All inputs are finite; a program needn't handle non-finite values.
Results may differ from the reference program's by a relative error of at most 0.018.
Values may be sent and summed in bfloat16 or wider, within the bound.
A program may use at most 192 MiB of HBM per device.

```python
import jax
import jax.numpy as jnp
from jax import lax

D = 768
DL = 1280
HEADS = 8
LAT = 256
FF = 768
SHORT_PAD = 128
QTOK = 16384
LONG_PAD = 2048
LONGS = 4
SHORTS = 64
N_DP = 8


def draw_query_lengths(key, part):
    key = jax.random.fold_in(key, 11)
    long_key, pick_key, short_key, full_key = jax.random.split(key, 4)
    long_length = jax.random.randint(long_key, (N_DP, LONGS), LONG_PAD // 8, LONG_PAD + 1)
    full_long = jax.random.randint(pick_key, (N_DP, 1), 0, LONGS)
    long_length = jnp.where(jnp.arange(LONGS)[None, :] == full_long, LONG_PAD, long_length)
    short_length = jax.random.randint(short_key, (N_DP, SHORTS), 1, SHORT_PAD + 1)
    full_item = jax.random.randint(full_key, (N_DP, 1), 0, SHORTS)
    short_length = jnp.where(jnp.arange(SHORTS)[None, :] == full_item, SHORT_PAD, short_length)
    return jnp.concatenate([long_length, short_length], axis=1).astype(jnp.int32)


def shard_levels(rng, shape, shards, low, top_value):
    def one(dim, shards_of):
        draws = jax.random.uniform(jax.random.fold_in(jax.random.fold_in(rng, 6), dim), (shards_of,), jnp.float32, low / len(shards), top_value / len(shards))
        return jnp.repeat(jnp.exp(draws), shape[dim] // shards_of).reshape((-1,) + (1,) * (len(shape) - dim - 1))

    level = one(*shards[0])
    for cut in shards[1:]:
        level = level * one(*cut)
    return level


def bell_draw(key, shape, deviation, most, shards=(), kind=jnp.bfloat16):
    entries = deviation * jax.random.normal(key, shape, jnp.float32)
    if shards:
        entries = entries * shard_levels(key, shape, shards, -0.22, 0.18)
    return jnp.clip(entries, -most, most).astype(kind)


def setup_inputs(seed: int = 0) -> dict:
    keys = jax.random.split(jax.random.key(seed), 13)
    queries = bell_draw(keys[0], (N_DP, QTOK, D), 1.0, 6.0, ((0, 8), (1, 16)))
    latents = bell_draw(keys[1], (N_DP, LAT, DL), 1.0, 6.0, ((0, 8), (1, 16)))
    query_lengths = draw_query_lengths(jax.random.fold_in(keys[12], 71), 0)
    q_weight = bell_draw(keys[3], (D, DL), (D // 2) ** -0.5, 0.3125)
    k_weight = bell_draw(keys[4], (DL, DL), DL ** -0.5, 0.15625)
    v_weight = bell_draw(keys[5], (DL, DL), DL ** -0.5, 0.15625)
    out_weight = bell_draw(keys[6], (DL, D), (DL // 64) ** -0.5, 1.25)
    up_weight = bell_draw(keys[7], (D, FF), D ** -0.5, 0.21875)
    down_weight = bell_draw(keys[8], (FF, D), (FF // 2) ** -0.5, 0.3125)
    gain_attn = jnp.clip(1.0 + 0.18 * jax.random.normal(keys[9], (D,), jnp.float32), 0.1, 1.9)
    gain_mlp = jnp.clip(1.0 + 0.18 * jax.random.normal(keys[10], (D,), jnp.float32), 0.1, 1.9)
    cotangent = bell_draw(keys[11], (N_DP, QTOK, D), 1.0, 6.0, ((0, 8), (1, 16)))
    return dict(queries=queries, latents=latents, query_lengths=query_lengths, q_weight=q_weight, k_weight=k_weight, v_weight=v_weight, out_weight=out_weight, up_weight=up_weight, down_weight=down_weight, gain_attn=gain_attn, gain_mlp=gain_mlp, cotangent=cotangent)


@jax.custom_vjp
def low(v):
    return lax.optimization_barrier(v.astype(jnp.bfloat16)).astype(jnp.float32)

@jax.custom_vjp
def low_back(v):
    return v

def low_keep(v):
    return (low(v), None)

def low_pass(kept, grad):
    return (grad,)

def back_keep(v):
    return (v, None)

def back_low(kept, grad):
    return (low(grad),)
low.defvjp(low_keep, low_pass)
low_back.defvjp(back_keep, back_low)
epsilon = 1e-05

def dot_high(left, right):
    return jnp.dot(left, right, precision=lax.Precision.HIGHEST, preferred_element_type=jnp.float32)

def norm_rows(values_in, gain):
    center = values_in - lax.optimization_barrier(jnp.mean(values_in, axis=-1, keepdims=True))
    spread = lax.optimization_barrier(jnp.mean(center * center, axis=-1, keepdims=True))
    return center * lax.rsqrt(spread + epsilon) * gain

def query_mask(lengths, total_rows):
    position = jnp.arange(total_rows, dtype=jnp.int32)
    half_rows = total_rows // 2
    in_long = position < half_rows
    short_position = jnp.maximum(position - half_rows, 0)
    item_index = jnp.where(in_long, position // LONG_PAD, LONGS + short_position // SHORT_PAD).astype(jnp.int32)
    offset = jnp.where(in_long, position % LONG_PAD, short_position % SHORT_PAD)
    return (offset < lengths[item_index]).astype(jnp.float32)

def example(example_rows, example_latents, example_mask, weights):
    q_weight, k_weight, v_weight, out_weight, up_weight, down_weight, gain_attn, gain_mlp = weights
    head_size = DL // HEADS
    first_norm = low(norm_rows(example_rows, gain_attn))
    query_low = low(low_back(dot_high(first_norm, q_weight) * head_size ** (-0.5)))
    key_rows = low(low_back(dot_high(example_latents, k_weight)))
    value_rows = low(low_back(dot_high(example_latents, v_weight)))
    head_query = query_low.reshape(-1, HEADS, head_size)
    head_keys = key_rows.reshape(-1, HEADS, head_size)
    head_values = value_rows.reshape(-1, HEADS, head_size)
    scores = low_back(jnp.einsum('qhd,khd->hqk', head_query, head_keys, precision=lax.Precision.HIGHEST))
    attention = jax.nn.softmax(scores, axis=-1)
    head_mixed = jnp.einsum('hqk,khd->qhd', low(attention), head_values, precision=lax.Precision.HIGHEST)
    mixed_low = low(low_back(head_mixed.reshape(-1, DL)))
    attn_out = low_back(dot_high(mixed_low, out_weight))
    residual = example_rows + attn_out
    second_norm = low(norm_rows(residual, gain_mlp))
    up_value = low_back(dot_high(second_norm, up_weight))
    activated_low = low(jax.nn.gelu(up_value, approximate=False))
    mlp_out = low_back(dot_high(activated_low, down_weight))
    return example_mask[:, None] * (residual + mlp_out)

def reference(queries, latents, query_lengths, q_weight, k_weight, v_weight, out_weight, up_weight, down_weight, gain_attn, gain_mlp, cotangent):
    row_masks = jax.vmap(lambda lengths: query_mask(lengths, queries.shape[1]))(query_lengths)

    def forward(query_float, latent_float, weights):

        def scan_step(carried, example_parts):
            example_rows, example_latents, example_mask = example_parts
            return (carried, jax.checkpoint(example)(example_rows, example_latents, example_mask, weights))
        _, outputs = lax.scan(scan_step, jnp.zeros((), jnp.float32), (query_float, latent_float, row_masks))
        return outputs
    weights = (q_weight.astype(jnp.float32), k_weight.astype(jnp.float32), v_weight.astype(jnp.float32), out_weight.astype(jnp.float32), up_weight.astype(jnp.float32), down_weight.astype(jnp.float32), gain_attn.astype(jnp.float32), gain_mlp.astype(jnp.float32))
    outputs, pullback = jax.vjp(forward, queries.astype(jnp.float32), latents.astype(jnp.float32), weights)
    grad_queries, grad_latents, grad_weights = pullback(cotangent.astype(jnp.float32))
    return (outputs.astype(jnp.bfloat16), grad_queries, grad_latents, grad_weights[0], grad_weights[1], grad_weights[2], grad_weights[3], grad_weights[4], grad_weights[5], grad_weights[6], grad_weights[7])
```

```python
import functools

import jax
import jax.numpy as jnp
from jax import lax
from jax.experimental import pallas as pl
from jax.experimental.pallas import tpu as pltpu
from jax.sharding import PartitionSpec as P

MESH = pl.DeviceIdType.MESH
F32 = jnp.float32
BF16 = jnp.bfloat16
HEADS = 8
HEAD = 160
LAT = 256
ROWS = 1024
TILE = 512
D = 768
DL = 1280
SCALE = HEAD ** (-0.5)
EPS = 1e-5
VMEM_LIMIT = 63 * 2**20


def dot(left, right, left_dim, right_dim):
    return lax.dot_general(
        left, right, (((left_dim,), (right_dim,)), ((), ())), preferred_element_type=F32
    )


class Place:
    def __init__(self):
        dp = lax.axis_index("dp")
        sq = lax.axis_index("seq")
        self.seq = sq
        self.dp = dp
        self.core = lax.rem(dp, 2)
        self.at = {"x": lax.div(dp, 2), "y": lax.rem(sq, 4), "z": lax.div(sq, 4)}

    def shifted(self, axis, step):
        return lax.rem(self.at[axis] + step, 4)

    def neighbour(self, axis, step):
        to = dict(self.at)
        to[axis] = self.shifted(axis, step)
        return (to["x"] * 2 + self.core, to["z"] * 4 + to["y"])

    def sibling(self):
        return (self.dp + 1 - 2 * self.core, self.seq)

    def in_seq(self, index):
        return (self.dp, index)


class Copies:
    def __init__(self, send, recv):
        self.send, self.recv, self.used, self.sent = send, recv, 0, []

    def start(self, src, dst, device):
        index = self.used
        self.used += 1
        copy = pltpu.make_async_remote_copy(
            src_ref=src,
            dst_ref=dst,
            send_sem=self.send.at[index],
            recv_sem=self.recv.at[index],
            device_id=device,
            device_id_type=MESH,
        )
        copy.start()
        self.sent.append(copy)
        return copy

    def drain(self):
        for copy in self.sent:
            copy.wait_send()


class Locals:
    def __init__(self, sems):
        self.sems, self.used = sems, 0

    def start(self, src, dst):
        copy = pltpu.make_async_copy(src, dst, self.sems.at[self.used])
        self.used += 1
        copy.start()
        return copy


AXES = ("x", "y", "z")


class SumSession:
    def __init__(self, place, copies, local, kind, width, part, rcore, ra, rb, rc, fin, out):
        self.p, self.copies, self.local = place, copies, local
        self.kind, self.width = kind, width
        self.part, self.rcore, self.ra, self.rb, self.rc, self.fin, self.out = part, rcore, ra, rb, rc, fin, out
        self.step_done = 0

    def region(self, i, c, a=None, b=None):
        if self.kind == "rows":
            row, high, col, wide = 256 * i + 128 * c, 128, 0, self.width
            if a is not None:
                row, high = row + 32 * a, 32
            if b is not None:
                row, high = row + 16 * lax.div(b, 2), 16
                wide = self.width // 2
                col = pl.multiple_of(lax.rem(b, 2) * wide, 128)
        else:
            row, high, col, wide = 640 * c, 640, 256 * i, 256
            if a is not None:
                row, high = row + 160 * a, 160
            if b is not None:
                row, high = row + 80 * lax.div(b, 2), 80
                wide = 128
                col = pl.multiple_of(256 * i + 128 * lax.rem(b, 2), 128)
        return pl.ds(pl.multiple_of(row, 16), high), pl.ds(col, wide)

    def axes(self, i):
        return AXES[i], AXES[(i + 1) % 3], AXES[(i + 2) % 3]

    def s0(self):
        other = 1 - self.p.core
        self.waits = [
            self.copies.start(self.part.at[self.region(i, other)], self.rcore.at[i], self.p.sibling())
            for i in range(3)
        ]

    def s1(self):
        c = self.p.core
        for i in range(3):
            self.waits[i].wait_recv()
            here = self.region(i, c)
            self.part[here] = self.part[here] + self.rcore[i]
        waits = []
        for i in range(3):
            axis = self.axes(i)[0]
            for k in range(3):
                to = self.p.shifted(axis, k + 1)
                waits.append(
                    self.copies.start(
                        self.part.at[self.region(i, c, to)], self.ra.at[i, k], self.p.neighbour(axis, k + 1)
                    )
                )
        self.waits = waits

    def s2(self):
        c = self.p.core
        for copy in self.waits:
            copy.wait_recv()
        waits = []
        for i in range(3):
            a_axis, b_axis, _ = self.axes(i)
            here = self.region(i, c, self.p.at[a_axis])
            total = self.part[here].astype(F32)
            for k in range(3):
                total = total + self.ra[i, k].astype(F32)
            self.part[here] = total.astype(BF16)
        for i in range(3):
            a_axis, b_axis, _ = self.axes(i)
            for k in range(3):
                to = self.p.shifted(b_axis, k + 1)
                waits.append(
                    self.copies.start(
                        self.part.at[self.region(i, c, self.p.at[a_axis], to)],
                        self.rb.at[i, k],
                        self.p.neighbour(b_axis, k + 1),
                    )
                )
        self.waits = waits

    def s3(self):
        c = self.p.core
        for copy in self.waits:
            copy.wait_recv()
        waits = []
        for i in range(3):
            a_axis, b_axis, c_axis = self.axes(i)
            total = self.part[self.region(i, c, self.p.at[a_axis], self.p.at[b_axis])].astype(F32)
            for k in range(3):
                total = total + self.rb[i, k].astype(F32)
            self.rc[i, pl.ds(self.p.at[c_axis], 1)] = total.astype(BF16)[None]
        for i in range(3):
            a_axis, b_axis, c_axis = self.axes(i)
            slot = self.rc.at[i, self.p.at[c_axis]]
            for k in range(3):
                waits.append(self.copies.start(slot, slot, self.p.neighbour(c_axis, k + 1)))
        self.waits = waits

    def s4(self):
        c = self.p.core
        for copy in self.waits:
            copy.wait_recv()
        waits, own = [], []
        for i in range(3):
            a_axis, b_axis, _ = self.axes(i)
            total = self.rc[i, 0].astype(F32)
            for k in range(1, 4):
                total = total + self.rc[i, k].astype(F32)
            self.fin[i] = total.astype(BF16)
        for i in range(3):
            a_axis, b_axis, _ = self.axes(i)
            there = self.out.at[self.region(i, c, self.p.at[a_axis], self.p.at[b_axis])]
            own.append(self.local.start(self.fin.at[i], there))
            for k in range(3):
                waits.append(self.copies.start(self.fin.at[i], there, self.p.neighbour(b_axis, k + 1)))
        self.waits, self.own = waits, own

    def s5(self):
        c = self.p.core
        for copy in self.waits:
            copy.wait_recv()
        for copy in self.own:
            copy.wait()
        waits = []
        for i in range(3):
            a_axis = self.axes(i)[0]
            there = self.out.at[self.region(i, c, self.p.at[a_axis])]
            for k in range(3):
                waits.append(self.copies.start(there, there, self.p.neighbour(a_axis, k + 1)))
        self.waits = waits

    def s6(self):
        for copy in self.waits:
            copy.wait_recv()
        self.waits = []
        for i in range(3):
            there = self.out.at[self.region(i, self.p.core)]
            self.waits.append(self.copies.start(there, there, self.p.sibling()))

    def s7(self):
        for copy in self.waits:
            copy.wait_recv()

    def step(self):
        getattr(self, "s%d" % self.step_done)()
        self.step_done += 1


class LatentSession:
    def __init__(self, place, copies, local, part, slots, send, recv, low, turned, turned_at, lat, half, rhalf, rx, fin, out):
        self.p, self.copies, self.local = place, copies, local
        self.part, self.slots, self.send, self.recv = part, slots, send, recv
        self.low, self.turned, self.turned_at, self.lat = low, turned, turned_at, lat
        self.half, self.rhalf, self.rx, self.fin, self.out = half, rhalf, rx, fin, out
        self.step_done = 0

    def copy_to(self, to):
        return pltpu.make_async_remote_copy(
            src_ref=self.part.at[pl.ds(pl.multiple_of(to * 80, 16), 80)],
            dst_ref=self.slots.at[self.p.seq],
            send_sem=self.send.at[to],
            recv_sem=self.recv.at[self.p.seq],
            device_id=self.p.in_seq(to),
            device_id_type=MESH,
        )

    def put(self, head, rows):
        self.part[pl.ds(pl.multiple_of(head * HEAD, 32), HEAD)] = rows.astype(BF16)
        for i in range(2):
            to = head * 2 + i

            @pl.when(to != self.p.seq)
            def _():
                self.copy_to(to).start()

            @pl.when(to == self.p.seq)
            def _():
                self.slots[pl.ds(to, 1)] = rows[80 * i : 80 * i + 80].astype(BF16)[None]

    def drain(self):
        for k in range(1, 16):
            self.copy_to(lax.rem(self.p.seq + k, 16)).wait_send()

    def s0(self):
        for k in range(1, 16):
            who = lax.rem(self.p.seq + k, 16)
            pltpu.make_async_remote_copy(
                src_ref=self.part.at[pl.ds(0, 80)],
                dst_ref=self.slots.at[who],
                send_sem=self.send.at[who],
                recv_sem=self.recv.at[who],
                device_id=self.p.in_seq(who),
                device_id_type=MESH,
            ).wait_recv()
        total = self.slots[0].astype(F32)
        for k in range(1, 16):
            total = total + self.slots[k].astype(F32)
        low = total.astype(BF16)
        self.low[...] = low
        product = dot(low, self.lat[...], 1, 0).astype(BF16)
        self.half[0] = product[:, :640]
        self.half[1] = product[:, 640:]
        self.waits = [self.copies.start(self.half.at[1 - self.p.core], self.rhalf, self.p.sibling())]
        self.turned[:, self.turned_at : self.turned_at + 80] = total.T

    def s1(self):
        self.waits[0].wait_recv()
        x = self.p.at["x"]
        self.rx[pl.ds(x, 1)] = self.half[pl.ds(self.p.core, 1)] + self.rhalf[...][None]
        slot = self.rx.at[x]
        self.waits = [self.copies.start(slot, slot, self.p.neighbour("x", k + 1)) for k in range(3)]

    def columns(self):
        return pl.ds(pl.multiple_of(640 * self.p.core, 128), 640)

    def s2(self):
        for copy in self.waits:
            copy.wait_recv()
        total = self.rx[0].astype(F32)
        for k in range(1, 4):
            total = total + self.rx[k].astype(F32)
        self.fin[...] = total.astype(BF16)
        y, z, cols = self.p.at["y"], self.p.at["z"], self.columns()
        self.own = [self.local.start(self.fin, self.out.at[z, y, :, cols])]
        self.waits = []
        for k in range(3):
            for axis, row, high in (("y", 0, 48), ("z", 48, 32)):
                self.waits.append(
                    self.copies.start(
                        self.fin.at[pl.ds(row, high)],
                        self.out.at[z, y, pl.ds(row, high), cols],
                        self.p.neighbour(axis, k + 1),
                    )
                )

    def s3(self):
        for copy in self.waits:
            copy.wait_recv()
        for copy in self.own:
            copy.wait()
        y, z, cols = self.p.at["y"], self.p.at["z"], self.columns()
        self.waits = []
        for k in range(3):
            first = self.out.at[z, :, pl.ds(0, 48), cols]
            second = self.out.at[:, y, pl.ds(48, 32), cols]
            self.waits.append(self.copies.start(first, first, self.p.neighbour("z", k + 1)))
            self.waits.append(self.copies.start(second, second, self.p.neighbour("y", k + 1)))

    def s4(self):
        for copy in self.waits:
            copy.wait_recv()
        there = self.out.at[:, :, :, self.columns()]
        self.waits = [self.copies.start(there, there, self.p.sibling())]

    def s5(self):
        for copy in self.waits:
            copy.wait_recv()

    def step(self):
        getattr(self, "s%d" % self.step_done)()
        self.step_done += 1


SUM_COPIES = 51
LATENT_COPIES = 17
N_LOCAL = 40


def main_kernel(
    lengths,
    gain1,
    gain2,
    queries,
    cotangent,
    latents,
    q_w,
    k_w,
    v_w,
    o_w,
    u_w,
    d_w,
    block_out,
    query_grad,
    latent_grad,
    g_du,
    g_o,
    g_q,
    g_k,
    g_v,
    qin,
    cin,
    lat,
    wq,
    wk,
    wv,
    wo,
    wu,
    wd,
    first,
    query,
    keys,
    values,
    att,
    mixed,
    resid,
    second,
    act,
    gup,
    gout,
    stats,
    gs,
    gcol,
    part_du,
    part_q,
    part_k,
    part_v,
    rcore_du,
    rcore_o,
    rcore_q,
    ra_du,
    ra_o,
    ra_q,
    rb_du,
    rb_o,
    rb_q,
    rc_du,
    rc_o,
    rc_q,
    fin_du,
    fin_o,
    fin_q,
    slots_k,
    slots_v,
    low_k,
    low_v,
    half_k,
    half_v,
    rhalf_k,
    rhalf_v,
    rx_k,
    rx_v,
    fin_k,
    fin_v,
    turned,
    turned_low,
    rturned,
    gathered_k,
    gathered_v,
    qg,
    du_send,
    du_recv,
    o_send,
    o_recv,
    q_send,
    q_recv,
    kk_send,
    kk_recv,
    vv_send,
    vv_recv,
    local_sem,
    lat_send,
    lat_recv,
    k_send,
    k_recv,
    v_send,
    v_recv,
    t_send,
    t_recv,
):
    p = Place()
    local = Locals(local_sem)
    load_q = [local.start(queries.at[pl.ds(TILE * j, TILE)], qin.at[pl.ds(TILE * j, TILE)]) for j in range(2)]
    load_wq = local.start(q_w, wq)
    load_own = local.start(latents, lat.at[pl.ds(pl.multiple_of(p.seq * 16, 16), 16)])
    load_c = local.start(cotangent, cin)
    load_wk = local.start(k_w, wk)
    load_wv = local.start(v_w, wv)
    load_wo = local.start(o_w, wo)
    load_wu = local.start(u_w, wu)
    load_wd = local.start(d_w, wd)

    barrier = pltpu.get_barrier_semaphore()
    for k in range(1, 16):
        pl.semaphore_signal(barrier, inc=1, device_id=p.in_seq(lax.rem(p.seq + k, 16)), device_id_type=MESH)
    for k in range(1, 4):
        pl.semaphore_signal(barrier, inc=1, device_id=p.neighbour("x", k), device_id_type=MESH)
    pl.semaphore_signal(barrier, inc=1, device_id=p.sibling(), device_id_type=MESH)
    pl.semaphore_wait(barrier, 19)

    load_own.wait()

    def lat_copy(who, slot):
        mine = lat.at[pl.ds(pl.multiple_of(slot * 16, 16), 16)]
        return pltpu.make_async_remote_copy(
            src_ref=mine,
            dst_ref=mine,
            send_sem=lat_send.at[who],
            recv_sem=lat_recv.at[slot],
            device_id=p.in_seq(who),
            device_id_type=MESH,
        )

    for k in range(1, 16):
        lat_copy(lax.rem(p.seq + k, 16), p.seq).start()

    turned[...] = jnp.zeros_like(turned)

    seq = p.seq
    is_long = (seq < 8).astype(jnp.int32)
    lane = lax.broadcasted_iota(jnp.int32, (1, 128), 1)
    for j in range(8):
        item = is_long * lax.div(seq, 2) + (1 - is_long) * (4 + (seq - 8) * 8 + j)
        offset = is_long * (lax.rem(seq, 2) * 1024 + 128 * j)
        stats[0:1, 128 * j : 128 * j + 128] = jnp.where(lane + offset < lengths[0, item], 1.0, 0.0).astype(F32)

    gcol[0] = jnp.broadcast_to(gain1[...], (128, D)).T
    gcol[1] = jnp.broadcast_to(gain2[...], (128, D)).T
    col1 = gcol[0][:, 0:1]
    col2 = gcol[1][:, 0:1]

    def normalized(x):
        center = x - jnp.mean(x, axis=0, keepdims=True)
        rstd = lax.rsqrt(jnp.mean(center * center, axis=0, keepdims=True) + EPS)
        return center * rstd, rstd

    tiles = [pl.ds(TILE * j, TILE) for j in range(2)]

    for j, t in enumerate(tiles):
        load_q[j].wait()
        x = qin[t, :].T.astype(F32)
        resid[:, t] = x
        n, _ = normalized(x)
        first[:, t] = (n * col1).astype(BF16)
        if j == 0:
            load_wq.wait()
        query[:, t] = (dot(wq[...], first[:, t], 0, 0) * SCALE).astype(BF16)
    load_c.wait()
    for j, t in enumerate(tiles):
        gout[:, t] = (stats[0:1, t] * cin[t, :].T.astype(F32)).astype(BF16)

    for k in range(1, 16):
        lat_copy(lax.rem(seq + k, 16), lax.rem(seq + k, 16)).wait_recv()
    load_wk.wait()
    keys[...] = dot(lat[...], wk[...], 1, 0).astype(BF16).T
    load_wv.wait()
    values[...] = dot(lat[...], wv[...], 1, 0).astype(BF16).T
    load_wo.wait()
    load_wu.wait()
    load_wd.wait()

    for t in tiles:
        for h in range(HEADS):
            r = pl.ds(HEAD * h, HEAD)
            s = dot(keys[r, :], query[r, t], 0, 0)
            e = jnp.exp(s - jnp.max(s, axis=0, keepdims=True))
            a = (e * (1.0 / jnp.sum(e, axis=0, keepdims=True))).astype(BF16)
            att[pl.ds(LAT * h, LAT), t] = a
            mixed[r, t] = dot(values[r, :], a, 1, 0).astype(BF16)
        x = resid[:, t] + dot(wo[...], mixed[:, t], 0, 0)
        resid[:, t] = x
        mu = jnp.mean(x, axis=0, keepdims=True)
        center = x - mu
        rstd = lax.rsqrt(jnp.mean(center * center, axis=0, keepdims=True) + EPS)
        stats[1:2, t] = mu
        stats[2:3, t] = rstd
        second[:, t] = (center * rstd * col2).astype(BF16)
        up = dot(wu[...], second[:, t], 0, 0)
        cdf = 0.5 * (1.0 + lax.erf(up * (0.5**0.5)))
        act[:, t] = (up * cdf).astype(BF16)
        slope = cdf + up * (jnp.exp(-0.5 * up * up) * 0.3989422804014327)
        gup[:, t] = (slope * dot(wd[...], gout[:, t], 1, 0)).astype(BF16)

    du = SumSession(p, Copies(du_send, du_recv), local, "rows", 1536, part_du, rcore_du, ra_du, rb_du, rc_du, fin_du, g_du)
    part_o = wk.at[:, pl.ds(0, D)]
    so = SumSession(p, Copies(o_send, o_recv), local, "cols", D, part_o, rcore_o, ra_o, rb_o, rc_o, fin_o, g_o)
    sq = SumSession(p, Copies(q_send, q_recv), local, "rows", DL, part_q, rcore_q, ra_q, rb_q, rc_q, fin_q, g_q)
    sk = LatentSession(
        p,
        Copies(kk_send, kk_recv),
        local,
        part_k,
        slots_k,
        k_send,
        k_recv,
        low_k,
        turned,
        0,
        lat,
        half_k,
        rhalf_k,
        rx_k,
        fin_k,
        g_k,
    )
    sv = LatentSession(
        p,
        Copies(vv_send, vv_recv),
        local,
        part_v,
        slots_v,
        v_send,
        v_recv,
        low_v,
        turned,
        128,
        lat,
        half_v,
        rhalf_v,
        rx_v,
        fin_v,
        g_v,
    )

    part_du[:, 0:D] = dot(act[...], gout[...], 1, 1).astype(BF16)
    part_du[:, D:] = dot(second[...], gup[...], 1, 1).astype(BF16)
    du.step()

    stores = []
    for j, t in enumerate(tiles):
        out = stats[0:1, t] * (resid[:, t] + dot(wd[...], act[:, t], 0, 0))
        cin[t, :] = out.astype(BF16).T
        stores.append(local.start(cin.at[t], block_out.at[t]))
        if j == 0:
            du.step()

    gal = act
    for j, t in enumerate(tiles):
        gg = dot(wu[...], gup[:, t], 1, 0) * col2
        rstd = stats[2:3, t]
        n = (resid[:, t] - stats[1:2, t]) * rstd
        mean_gg = jnp.mean(gg, axis=0, keepdims=True)
        mean_ggn = jnp.mean(gg * n, axis=0, keepdims=True)
        gr = gout[:, t].astype(F32) + rstd * (gg - mean_gg - n * mean_ggn)
        resid[:, t] = gr
        gal[:, t] = gr.astype(BF16)
    du.step()
    wk[:, 0:D] = dot(mixed[...], gal[...], 1, 1).astype(BF16)
    so.step()
    du.step()

    gm = wv.at[:, pl.ds(0, ROWS)]
    for j, t in enumerate(tiles):
        gm[:, t] = dot(wo[...], gal[:, t], 1, 0).astype(BF16)
        if j == 0:
            so.step()
    du.step()

    start = lax.div(seq, 2)

    def rows_of(i):
        h = lax.rem(start + i, HEADS)
        return h, pl.ds(pl.multiple_of(h * HEAD, 32), HEAD), pl.ds(pl.multiple_of(h * LAT, 256), LAT)

    def value_loop(low, high):
        @pl.loop(low, high)
        def _(i):
            h, r, l = rows_of(i)
            sv.put(h, dot(gm[r, :], att[l, :], 1, 1))

    value_loop(0, 4)
    so.step()
    value_loop(4, 8)
    du.step()

    def key_loop(low, high):
        @pl.loop(low, high)
        def _(i):
            h, r, l = rows_of(i)
            for t in tiles:
                ga = dot(values[r, :], gm[r, t], 0, 0)
                a = att[l, t].astype(F32)
                gs[:, t] = (a * (ga - jnp.sum(ga * a, axis=0, keepdims=True))).astype(BF16)
            sk.put(h, dot(query[r, :], gs[...], 1, 1))
            gm[r, :] = dot(keys[r, :], gs[...], 1, 0).astype(BF16)

    key_loop(0, 2)
    so.step()
    sv.step()
    key_loop(2, 4)
    du.step()
    so.step()
    sv.step()
    key_loop(4, 6)
    so.step()
    sv.step()
    key_loop(6, 8)
    so.step()
    sv.step()
    part_q[...] = (dot(first[...], gm[...], 1, 1) * SCALE).astype(BF16)
    sq.step()
    du.step()

    for j, t in enumerate(tiles):
        gg = dot(wq[...], gm[:, t], 1, 0) * (col1 * SCALE)
        n, rstd = normalized(qin[t, :].T.astype(F32))
        mean_gg = jnp.mean(gg, axis=0, keepdims=True)
        mean_ggn = jnp.mean(gg * n, axis=0, keepdims=True)
        total = (resid[:, t] + rstd * (gg - mean_gg - n * mean_ggn)).T
        if j == 1:
            stores.pop().wait()
        qg[...] = total
        stores.append(local.start(qg, query_grad.at[t]))
        if j == 0:
            sq.step()
            sk.step()
            sv.step()

    so.step()
    turned_low[...] = turned[...].astype(BF16)

    def turned_copy(who, slot):
        return pltpu.make_async_remote_copy(
            src_ref=turned_low.at[pl.ds(pl.multiple_of(who * 16, 16), 16)],
            dst_ref=rturned.at[slot],
            send_sem=t_send.at[who],
            recv_sem=t_recv.at[slot],
            device_id=p.in_seq(who),
            device_id_type=MESH,
        )

    for k in range(1, 16):
        turned_copy(lax.rem(seq + k, 16), seq).start()
    rturned[pl.ds(seq, 1)] = turned_low[pl.ds(pl.multiple_of(seq * 16, 16), 16), :][None]

    sk.step()
    sq.step()
    sv.step()
    sk.step()
    sq.step()
    so.copies.drain()
    load_wk = local.start(k_w, wk)
    load_wv = local.start(v_w, wv)
    sk.step()
    sq.step()
    for k in range(1, 16):
        turned_copy(lax.rem(seq + k, 16), lax.rem(seq + k, 16)).wait_recv()
    for s in range(16):
        block = rturned[s].astype(F32).T
        gathered_k[pl.ds(80 * s, 80), :] = block[0:80, :]
        gathered_v[pl.ds(80 * s, 80), :] = block[128:208, :]
    load_wk.wait()
    load_wv.wait()
    sk.step()
    sq.step()
    latent_grad[...] = dot(gathered_k[...].T.astype(BF16), wk[...], 1, 1) + dot(
        gathered_v[...].T.astype(BF16), wv[...], 1, 1
    )
    sk.step()
    sq.step()
    sq.step()
    for copy in stores:
        copy.wait()
    for k in range(1, 16):
        lat_copy(lax.rem(seq + k, 16), seq).wait_send()
        turned_copy(lax.rem(seq + k, 16), seq).wait_send()
    sk.drain()
    sv.drain()
    for session in (du, sq, sk, sv):
        session.copies.drain()
    assert [s.step_done for s in (du, so, sq, sk, sv)] == [8, 8, 8, 6, 6]


def convert_kernel(du, o, q, k, v, u_w, q_w, gain1, gain2, out_q, out_k, out_v, out_o, out_u, out_d, out_g1, out_g2):
    block = du[...].astype(F32)
    out_d[...] = block[:, :D]
    up = block[:, D:]
    out_u[...] = up
    qq = q[...].astype(F32)
    out_q[...] = qq
    out_o[...] = o[...].astype(F32)
    out_k[...] = k[...].T.astype(F32)
    out_v[...] = v[...].T.astype(F32)

    def as_row(column):
        return jnp.broadcast_to(column, (128, 128)).T[0:1, :]

    out_g2[...] = as_row(jnp.sum(up * u_w[...].astype(F32), axis=1, keepdims=True)) / gain2[...]
    out_g1[...] = as_row(jnp.sum(qq * q_w[...].astype(F32), axis=1, keepdims=True)) / gain1[...]


def vm(shape, dtype=BF16):
    return pltpu.VMEM(shape, dtype)


def on_device(queries, latents, lengths, q_w, k_w, v_w, o_w, u_w, d_w, gain1, gain2, cotangent):
    any_spec = pl.BlockSpec(memory_space=pl.ANY)
    vmem_spec = pl.BlockSpec(memory_space=pltpu.VMEM)
    dma = pltpu.SemaphoreType.DMA
    g1 = gain1.reshape(1, D)
    g2 = gain2.reshape(1, D)
    sds = jax.ShapeDtypeStruct
    outs = pl.pallas_call(
        main_kernel,
        out_shape=(
            sds((ROWS, D), BF16),
            sds((ROWS, D), F32),
            sds((16, DL), F32),
            sds((D, 1536), BF16),
            sds((DL, D), BF16),
            sds((D, DL), BF16),
            sds((4, 4, 80, DL), BF16),
            sds((4, 4, 80, DL), BF16),
        ),
        in_specs=[pl.BlockSpec(memory_space=pltpu.SMEM), vmem_spec, vmem_spec] + [any_spec] * 9,
        out_specs=(any_spec, any_spec, vmem_spec) + (any_spec,) * 5,
        scratch_shapes=[
            vm((ROWS, D)),
            vm((ROWS, D)),
            vm((LAT, DL)),
            vm((D, DL)),
            vm((DL, DL)),
            vm((DL, DL)),
            vm((DL, D)),
            vm((D, D)),
            vm((D, D)),
            vm((D, ROWS)),
            vm((DL, ROWS)),
            vm((DL, LAT)),
            vm((DL, LAT)),
            vm((HEADS * LAT, ROWS)),
            vm((DL, ROWS)),
            vm((D, ROWS), F32),
            vm((D, ROWS)),
            vm((D, ROWS)),
            vm((D, ROWS)),
            vm((D, ROWS)),
            vm((8, ROWS), F32),
            vm((LAT, ROWS)),
            vm((2, D, 128), F32),
            vm((D, 1536)),
            vm((D, DL)),
            vm((DL, LAT)),
            vm((DL, LAT)),
            vm((3, 128, 1536)),
            vm((3, 640, 256)),
            vm((3, 128, DL)),
            vm((3, 3, 32, 1536)),
            vm((3, 3, 160, 256)),
            vm((3, 3, 32, DL)),
            vm((3, 3, 16, 768)),
            vm((3, 3, 80, 128)),
            vm((3, 3, 16, 640)),
            vm((3, 4, 16, 768)),
            vm((3, 4, 80, 128)),
            vm((3, 4, 16, 640)),
            vm((3, 16, 768)),
            vm((3, 80, 128)),
            vm((3, 16, 640)),
            vm((16, 80, LAT)),
            vm((16, 80, LAT)),
            vm((80, LAT)),
            vm((80, LAT)),
            vm((2, 80, 640)),
            vm((2, 80, 640)),
            vm((80, 640)),
            vm((80, 640)),
            vm((4, 80, 640)),
            vm((4, 80, 640)),
            vm((80, 640)),
            vm((80, 640)),
            vm((LAT, 256), F32),
            vm((LAT, 256)),
            vm((16, 16, 256)),
            vm((DL, 16), F32),
            vm((DL, 16), F32),
            vm((TILE, D), F32),
        ]
        + [dma((SUM_COPIES,))] * 6
        + [dma((LATENT_COPIES,))] * 4
        + [
            dma((N_LOCAL,)),
        ]
        + [dma((16,))] * 8,
        compiler_params=pltpu.CompilerParams(
            collective_id=0, has_side_effects=True, vmem_limit_bytes=VMEM_LIMIT
        ),
        name="decoder_block",
    )(lengths, g1, g2, queries[0], cotangent[0], latents[0], q_w, k_w, v_w, o_w, u_w, d_w)
    block_out, query_grad, latent_grad, g_du, g_o, g_q, g_k, g_v = outs

    six = lambda i: (jnp.minimum(i, 5), 0)
    six_row = lambda i: (0, jnp.minimum(i, 5))
    conv = pl.pallas_call(
        convert_kernel,
        grid=(10,),
        out_shape=(
            sds((D, DL), F32),
            sds((DL, DL), F32),
            sds((DL, DL), F32),
            sds((DL, D), F32),
            sds((D, D), F32),
            sds((D, D), F32),
            sds((1, D), F32),
            sds((1, D), F32),
        ),
        in_specs=[
            pl.BlockSpec((128, 1536), six),
            pl.BlockSpec((128, D), lambda i: (i, 0)),
            pl.BlockSpec((128, DL), six),
            pl.BlockSpec((DL, 128), lambda i: (0, i)),
            pl.BlockSpec((DL, 128), lambda i: (0, i)),
            pl.BlockSpec((128, D), six),
            pl.BlockSpec((128, DL), six),
            pl.BlockSpec((1, 128), six_row),
            pl.BlockSpec((1, 128), six_row),
        ],
        out_specs=(
            pl.BlockSpec((128, DL), six),
            pl.BlockSpec((128, DL), lambda i: (i, 0)),
            pl.BlockSpec((128, DL), lambda i: (i, 0)),
            pl.BlockSpec((128, D), lambda i: (i, 0)),
            pl.BlockSpec((128, D), six),
            pl.BlockSpec((128, D), six),
            pl.BlockSpec((1, 128), six_row),
            pl.BlockSpec((1, 128), six_row),
        ),
        compiler_params=pltpu.CompilerParams(vmem_limit_bytes=VMEM_LIMIT),
        name="to_float32",
    )(g_du, g_o, g_q, g_k.reshape(DL, DL), g_v.reshape(DL, DL), u_w, q_w, g1, g2)
    q_grad, k_grad, v_grad, o_grad, u_grad, d_grad, g1_grad, g2_grad = conv
    return (
        block_out[None],
        query_grad[None],
        latent_grad[None],
        q_grad,
        k_grad,
        v_grad,
        o_grad,
        u_grad,
        d_grad,
        g1_grad.reshape(D),
        g2_grad.reshape(D),
    )


def solution(mesh):
    rows = P("dp", "seq", None)
    in_specs = (rows, rows, P("dp", None)) + (P(),) * 8 + (rows,)
    out_specs = (rows, rows, rows) + (P(),) * 8
    return jax.shard_map(on_device, mesh=mesh, in_specs=in_specs, out_specs=out_specs, check_vma=False)
```

```python
import functools

import jax
import jax.numpy as jnp
from jax import lax
from jax.experimental import pallas as pl
from jax.experimental.pallas import tpu as pltpu
from jax.sharding import PartitionSpec as P

MESH = pl.DeviceIdType.MESH
F32 = jnp.float32
BF16 = jnp.bfloat16
HEADS = 8
HEAD = 160
LAT = 256
ROWS = 1024
TILE = 512
D = 768
DL = 1280
SCALE = HEAD ** (-0.5)
EPS = 1e-5
VMEM_LIMIT = 63 * 2**20
ORDERS = {
    "du": ("xyz", "yzx", "zxy"),
    "o": ("xyz", "yzx", "zxy"),
    "q": ("xyz", "yzx", "zxy"),
}
PLAN = (
    "w0", "d", "b0", "b1", "m0", "d", "m1", "V0", "V1", "V2", "V3", "K0",
    "K1", "K2", "O0", "O1", "o", "v", "d", "K3", "g0", "g1", "o", "v",
    "Q0", "d", "v", "Q1", "q", "o", "k", "d", "q", "o", "d", "q",
    "v", "x0", "d", "o", "k", "x1", "q", "v", "k", "q", "B0", "o",
    "v", "k", "d", "v", "q", "R0", "o", "k", "v", "q", "k", "T0",
    "o", "d", "L0", "v", "B1", "k", "q", "k", "o", "q", "d", "k",
    "o", "q",
)


def dot(left, right, left_dim, right_dim):
    return lax.dot_general(
        left, right, (((left_dim,), (right_dim,)), ((), ())), preferred_element_type=F32
    )


class Place:
    def __init__(self):
        dp = lax.axis_index("dp")
        sq = lax.axis_index("seq")
        self.seq = sq
        self.dp = dp
        self.core = lax.rem(dp, 2)
        self.at = {"x": lax.div(dp, 2), "y": lax.rem(sq, 4), "z": lax.div(sq, 4)}

    def shifted(self, axis, step):
        return lax.rem(self.at[axis] + step, 4)

    def neighbour(self, axis, step):
        to = dict(self.at)
        to[axis] = self.shifted(axis, step)
        return (to["x"] * 2 + self.core, to["z"] * 4 + to["y"])

    def sibling(self):
        return (self.dp + 1 - 2 * self.core, self.seq)

    def in_seq(self, index):
        return (self.dp, index)


class Rounds:
    def __init__(self, place, send, recv):
        self.place, self.send, self.recv, self.size = place, send, recv, {}

    def copy(self, index, src, dst, device):
        return pltpu.make_async_remote_copy(
            src_ref=src,
            dst_ref=dst,
            send_sem=self.send.at[index],
            recv_sem=self.recv.at[index],
            device_id=device,
            device_id_type=MESH,
        )

    def start(self, index, src, dst, device):
        self.copy(index, src, dst, device).start()

    def wait(self, index, same_size):
        self.size[index] = same_size
        self.copy(index, same_size, same_size, self.place.sibling()).wait_recv()

    def drain(self, only=None):
        for index in list(self.size) if only is None else only:
            same_size = self.size.pop(index)
            self.copy(index, same_size, same_size, self.place.sibling()).wait_send()


class Locals:
    def __init__(self, sems):
        self.sems, self.used = sems, 0

    def start(self, src, dst):
        copy = pltpu.make_async_copy(src, dst, self.sems.at[self.used])
        self.used += 1
        copy.start()
        return copy


class SumSession:
    def __init__(self, place, rounds, local, kind, orders, width, part, rcore, relay, ra, rb, rc, fin, out):
        self.p, self.r, self.local = place, rounds, local
        self.kind, self.orders, self.width = kind, orders, width
        self.part, self.rcore, self.relay, self.ra, self.rb, self.rc = part, rcore, relay, ra, rb, rc
        self.fin, self.out = fin, out
        self.step_done = 0

    def region(self, i, c, a=None, b=None, half=None):
        if self.kind == "rows":
            row, high, col, wide = 256 * i + 128 * c, 128, 0, self.width
            if a is not None:
                row, high = row + 32 * a, 32
            if half is not None:
                row, high = row + 16 * half, 16
            if b is not None:
                row, high = row + 16 * lax.div(b, 2), 16
                wide = self.width // 2
                col = pl.multiple_of(lax.rem(b, 2) * wide, 128)
        else:
            row, high, col, wide = 640 * c, 640, 256 * i, 256
            if a is not None:
                row, high = row + 160 * a, 160
            if half is not None:
                row, high = row + 80 * half, 80
            if b is not None:
                row, high = row + 80 * lax.div(b, 2), 80
                wide = 128
                col = pl.multiple_of(256 * i + 128 * lax.rem(b, 2), 128)
        return pl.ds(pl.multiple_of(row, 16), high), pl.ds(col, wide)

    def here(self, i, *rest):
        return self.region(i, self.p.core, *rest)

    def axes(self, i):
        return self.orders[i]

    def s0(self):
        for i in range(3):
            self.r.start(0, self.part.at[self.region(i, 1 - self.p.core)], self.rcore.at[i], self.p.sibling())

    def s1(self):
        self.r.wait(0, self.rcore)
        for i in range(3):
            here = self.here(i)
            self.part[here] = self.part[here] + self.rcore[i]
        for i in range(3):
            axis = self.axes(i)[0]
            up, down = self.p.neighbour(axis, 1), self.p.neighbour(axis, 3)
            at = [self.p.shifted(axis, k) for k in range(4)]
            self.r.start(1, self.part.at[self.here(i, at[2], None, 0)], self.relay.at[i, 0], down)
            self.r.start(1, self.part.at[self.here(i, at[2], None, 1)], self.relay.at[i, 1], up)
            self.r.start(2, self.part.at[self.here(i, at[1], None, 0)], self.ra.at[i, 0], up)
            self.r.start(2, self.part.at[self.here(i, at[3], None, 1)], self.ra.at[i, 1], down)

    def s2(self):
        self.r.wait(1, self.relay)
        for i in range(3):
            axis = self.axes(i)[0]
            for half, k in ((0, 3), (1, 1)):
                there = self.here(i, self.p.shifted(axis, k), None, half)
                self.part[there] = self.part[there] + self.relay[i, half]
                self.r.start(2, self.part.at[there], self.ra.at[i, 2 + half], self.p.neighbour(axis, k))

    def s3(self):
        self.r.wait(2, self.ra)
        for i in range(3):
            a = self.p.at[self.axes(i)[0]]
            for half in range(2):
                here = self.here(i, a, None, half)
                total = self.part[here].astype(F32) + self.ra[i, half].astype(F32) + self.ra[i, 2 + half].astype(F32)
                self.part[here] = total.astype(BF16)
        for i in range(3):
            a_axis, b_axis, _ = self.axes(i)
            for k in range(3):
                to = self.p.shifted(b_axis, k + 1)
                self.r.start(
                    3,
                    self.part.at[self.here(i, self.p.at[a_axis], to)],
                    self.rb.at[i, k],
                    self.p.neighbour(b_axis, k + 1),
                )

    def s4(self):
        self.r.wait(3, self.rb)
        for i in range(3):
            a_axis, b_axis, c_axis = self.axes(i)
            total = self.part[self.here(i, self.p.at[a_axis], self.p.at[b_axis])].astype(F32)
            for k in range(3):
                total = total + self.rb[i, k].astype(F32)
            self.rc[i, pl.ds(self.p.at[c_axis], 1)] = total.astype(BF16)[None]
        for i in range(3):
            c_axis = self.axes(i)[2]
            slot = self.rc.at[i, self.p.at[c_axis]]
            for k in range(3):
                self.r.start(4, slot, slot, self.p.neighbour(c_axis, k + 1))

    def s5(self):
        self.r.wait(4, self.rb)
        self.own = []
        for i in range(3):
            total = self.rc[i, 0].astype(F32)
            for k in range(1, 4):
                total = total + self.rc[i, k].astype(F32)
            self.fin[i] = total.astype(BF16)
        for i in range(3):
            a_axis, b_axis, _ = self.axes(i)
            there = self.out.at[self.here(i, self.p.at[a_axis], self.p.at[b_axis])]
            self.own.append(self.local.start(self.fin.at[i], there))
            for k in range(3):
                self.r.start(5, self.fin.at[i], there, self.p.neighbour(b_axis, k + 1))

    def s6(self):
        self.r.wait(5, self.rb)
        for copy in self.own:
            copy.wait()
        for i in range(3):
            axis = self.axes(i)[0]
            there = self.out.at[self.here(i, self.p.at[axis])]
            for k in (1, 3):
                self.r.start(6, there, there, self.p.neighbour(axis, k))

    def s7(self):
        self.r.wait(6, self.ra)
        for i in range(3):
            axis = self.axes(i)[0]
            for half, k in ((0, 3), (1, 1)):
                there = self.out.at[self.here(i, self.p.shifted(axis, k), None, half)]
                self.r.start(7, there, there, self.p.neighbour(axis, 4 - k))

    def s8(self):
        self.r.wait(7, self.relay)
        for i in range(3):
            there = self.out.at[self.here(i)]
            self.r.start(8, there, there, self.p.sibling())

    def s9(self):
        self.r.wait(8, self.rcore)

    def step(self):
        getattr(self, "s%d" % self.step_done)()
        self.step_done += 1


class LatentSession:
    def __init__(self, place, rounds, local, first, other, part, slots, sums, slots2, turned, turned_at, lat, buffers, out):
        self.p, self.r, self.local, self.first, self.other = place, rounds, local, first, other
        self.part, self.slots, self.sums, self.slots2 = part, slots, sums, slots2
        self.turned, self.turned_at, self.lat, self.out = turned, turned_at, lat, out
        self.half, self.rhalf, self.ra, self.rb, self.rc, self.rd, self.fa, self.fb, self.fc, self.fd = buffers
        self.f, self.g = place.at[first], place.at[other]
        self.step_done = 0

    def rows(self, step):
        return pl.ds(pl.multiple_of(320 * self.p.shifted(self.first, step), 64), 320)

    def send(self, step):
        if step > 0:
            self.r.start(0, self.part.at[self.rows(step)], self.slots.at[step - 1], self.p.neighbour(self.first, step))

    def s0(self):
        self.r.wait(0, self.slots)
        total = self.part[self.rows(0)].astype(F32)
        for k in range(3):
            total = total + self.slots[k].astype(F32)
        for k in range(4):
            self.sums[k] = total[80 * k : 80 * k + 80].astype(BF16)
        for k in range(1, 4):
            to = self.p.shifted(self.other, k)
            self.r.start(1, self.sums.at[to], self.slots2.at[k - 1], self.p.neighbour(self.other, k))

    def s1(self):
        self.r.wait(1, self.slots2)
        total = self.sums[self.g].astype(F32)
        for k in range(3):
            total = total + self.slots2[k].astype(F32)
        product = dot(total.astype(BF16), self.lat[...].reshape(LAT, DL), 1, 0).astype(BF16)
        self.half[0] = product[:, :640]
        self.half[1] = product[:, 640:]
        self.r.start(2, self.half.at[1 - self.p.core], self.rhalf, self.p.sibling())
        self.turned[:, self.turned_at : self.turned_at + 80] = total.T

    def s2(self):
        self.r.wait(2, self.rhalf)
        x = self.p.at["x"]
        total = self.half[self.p.core] + self.rhalf[...]
        self.half[self.p.core] = total
        self.rb[pl.ds(x, 1)] = total[0:64, 256:512][None]
        self.rc[pl.ds(x, 1)] = total[0:64, 512:][None]
        self.rd[pl.ds(x, 1)] = total[64:80][None]
        for k in range(1, 4):
            rows = pl.ds(pl.multiple_of(16 * self.p.shifted("x", k), 16), 16)
            self.r.start(
                3, self.half.at[self.p.core, rows, pl.ds(0, 256)], self.ra.at[k - 1], self.p.neighbour("x", k)
            )
        for k in range(1, 4):
            for index, buf in ((4, self.rb), (5, self.rc), (6, self.rd)):
                self.r.start(index, buf.at[x], buf.at[x], self.p.neighbour("x", k))

    def columns(self, start, size):
        return pl.ds(pl.multiple_of(640 * self.p.core + start, 128), size)

    def a_part(self):
        return pl.ds(pl.multiple_of(16 * self.p.at["x"], 16), 16), self.columns(0, 256)

    def b_part(self):
        return pl.ds(0, 64), self.columns(256, 256)

    def c_part(self):
        return pl.ds(0, 64), self.columns(512, 128)

    def d_part(self):
        return pl.ds(64, 16), self.columns(0, 640)

    def same(self, index, *lead):
        rows, cols = ((16, 256), (64, 256), (64, 128), (16, 640))[index]
        return self.out.at[lead + (pl.ds(0, rows), pl.ds(0, cols))]

    def s3(self):
        three = pl.ds(0, 3)
        self.r.wait(3, self.ra)
        total = self.half[self.p.core, self.a_part()[0], 0:256].astype(F32)
        for k in range(3):
            total = total + self.ra[k].astype(F32)
        self.fa[...] = total.astype(BF16)
        for index, buf, fin in ((4, self.rb, self.fb), (5, self.rc, self.fc), (6, self.rd, self.fd)):
            self.r.wait(index, buf.at[three])
            total = buf[0].astype(F32)
            for k in range(1, 4):
                total = total + buf[k].astype(F32)
            fin[...] = total.astype(BF16)
        block = self.out.at[self.f, self.g]
        self.own = []
        for index, fin, part, axis in (
            (7, self.fa, self.a_part(), self.first),
            (9, self.fc, self.c_part(), self.other),
            (10, self.fd, self.d_part(), self.other),
            (8, self.fb, self.b_part(), self.first),
        ):
            there = block.at[part]
            self.own.append(self.local.start(fin, there))
            for k in range(1, 4):
                self.r.start(index, fin, there, self.p.neighbour(axis, k))

    def s4(self):
        three = pl.ds(0, 3)
        for index in range(4):
            self.r.wait(7 + index, self.same(index, 0, three))
        for copy in self.own:
            copy.wait()
        along_first, along_other = self.out.at[:, self.g], self.out.at[self.f]
        every = slice(None)
        for index, line, part, axis in (
            (11, along_first, self.a_part(), self.other),
            (13, along_other, self.c_part(), self.first),
            (14, along_other, self.d_part(), self.first),
            (12, along_first, self.b_part(), self.other),
        ):
            there = line.at[(every,) + part]
            for k in range(1, 4):
                self.r.start(index, there, there, self.p.neighbour(axis, k))

    def s5(self):
        self.r.wait(11, self.same(0, pl.ds(0, 3), slice(None)))
        there = self.out.at[(slice(None), slice(None)) + self.a_part()]
        for k in range(1, 4):
            self.r.start(15, there, there, self.p.neighbour("x", k))

    def s6(self):
        three, every = pl.ds(0, 3), slice(None)
        for index, part in ((1, self.b_part()), (2, self.c_part()), (3, self.d_part())):
            self.r.wait(11 + index, self.same(index, three, every))
            there = self.out.at[(every, every) + part]
            self.r.start(15 + index, there, there, self.p.sibling())

    def s7(self):
        every = slice(None)
        self.r.wait(15, self.out.at[:, :, pl.ds(0, 48), pl.ds(0, 256)])
        there = self.out.at[every, every, pl.ds(0, 64), self.columns(0, 256)]
        self.r.start(19, there, there, self.p.sibling())

    def s8(self):
        every = slice(None)
        for index in (1, 2, 3):
            self.r.wait(15 + index, self.same(index, every, every))
        self.r.wait(19, self.out.at[:, :, pl.ds(0, 64), pl.ds(0, 256)])

    def step(self):
        getattr(self, "s%d" % self.step_done)()
        self.step_done += 1


SUM_ROUNDS = 9
LATENT_ROUNDS = 20
N_LOCAL = 40


def main_kernel(
    lengths,
    gain1,
    gain2,
    queries,
    cotangent,
    latents,
    q_w,
    k_w,
    v_w,
    o_w,
    u_w,
    d_w,
    block_out,
    query_grad,
    latent_grad,
    g_du,
    g_o,
    g_q,
    g_k,
    g_v,
    qin,
    cin,
    lat,
    wq,
    wk,
    wv,
    wo,
    wu,
    wd,
    first,
    query,
    keys,
    values,
    att,
    mixed,
    resid,
    second,
    act,
    gup,
    gout,
    stats,
    gcol,
    part_du,
    part_q,
    part_k,
    part_v,
    rcore_du,
    rcore_o,
    rcore_q,
    relay_du,
    relay_o,
    relay_q,
    ra_du,
    ra_o,
    ra_q,
    rb_du,
    rb_o,
    rb_q,
    rc_du,
    rc_o,
    rc_q,
    fin_du,
    fin_o,
    fin_q,
    slots_k,
    slots_v,
    sums_k,
    sums_v,
    slots2_k,
    slots2_v,
    *rest,
):
    buffers_k, buffers_v = rest[0:10], rest[10:20]
    (
        turned,
        turned_low,
        rturned,
        gathered_k,
        gathered_v,
        du_send,
        du_recv,
        o_send,
        o_recv,
        q_send,
        q_recv,
        k_send,
        k_recv,
        v_send,
        v_recv,
        a_send,
        a_recv,
        local_sem,
    ) = rest[20:]
    p = Place()
    local = Locals(local_sem)
    load_q = [local.start(queries.at[pl.ds(TILE * j, TILE)], qin.at[pl.ds(TILE * j, TILE)]) for j in range(2)]
    z, y = p.at["z"], p.at["y"]
    load_own = local.start(latents, lat.at[z, y])
    load_wq = local.start(q_w, wq)

    barrier = pltpu.get_barrier_semaphore()
    for k in range(1, 16):
        pl.semaphore_signal(barrier, inc=1, device_id=p.in_seq(lax.rem(p.seq + k, 16)), device_id_type=MESH)
    for k in range(1, 4):
        pl.semaphore_signal(barrier, inc=1, device_id=p.neighbour("x", k), device_id_type=MESH)
    pl.semaphore_signal(barrier, inc=1, device_id=p.sibling(), device_id_type=MESH)

    seq = p.seq
    is_long = (seq < 8).astype(jnp.int32)
    lane = lax.broadcasted_iota(jnp.int32, (1, 128), 1)
    for j in range(8):
        item = is_long * lax.div(seq, 2) + (1 - is_long) * (4 + (seq - 8) * 8 + j)
        offset = is_long * (lax.rem(seq, 2) * 1024 + 128 * j)
        stats[0:1, 128 * j : 128 * j + 128] = jnp.where(lane + offset < lengths[0, item], 1.0, 0.0).astype(F32)

    gcol[0] = jnp.broadcast_to(gain1[...].reshape(1, D), (128, D)).T
    gcol[1] = jnp.broadcast_to(gain2[...].reshape(1, D), (128, D)).T
    col1 = gcol[0][:, 0:1]
    col2 = gcol[1][:, 0:1]
    turned[...] = jnp.zeros_like(turned)

    def normalized(x):
        center = x - jnp.mean(x, axis=0, keepdims=True)
        rstd = lax.rsqrt(jnp.mean(center * center, axis=0, keepdims=True) + EPS)
        return center * rstd, rstd

    tiles = [pl.ds(TILE * j, TILE) for j in range(2)]

    def first_part(j):
        t = tiles[j]
        load_q[j].wait()
        x = qin[t, :].T.astype(F32)
        resid[:, t] = x
        n, _ = normalized(x)
        first[:, t] = (n * col1).astype(BF16)

    load_c = local.start(cotangent, cin)
    load_wd = local.start(d_w, wd)
    load_wk = local.start(k_w, wk)
    load_wv = local.start(v_w, wv)
    load_wo = local.start(o_w, wo)
    load_wu = local.start(u_w, wu)
    first_part(0)
    load_own.wait()
    pl.semaphore_wait(barrier, 19)

    early = Rounds(p, a_send, a_recv)
    left, right = pl.ds(0, 640), pl.ds(640, 640)
    for k in range(1, 4):
        early.start(0, lat.at[z, y, :, left], lat.at[z, y, :, left], p.neighbour("y", k))
        early.start(0, lat.at[z, y, :, right], lat.at[z, y, :, right], p.neighbour("z", k))

    def latents_on():
        early.wait(0, lat.at[0, pl.ds(0, 3)])
        for k in range(1, 4):
            early.start(1, lat.at[z, :, :, left], lat.at[z, :, :, left], p.neighbour("z", k))
            early.start(1, lat.at[:, y, :, right], lat.at[:, y, :, right], p.neighbour("y", k))

    first_part(1)
    load_wq.wait()
    for j, t in enumerate(tiles):
        query[:, t] = (dot(wq[...], first[:, t], 0, 0) * SCALE).astype(BF16)
        if j == 0:
            latents_on()
    load_c.wait()
    load_wd.wait()
    for t in tiles:
        gout[:, t] = (stats[0:1, t] * cin[t, :].T.astype(F32)).astype(BF16)
        gup[:, t] = dot(wd[...], gout[:, t], 1, 0).astype(BF16)

    early.wait(1, lat.at[pl.ds(0, 3)])
    all_latents = lat[...].reshape(LAT, DL)
    load_wk.wait()
    keys[...] = dot(all_latents, wk[...], 1, 0).astype(BF16).T
    load_wv.wait()
    values[...] = dot(all_latents, wv[...], 1, 0).astype(BF16).T
    load_wo.wait()
    load_wu.wait()

    def mix(h):
        r = pl.ds(HEAD * h, HEAD)
        mixed[r, :] = dot(values[r, :], att[pl.ds(LAT * h, LAT), :], 1, 0).astype(BF16)

    for h in range(HEADS):
        r = pl.ds(HEAD * h, HEAD)
        for t in tiles:
            s = dot(keys[r, :], query[r, t], 0, 0)
            e = jnp.exp(s - jnp.max(s, axis=0, keepdims=True))
            att[pl.ds(LAT * h, LAT), t] = (e * (1.0 / jnp.sum(e, axis=0, keepdims=True))).astype(BF16)
        if h > 0:
            mix(h - 1)
    mix(HEADS - 1)
    for t in tiles:
        x = resid[:, t] + dot(wo[...], mixed[:, t], 0, 0)
        resid[:, t] = x
        mu = jnp.mean(x, axis=0, keepdims=True)
        center = x - mu
        rstd = lax.rsqrt(jnp.mean(center * center, axis=0, keepdims=True) + EPS)
        stats[1:2, t] = mu
        stats[2:3, t] = rstd
        second[:, t] = (center * rstd * col2).astype(BF16)
        up = dot(wu[...], second[:, t], 0, 0)
        cdf = 0.5 * (1.0 + lax.erf(up * (0.5**0.5)))
        act[:, t] = (up * cdf).astype(BF16)
        slope = cdf + up * (jnp.exp(-0.5 * up * up) * 0.3989422804014327)
        gup[:, t] = (slope * gup[:, t].astype(F32)).astype(BF16)

    part_o = wk.at[:, pl.ds(0, D)]
    du = SumSession(
        p,
        Rounds(p, du_send, du_recv),
        local,
        "rows",
        ORDERS["du"],
        1536,
        part_du,
        rcore_du,
        relay_du,
        ra_du,
        rb_du,
        rc_du,
        fin_du,
        g_du,
    )
    so = SumSession(
        p,
        Rounds(p, o_send, o_recv),
        local,
        "cols",
        ORDERS["o"],
        D,
        part_o,
        rcore_o,
        relay_o,
        ra_o,
        rb_o,
        rc_o,
        fin_o,
        g_o,
    )
    sq = SumSession(
        p,
        Rounds(p, q_send, q_recv),
        local,
        "rows",
        ORDERS["q"],
        DL,
        part_q,
        rcore_q,
        relay_q,
        ra_q,
        rb_q,
        rc_q,
        fin_q,
        g_q,
    )
    sk = LatentSession(
        p,
        Rounds(p, k_send, k_recv),
        local,
        "y",
        "z",
        part_k,
        slots_k,
        sums_k,
        slots2_k,
        turned,
        0,
        lat,
        buffers_k,
        g_k,
    )
    sv = LatentSession(
        p,
        Rounds(p, v_send, v_recv),
        local,
        "z",
        "y",
        part_v,
        slots_v,
        sums_v,
        slots2_v,
        turned,
        128,
        lat,
        buffers_v,
        g_v,
    )
    gal = second
    gm = wv.at[:, pl.ds(0, ROWS)]
    stores = []

    def heads_of(axis, j):
        for i in range(2):
            h = 2 * p.shifted(axis, j) + i
            yield pl.ds(pl.multiple_of(h * HEAD, 32), HEAD), pl.ds(pl.multiple_of(h * LAT, 256), LAT)

    def mlp_back(j):
        t = tiles[j]
        gg = dot(wu[...], gup[:, t], 1, 0) * col2
        rstd = stats[2:3, t]
        n = (resid[:, t] - stats[1:2, t]) * rstd
        mean_gg = jnp.mean(gg, axis=0, keepdims=True)
        mean_ggn = jnp.mean(gg * n, axis=0, keepdims=True)
        gal[:, t] = (gout[:, t].astype(F32) + rstd * (gg - mean_gg - n * mean_ggn)).astype(BF16)

    def mixed_back(j):
        gm[:, tiles[j]] = dot(wo[...], gal[:, tiles[j]], 1, 0).astype(BF16)

    def value_heads(j):
        for r, l in heads_of("z", j):
            part_v[r, :] = dot(gm[r, :], att[l, :], 1, 1).astype(BF16)
        sv.send(j)

    def key_heads(j):
        for r, l in heads_of("y", j):
            for t in tiles:
                ga = dot(values[r, :], gm[r, t], 0, 0)
                a = att[l, t].astype(F32)
                att[l, t] = (a * (ga - jnp.sum(ga * a, axis=0, keepdims=True))).astype(BF16)
            part_k[r, :] = dot(query[r, :], att[l, :], 1, 1).astype(BF16)
        sk.send(j)

    def query_back(j):
        for h in range(4 * j, 4 * j + 4):
            r = pl.ds(h * HEAD, HEAD)
            gm[r, :] = dot(keys[r, :], att[pl.ds(h * LAT, LAT), :], 1, 0).astype(BF16)

    def query_weight(j):
        c = pl.ds(640 * j, 640)
        part_q[:, c] = (dot(first[...], gm[c, :], 1, 1) * SCALE).astype(BF16)

    def out_weight(j):
        c = pl.ds(640 * j, 640)
        wk[c, 0:D] = dot(mixed[c, :], gal[...], 1, 1).astype(BF16)

    def query_out(j):
        t = tiles[j]
        gg = dot(wq[...], gm[:, t], 1, 0) * (col1 * SCALE)
        n, rstd = normalized(qin[t, :].T.astype(F32))
        mean_gg = jnp.mean(gg, axis=0, keepdims=True)
        mean_ggn = jnp.mean(gg * n, axis=0, keepdims=True)
        total = gal[:, t].astype(F32) + rstd * (gg - mean_gg - n * mean_ggn)
        qin[t, :] = total.astype(BF16).T
        stores.append(local.start(qin.at[t], query_grad.at[t]))

    def block(j):
        t = tiles[j]
        out = stats[0:1, t] * (resid[:, t] + dot(wd[...], act[:, t], 0, 0))
        cin[t, :] = out.astype(BF16).T
        stores.append(local.start(cin.at[t], block_out.at[t]))

    def turn_send(j):
        turned_low[...] = turned[...].astype(BF16)
        for k in range(1, 16):
            who = lax.rem(seq + k, 16)
            mine = turned_low.at[pl.ds(pl.multiple_of(who * 16, 16), 16)]
            early.start(2, mine, rturned.at[seq], p.in_seq(who))
        rturned[pl.ds(seq, 1)] = turned_low[pl.ds(pl.multiple_of(seq * 16, 16), 16), :][None]

    reload = []

    def load_again(j):
        so.r.drain((0, 1, 2, 3))
        reload.append(local.start(k_w, wk))
        reload.append(local.start(v_w, wv))

    def latent_back(j):
        early.wait(2, rturned.at[pl.ds(0, 15)])
        for i in range(16):
            piece = rturned[i].astype(F32).T
            gathered_k[pl.ds(80 * (4 * (i % 4) + i // 4), 80), :] = piece[0:80, :]
            gathered_v[pl.ds(80 * i, 80), :] = piece[128:208, :]
        for load in reload:
            load.wait()
        latent_grad[...] = dot(gathered_k[...].T.astype(BF16), wk[...], 1, 1) + dot(
            gathered_v[...].T.astype(BF16), wv[...], 1, 1
        )

    def down_up(j):
        part_du[:, 0:D] = dot(act[...], gout[...], 1, 1).astype(BF16)
        part_du[:, D:] = dot(second[...], gup[...], 1, 1).astype(BF16)

    parts = {
        "w": down_up,
        "b": mlp_back,
        "m": mixed_back,
        "V": value_heads,
        "K": key_heads,
        "g": query_back,
        "Q": query_weight,
        "O": out_weight,
        "x": query_out,
        "B": block,
        "T": turn_send,
        "R": load_again,
        "L": latent_back,
    }
    sessions = {"d": du, "o": so, "q": sq, "k": sk, "v": sv}
    for item in PLAN:
        if item in sessions:
            sessions[item].step()
        else:
            parts[item[0]](int(item[1]))
    for copy in stores:
        copy.wait()
    early.drain()
    for session in (du, so, sq, sk, sv):
        session.r.drain()
    assert [s.step_done for s in (du, so, sq, sk, sv)] == [10, 10, 10, 9, 9]


def convert_kernel(
    gain1,
    gain2,
    du,
    o,
    q,
    k,
    v,
    u_w,
    q_w,
    block,
    query,
    out_q,
    out_k,
    out_v,
    out_o,
    out_u,
    out_d,
    out_block,
    out_query,
    out_g1,
    out_g2,
    b_du,
    b_o,
    b_q,
    b_k,
    b_v,
    b_uw,
    b_qw,
    b_query,
    b_block,
    f_q,
    f_k,
    f_v,
    f_o,
    f_u,
    f_d,
    f_query,
    sems_in,
    sems_out,
):
    loads, stores = Locals(sems_in), Locals(sems_out)
    jobs = []
    for j in range(5):
        c = pl.ds(256 * j, 256)
        for src, buf, wide, out in ((k, b_k, f_k, out_k), (v, b_v, f_v, out_v)):
            jobs.append((loads.start(src.at[:, c], buf.at[:, c]), "turn", buf, wide, out, c))
    for j in range(4):
        r = pl.ds(320 * j, 320)
        jobs.append((loads.start(o.at[r], b_o.at[r]), "plain", b_o, f_o, out_o, r))
    load_qw = loads.start(q_w, b_qw)
    load_uw = loads.start(u_w, b_uw)
    for j in range(3):
        r = pl.ds(256 * j, 256)
        jobs.append((loads.start(q.at[r], b_q.at[r]), "q", b_q, f_q, out_q, r))
    for j in range(3):
        r = pl.ds(256 * j, 256)
        jobs.append((loads.start(du.at[r], b_du.at[r]), "du", b_du, None, None, r))
    for j in range(2):
        r = pl.ds(512 * j, 512)
        jobs.append((loads.start(query.at[r], b_query.at[r]), "plain", b_query, f_query, out_query, r))
    load_block = loads.start(block, b_block)
    pending = []

    def per_row(product, gain):
        total = jnp.sum(product, axis=1, keepdims=True)
        return (jnp.broadcast_to(total, (256, 128)).T[0:1, :] / gain.reshape(1, 256)).reshape(256)

    load_qw.wait()
    load_uw.wait()
    load_block.wait()
    pending.append(stores.start(b_block, out_block))
    for load, kind, buf, wide, out, r in jobs:
        load.wait()
        if kind == "turn":
            wide[r, :] = buf[:, r].T.astype(F32)
        elif kind == "du":
            f_d[r, :] = buf[r, 0:D].astype(F32)
            up = buf[r, D:].astype(F32)
            f_u[r, :] = up
            out_g2[r] = per_row(up * b_uw[r, :].astype(F32), gain2[r])
            pending.append(stores.start(f_d.at[r], out_d.at[r]))
            pending.append(stores.start(f_u.at[r], out_u.at[r]))
            continue
        else:
            value = buf[r, :].astype(F32)
            wide[r, :] = value
            if kind == "q":
                out_g1[r] = per_row(value * b_qw[r, :].astype(F32), gain1[r])
        pending.append(stores.start(wide.at[r], out.at[r]))
    for copy in pending:
        copy.wait()


def vm(shape, dtype=BF16):
    return pltpu.VMEM(shape, dtype)


def on_device(queries, latents, lengths, q_w, k_w, v_w, o_w, u_w, d_w, gain1, gain2, cotangent):
    any_spec = pl.BlockSpec(memory_space=pl.ANY)
    vmem_spec = pl.BlockSpec(memory_space=pltpu.VMEM)
    dma = pltpu.SemaphoreType.DMA
    sds = jax.ShapeDtypeStruct
    outs = pl.pallas_call(
        main_kernel,
        out_shape=(
            sds((ROWS, D), BF16),
            sds((ROWS, D), BF16),
            sds((16, DL), F32),
            sds((D, 1536), BF16),
            sds((DL, D), BF16),
            sds((D, DL), BF16),
            sds((4, 4, 80, DL), BF16),
            sds((4, 4, 80, DL), BF16),
        ),
        in_specs=[pl.BlockSpec(memory_space=pltpu.SMEM), vmem_spec, vmem_spec] + [any_spec] * 9,
        out_specs=(any_spec, any_spec, vmem_spec) + (any_spec,) * 5,
        scratch_shapes=[
            vm((ROWS, D)),
            vm((ROWS, D)),
            vm((4, 4, 16, DL)),
            vm((D, DL)),
            vm((DL, DL)),
            vm((DL, DL)),
            vm((DL, D)),
            vm((D, D)),
            vm((D, D)),
            vm((D, ROWS)),
            vm((DL, ROWS)),
            vm((DL, LAT)),
            vm((DL, LAT)),
            vm((HEADS * LAT, ROWS)),
            vm((DL, ROWS)),
            vm((D, ROWS), F32),
            vm((D, ROWS)),
            vm((D, ROWS)),
            vm((D, ROWS)),
            vm((D, ROWS)),
            vm((8, ROWS), F32),
            vm((2, D, 128), F32),
            vm((D, 1536)),
            vm((D, DL)),
            vm((DL, LAT)),
            vm((DL, LAT)),
            vm((3, 128, 1536)),
            vm((3, 640, 256)),
            vm((3, 128, DL)),
            vm((3, 2, 16, 1536)),
            vm((3, 2, 80, 256)),
            vm((3, 2, 16, DL)),
            vm((3, 4, 16, 1536)),
            vm((3, 4, 80, 256)),
            vm((3, 4, 16, DL)),
            vm((3, 3, 16, 768)),
            vm((3, 3, 80, 128)),
            vm((3, 3, 16, 640)),
            vm((3, 4, 16, 768)),
            vm((3, 4, 80, 128)),
            vm((3, 4, 16, 640)),
            vm((3, 16, 768)),
            vm((3, 80, 128)),
            vm((3, 16, 640)),
            vm((3, 320, LAT)),
            vm((3, 320, LAT)),
            vm((4, 80, LAT)),
            vm((4, 80, LAT)),
            vm((3, 80, LAT)),
            vm((3, 80, LAT)),
        ]
        + [
            vm((2, 80, 640)),
            vm((80, 640)),
            vm((3, 16, 256)),
            vm((4, 64, 256)),
            vm((4, 64, 128)),
            vm((4, 16, 640)),
            vm((16, 256)),
            vm((64, 256)),
            vm((64, 128)),
            vm((16, 640)),
        ]
        * 2
        + [
            vm((LAT, 256), F32),
            vm((LAT, 256)),
            vm((16, 16, 256)),
            vm((DL, 16), F32),
            vm((DL, 16), F32),
        ]
        + [dma((SUM_ROUNDS,))] * 6
        + [dma((LATENT_ROUNDS,))] * 4
        + [dma((3,)), dma((3,)), dma((N_LOCAL,))],
        compiler_params=pltpu.CompilerParams(
            collective_id=0, has_side_effects=True, vmem_limit_bytes=VMEM_LIMIT
        ),
        name="decoder_block",
    )(lengths, gain1, gain2, queries[0], cotangent[0], latents[0], q_w, k_w, v_w, o_w, u_w, d_w)
    block_out, query_grad, latent_grad, g_du, g_o, g_q, g_k, g_v = outs

    conv = pl.pallas_call(
        convert_kernel,
        out_shape=(
            sds((D, DL), F32),
            sds((DL, DL), F32),
            sds((DL, DL), F32),
            sds((DL, D), F32),
            sds((D, D), F32),
            sds((D, D), F32),
            sds((ROWS, D), BF16),
            sds((ROWS, D), F32),
            sds((D,), F32),
            sds((D,), F32),
        ),
        in_specs=[vmem_spec, vmem_spec] + [any_spec] * 9,
        out_specs=(any_spec,) * 8 + (vmem_spec, vmem_spec),
        scratch_shapes=[
            vm((D, 1536)),
            vm((DL, D)),
            vm((D, DL)),
            vm((DL, DL)),
            vm((DL, DL)),
            vm((D, D)),
            vm((D, DL)),
            vm((ROWS, D)),
            vm((ROWS, D)),
            vm((D, DL), F32),
            vm((DL, DL), F32),
            vm((DL, DL), F32),
            vm((DL, D), F32),
            vm((D, D), F32),
            vm((D, D), F32),
            vm((ROWS, D), F32),
            dma((32,)),
            dma((32,)),
        ],
        compiler_params=pltpu.CompilerParams(vmem_limit_bytes=VMEM_LIMIT),
        name="to_float32",
    )(
        gain1,
        gain2,
        g_du,
        g_o,
        g_q,
        g_k.reshape(DL, DL),
        g_v.reshape(DL, DL),
        u_w,
        q_w,
        block_out,
        query_grad,
    )
    q_grad, k_grad, v_grad, o_grad, u_grad, d_grad, block_out, query_grad, g1_grad, g2_grad = conv
    return (
        block_out[None],
        query_grad[None],
        latent_grad[None],
        q_grad,
        k_grad,
        v_grad,
        o_grad,
        u_grad,
        d_grad,
        g1_grad,
        g2_grad,
    )


def solution(mesh):
    rows = P("dp", "seq", None)
    in_specs = (rows, rows, P("dp", None)) + (P(),) * 8 + (rows,)
    out_specs = (rows, rows, rows) + (P(),) * 8
    return jax.shard_map(on_device, mesh=mesh, in_specs=in_specs, out_specs=out_specs, check_vma=False)
```

```python
import functools

import jax
import jax.numpy as jnp
from jax import lax
from jax.experimental import pallas as pl
from jax.experimental.pallas import tpu as pltpu
from jax.sharding import PartitionSpec as P

MESH = pl.DeviceIdType.MESH
F32 = jnp.float32
BF16 = jnp.bfloat16
HEADS = 8
HEAD = 160
LAT = 256
ROWS = 1024
TILE = 512
D = 768
DL = 1280
SCALE = HEAD ** (-0.5)
EPS = 1e-5
VMEM_LIMIT = 63 * 2**20
ORDERS = {
    "du": ("xyz", "yzx", "zxy"),
    "o": ("xyz", "yzx", "zxy"),
    "q": ("xyz", "yzx", "zxy"),
}
PLAN = (
    "w0", "d", "b0", "b1", "m0", "m1", "V0", "V1", "V2", "V3", "d", "K0",
    "K1", "K2", "O0", "K3", "O1", "o", "g0", "v", "g1", "d", "Q0", "o",
    "Q1", "v", "q", "d", "o", "k", "v", "q", "B0", "d", "k", "o",
    "v", "q", "k", "d", "v", "q", "v", "o", "k", "v", "q", "d",
    "x0", "v", "k", "q", "o", "x1", "R0", "k", "d", "k", "v", "q",
    "o", "T0", "v", "k", "k", "q", "d", "o", "k", "v", "q", "B1",
    "o", "d", "L0", "q", "k", "o",
)


def dot(left, right, left_dim, right_dim):
    return lax.dot_general(
        left, right, (((left_dim,), (right_dim,)), ((), ())), preferred_element_type=F32
    )


class Place:
    def __init__(self):
        dp = lax.axis_index("dp")
        sq = lax.axis_index("seq")
        self.seq = sq
        self.dp = dp
        self.core = lax.rem(dp, 2)
        self.at = {"x": lax.div(dp, 2), "y": lax.rem(sq, 4), "z": lax.div(sq, 4)}

    def shifted(self, axis, step):
        return lax.rem(self.at[axis] + step, 4)

    def neighbour(self, axis, step):
        to = dict(self.at)
        to[axis] = self.shifted(axis, step)
        return (to["x"] * 2 + self.core, to["z"] * 4 + to["y"])

    def sibling(self):
        return (self.dp + 1 - 2 * self.core, self.seq)

    def in_seq(self, index):
        return (self.dp, index)


class Rounds:
    def __init__(self, place, send, recv):
        self.place, self.send, self.recv, self.size = place, send, recv, {}

    def copy(self, index, src, dst, device):
        return pltpu.make_async_remote_copy(
            src_ref=src,
            dst_ref=dst,
            send_sem=self.send.at[index],
            recv_sem=self.recv.at[index],
            device_id=device,
            device_id_type=MESH,
        )

    def start(self, index, src, dst, device):
        self.copy(index, src, dst, device).start()

    def wait(self, index, same_size):
        self.size[index] = same_size
        self.copy(index, same_size, same_size, self.place.sibling()).wait_recv()

    def drain(self, only=None):
        for index in list(self.size) if only is None else only:
            same_size = self.size.pop(index)
            self.copy(index, same_size, same_size, self.place.sibling()).wait_send()


class Locals:
    def __init__(self, sems):
        self.sems, self.used = sems, 0

    def start(self, src, dst):
        copy = pltpu.make_async_copy(src, dst, self.sems.at[self.used])
        self.used += 1
        copy.start()
        return copy


class SumSession:
    def __init__(self, place, rounds, local, kind, orders, width, part, rcore, relay, ra, rb, rc, fin, out):
        self.p, self.r, self.local = place, rounds, local
        self.kind, self.orders, self.width = kind, orders, width
        self.part, self.rcore, self.relay, self.ra, self.rb, self.rc = part, rcore, relay, ra, rb, rc
        self.fin, self.out = fin, out
        self.step_done = 0

    def region(self, i, c, a=None, b=None, half=None):
        if self.kind == "rows":
            row, high, col, wide = 256 * i + 128 * c, 128, 0, self.width
            if a is not None:
                row, high = row + 32 * a, 32
            if half is not None:
                row, high = row + 16 * half, 16
            if b is not None:
                row, high = row + 16 * lax.div(b, 2), 16
                wide = self.width // 2
                col = pl.multiple_of(lax.rem(b, 2) * wide, 128)
        else:
            row, high, col, wide = 640 * c, 640, 256 * i, 256
            if a is not None:
                row, high = row + 160 * a, 160
            if half is not None:
                row, high = row + 80 * half, 80
            if b is not None:
                row, high = row + 80 * lax.div(b, 2), 80
                wide = 128
                col = pl.multiple_of(256 * i + 128 * lax.rem(b, 2), 128)
        return pl.ds(pl.multiple_of(row, 16), high), pl.ds(col, wide)

    def here(self, i, *rest):
        return self.region(i, self.p.core, *rest)

    def axes(self, i):
        return self.orders[i]

    def s0(self):
        for i in range(3):
            self.r.start(0, self.part.at[self.region(i, 1 - self.p.core)], self.rcore.at[i], self.p.sibling())

    def s1(self):
        self.r.wait(0, self.rcore)
        for i in range(3):
            here = self.here(i)
            self.part[here] = self.part[here] + self.rcore[i]
        for i in range(3):
            axis = self.axes(i)[0]
            up, down = self.p.neighbour(axis, 1), self.p.neighbour(axis, 3)
            at = [self.p.shifted(axis, k) for k in range(4)]
            self.r.start(1, self.part.at[self.here(i, at[2], None, 0)], self.relay.at[i, 0], down)
            self.r.start(1, self.part.at[self.here(i, at[2], None, 1)], self.relay.at[i, 1], up)
            self.r.start(2, self.part.at[self.here(i, at[1], None, 0)], self.ra.at[i, 0], up)
            self.r.start(2, self.part.at[self.here(i, at[3], None, 1)], self.ra.at[i, 1], down)

    def s2(self):
        self.r.wait(1, self.relay)
        for i in range(3):
            axis = self.axes(i)[0]
            for half, k in ((0, 3), (1, 1)):
                there = self.here(i, self.p.shifted(axis, k), None, half)
                self.part[there] = self.part[there] + self.relay[i, half]
                self.r.start(2, self.part.at[there], self.ra.at[i, 2 + half], self.p.neighbour(axis, k))

    def s3(self):
        self.r.wait(2, self.ra)
        for i in range(3):
            a = self.p.at[self.axes(i)[0]]
            for half in range(2):
                here = self.here(i, a, None, half)
                total = self.part[here].astype(F32) + self.ra[i, half].astype(F32) + self.ra[i, 2 + half].astype(F32)
                self.part[here] = total.astype(BF16)
        for i in range(3):
            a_axis, b_axis, _ = self.axes(i)
            for k in range(3):
                to = self.p.shifted(b_axis, k + 1)
                self.r.start(
                    3,
                    self.part.at[self.here(i, self.p.at[a_axis], to)],
                    self.rb.at[i, k],
                    self.p.neighbour(b_axis, k + 1),
                )

    def s4(self):
        self.r.wait(3, self.rb)
        for i in range(3):
            a_axis, b_axis, c_axis = self.axes(i)
            total = self.part[self.here(i, self.p.at[a_axis], self.p.at[b_axis])].astype(F32)
            for k in range(3):
                total = total + self.rb[i, k].astype(F32)
            self.rc[i, pl.ds(self.p.at[c_axis], 1)] = total.astype(BF16)[None]
        for i in range(3):
            c_axis = self.axes(i)[2]
            slot = self.rc.at[i, self.p.at[c_axis]]
            for k in range(3):
                self.r.start(4, slot, slot, self.p.neighbour(c_axis, k + 1))

    def s5(self):
        self.r.wait(4, self.rb)
        self.own = []
        for i in range(3):
            total = self.rc[i, 0].astype(F32)
            for k in range(1, 4):
                total = total + self.rc[i, k].astype(F32)
            self.fin[i] = total.astype(BF16)
        for i in range(3):
            a_axis, b_axis, _ = self.axes(i)
            there = self.out.at[self.here(i, self.p.at[a_axis], self.p.at[b_axis])]
            self.own.append(self.local.start(self.fin.at[i], there))
            for k in range(3):
                self.r.start(5, self.fin.at[i], there, self.p.neighbour(b_axis, k + 1))

    def s6(self):
        self.r.wait(5, self.rb)
        for copy in self.own:
            copy.wait()
        for i in range(3):
            axis = self.axes(i)[0]
            there = self.out.at[self.here(i, self.p.at[axis])]
            for k in (1, 3):
                self.r.start(6, there, there, self.p.neighbour(axis, k))

    def s7(self):
        self.r.wait(6, self.ra)
        for i in range(3):
            axis = self.axes(i)[0]
            for half, k in ((0, 3), (1, 1)):
                there = self.out.at[self.here(i, self.p.shifted(axis, k), None, half)]
                self.r.start(7, there, there, self.p.neighbour(axis, 4 - k))

    def s8(self):
        self.r.wait(7, self.relay)
        for i in range(3):
            there = self.out.at[self.here(i)]
            self.r.start(8, there, there, self.p.sibling())

    def s9(self):
        self.r.wait(8, self.rcore)

    def step(self):
        getattr(self, "s%d" % self.step_done)()
        self.step_done += 1


class LatentSession:
    def __init__(self, place, rounds, local, first, other, part, slots, sums, slots2, turned, turned_at, lat, buffers, out):
        self.p, self.r, self.local, self.first, self.other = place, rounds, local, first, other
        self.part, self.slots, self.sums, self.slots2 = part, slots, sums, slots2
        self.turned, self.turned_at, self.lat, self.out = turned, turned_at, lat, out
        self.half, self.rhalf, self.ra, self.rb, self.rc, self.rd, self.fa, self.fb, self.fc, self.fd = buffers
        self.f, self.g = place.at[first], place.at[other]
        self.step_done = 0

    def rows(self, step):
        return pl.ds(pl.multiple_of(320 * self.p.shifted(self.first, step), 64), 320)

    def send(self, step):
        if step > 0:
            self.r.start(0, self.part.at[self.rows(step)], self.slots.at[step - 1], self.p.neighbour(self.first, step))

    def s0(self):
        self.r.wait(0, self.slots)
        total = self.part[self.rows(0)].astype(F32)
        for k in range(3):
            total = total + self.slots[k].astype(F32)
        for k in range(4):
            self.sums[k] = total[80 * k : 80 * k + 80].astype(BF16)
        for k in range(1, 4):
            to = self.p.shifted(self.other, k)
            self.r.start(1, self.sums.at[to], self.slots2.at[k - 1], self.p.neighbour(self.other, k))

    def s1(self):
        self.r.wait(1, self.slots2)
        total = self.sums[self.g].astype(F32)
        for k in range(3):
            total = total + self.slots2[k].astype(F32)
        product = dot(total.astype(BF16), self.lat[...].reshape(LAT, DL), 1, 0).astype(BF16)
        self.half[0] = product[:, :640]
        self.half[1] = product[:, 640:]
        self.r.start(2, self.half.at[1 - self.p.core], self.rhalf, self.p.sibling())
        self.turned[:, self.turned_at : self.turned_at + 80] = total.T

    def s2(self):
        self.r.wait(2, self.rhalf)
        x = self.p.at["x"]
        total = self.half[self.p.core] + self.rhalf[...]
        self.half[self.p.core] = total
        self.rb[pl.ds(x, 1)] = total[0:64, 256:512][None]
        self.rc[pl.ds(x, 1)] = total[0:64, 512:][None]
        self.rd[pl.ds(x, 1)] = total[64:80][None]
        for k in range(1, 4):
            rows = pl.ds(pl.multiple_of(16 * self.p.shifted("x", k), 16), 16)
            self.r.start(
                3, self.half.at[self.p.core, rows, pl.ds(0, 256)], self.ra.at[k - 1], self.p.neighbour("x", k)
            )
        for k in range(1, 4):
            for index, buf in ((4, self.rb), (5, self.rc), (6, self.rd)):
                self.r.start(index, buf.at[x], buf.at[x], self.p.neighbour("x", k))

    def columns(self, start, size):
        return pl.ds(pl.multiple_of(640 * self.p.core + start, 128), size)

    def a_part(self):
        return pl.ds(pl.multiple_of(16 * self.p.at["x"], 16), 16), self.columns(0, 256)

    def b_part(self):
        return pl.ds(0, 64), self.columns(256, 256)

    def c_part(self):
        return pl.ds(0, 64), self.columns(512, 128)

    def d_part(self):
        return pl.ds(64, 16), self.columns(0, 640)

    def same(self, index, *lead):
        rows, cols = ((16, 256), (64, 256), (64, 128), (16, 640))[index]
        return self.out.at[lead + (pl.ds(0, rows), pl.ds(0, cols))]

    def s3(self):
        three = pl.ds(0, 3)
        self.r.wait(3, self.ra)
        total = self.half[self.p.core, self.a_part()[0], 0:256].astype(F32)
        for k in range(3):
            total = total + self.ra[k].astype(F32)
        self.fa[...] = total.astype(BF16)
        for index, buf, fin in ((4, self.rb, self.fb), (5, self.rc, self.fc), (6, self.rd, self.fd)):
            self.r.wait(index, buf.at[three])
            total = buf[0].astype(F32)
            for k in range(1, 4):
                total = total + buf[k].astype(F32)
            fin[...] = total.astype(BF16)
        block = self.out.at[self.f, self.g]
        self.own = []
        for index, fin, part, axis in (
            (7, self.fa, self.a_part(), self.first),
            (9, self.fc, self.c_part(), self.other),
            (10, self.fd, self.d_part(), self.other),
            (8, self.fb, self.b_part(), self.first),
        ):
            there = block.at[part]
            self.own.append(self.local.start(fin, there))
            for k in range(1, 4):
                self.r.start(index, fin, there, self.p.neighbour(axis, k))

    def s4(self):
        three, every = pl.ds(0, 3), slice(None)
        for index in range(4):
            self.r.wait(7 + index, self.same(index, 0, three))
        for copy in self.own:
            copy.wait()
        there = self.out.at[(every, self.g) + self.a_part()]
        for k in range(1, 4):
            self.r.start(11, there, there, self.p.neighbour(self.other, k))
        for index, part in ((13, self.c_part()), (14, self.d_part())):
            there = self.out.at[(self.f, every) + part]
            for k in (1, 3):
                self.r.start(index, there, there, self.p.neighbour(self.first, k))
        there = self.out.at[(every, self.g) + self.b_part()]
        for k in (1, 3):
            self.r.start(12, there, there, self.p.neighbour(self.other, k))

    def s5(self):
        every = slice(None)
        self.r.wait(11, self.same(0, pl.ds(0, 3), every))
        there = self.out.at[(every, every) + self.a_part()]
        for k in (1, 3):
            self.r.start(15, there, there, self.p.neighbour("x", k))

    def s6(self):
        two, every = pl.ds(0, 2), slice(None)
        self.r.wait(13, self.same(2, two, every))
        self.r.wait(14, self.same(3, two, every))
        for index, part in ((21, self.c_part()), (22, self.d_part())):
            for low, k in ((0, 3), (2, 1)):
                there = self.out.at[(self.p.shifted(self.first, k), pl.ds(low, 2)) + part]
                self.r.start(index, there, there, self.p.neighbour(self.first, 4 - k))
        self.r.wait(12, self.same(1, two, every))
        for low, k in ((0, 3), (2, 1)):
            there = self.out.at[(pl.ds(low, 2), self.p.shifted(self.other, k)) + self.b_part()]
            self.r.start(20, there, there, self.p.neighbour(self.other, 4 - k))

    def s7(self):
        self.r.wait(15, self.out.at[:, :, pl.ds(0, 32), pl.ds(0, 256)])
        for low, k in ((0, 3), (2, 1)):
            rows = pl.ds(pl.multiple_of(16 * self.p.shifted("x", k), 16), 16)
            there = self.out.at[pl.ds(low, 2), :, rows, self.columns(0, 256)]
            self.r.start(23, there, there, self.p.neighbour("x", 4 - k))

    def s8(self):
        every = slice(None)
        for index, part in ((1, self.b_part()), (2, self.c_part()), (3, self.d_part())):
            self.r.wait(19 + index, self.same(index, 0, every))
            there = self.out.at[(every, every) + part]
            self.r.start(15 + index, there, there, self.p.sibling())

    def s9(self):
        every = slice(None)
        self.r.wait(23, self.same(0, every, every))
        there = self.out.at[every, every, pl.ds(0, 64), self.columns(0, 256)]
        self.r.start(19, there, there, self.p.sibling())

    def s10(self):
        every = slice(None)
        for index in (1, 2, 3):
            self.r.wait(15 + index, self.same(index, every, every))
        self.r.wait(19, self.out.at[:, :, pl.ds(0, 64), pl.ds(0, 256)])

    def step(self):
        getattr(self, "s%d" % self.step_done)()
        self.step_done += 1


SUM_ROUNDS = 9
LATENT_ROUNDS = 24
N_LOCAL = 40


def main_kernel(
    lengths,
    gain1,
    gain2,
    queries,
    cotangent,
    latents,
    q_w,
    k_w,
    v_w,
    o_w,
    u_w,
    d_w,
    block_out,
    query_grad,
    latent_grad,
    g_du,
    g_o,
    g_q,
    g_k,
    g_v,
    qin,
    cin,
    lat,
    wq,
    wk,
    wv,
    wo,
    wu,
    wd,
    first,
    query,
    keys,
    values,
    att,
    mixed,
    resid,
    second,
    act,
    gup,
    gout,
    stats,
    gcol,
    part_du,
    part_q,
    part_k,
    part_v,
    rcore_du,
    rcore_o,
    rcore_q,
    relay_du,
    relay_o,
    relay_q,
    ra_du,
    ra_o,
    ra_q,
    rb_du,
    rb_o,
    rb_q,
    rc_du,
    rc_o,
    rc_q,
    fin_du,
    fin_o,
    fin_q,
    slots_k,
    slots_v,
    sums_k,
    sums_v,
    slots2_k,
    slots2_v,
    *rest,
):
    buffers_k, buffers_v = rest[0:10], rest[10:20]
    (
        turned,
        turned_low,
        rturned,
        gathered_k,
        gathered_v,
        du_send,
        du_recv,
        o_send,
        o_recv,
        q_send,
        q_recv,
        k_send,
        k_recv,
        v_send,
        v_recv,
        a_send,
        a_recv,
        local_sem,
    ) = rest[20:]
    p = Place()
    local = Locals(local_sem)
    load_q = [local.start(queries.at[pl.ds(TILE * j, TILE)], qin.at[pl.ds(TILE * j, TILE)]) for j in range(2)]
    z, y = p.at["z"], p.at["y"]
    load_own = local.start(latents, lat.at[z, y])
    load_wq = local.start(q_w, wq)

    barrier = pltpu.get_barrier_semaphore()
    for k in range(1, 16):
        pl.semaphore_signal(barrier, inc=1, device_id=p.in_seq(lax.rem(p.seq + k, 16)), device_id_type=MESH)
    for k in range(1, 4):
        pl.semaphore_signal(barrier, inc=1, device_id=p.neighbour("x", k), device_id_type=MESH)
    pl.semaphore_signal(barrier, inc=1, device_id=p.sibling(), device_id_type=MESH)

    seq = p.seq
    is_long = (seq < 8).astype(jnp.int32)
    lane = lax.broadcasted_iota(jnp.int32, (1, 128), 1)
    for j in range(8):
        item = is_long * lax.div(seq, 2) + (1 - is_long) * (4 + (seq - 8) * 8 + j)
        offset = is_long * (lax.rem(seq, 2) * 1024 + 128 * j)
        stats[0:1, 128 * j : 128 * j + 128] = jnp.where(lane + offset < lengths[0, item], 1.0, 0.0).astype(F32)

    gcol[0] = jnp.broadcast_to(gain1[...].reshape(1, D), (128, D)).T
    gcol[1] = jnp.broadcast_to(gain2[...].reshape(1, D), (128, D)).T
    col1 = gcol[0][:, 0:1]
    col2 = gcol[1][:, 0:1]
    turned[...] = jnp.zeros_like(turned)

    def normalized(x):
        center = x - jnp.mean(x, axis=0, keepdims=True)
        rstd = lax.rsqrt(jnp.mean(center * center, axis=0, keepdims=True) + EPS)
        return center * rstd, rstd

    tiles = [pl.ds(TILE * j, TILE) for j in range(2)]

    def first_part(j):
        t = tiles[j]
        load_q[j].wait()
        x = qin[t, :].T.astype(F32)
        resid[:, t] = x
        n, _ = normalized(x)
        first[:, t] = (n * col1).astype(BF16)

    load_c = local.start(cotangent, cin)
    load_wd = local.start(d_w, wd)
    load_wk = local.start(k_w, wk)
    load_wv = local.start(v_w, wv)
    load_wo = local.start(o_w, wo)
    load_wu = local.start(u_w, wu)
    first_part(0)
    load_own.wait()
    pl.semaphore_wait(barrier, 19)

    early = Rounds(p, a_send, a_recv)
    left, right = pl.ds(0, 640), pl.ds(640, 640)
    for k in range(1, 4):
        early.start(0, lat.at[z, y, :, left], lat.at[z, y, :, left], p.neighbour("y", k))
        early.start(0, lat.at[z, y, :, right], lat.at[z, y, :, right], p.neighbour("z", k))

    def latents_on():
        early.wait(0, lat.at[0, pl.ds(0, 3)])
        for k in range(1, 4):
            early.start(1, lat.at[z, :, :, left], lat.at[z, :, :, left], p.neighbour("z", k))
            early.start(1, lat.at[:, y, :, right], lat.at[:, y, :, right], p.neighbour("y", k))

    first_part(1)
    load_wq.wait()
    for j, t in enumerate(tiles):
        query[:, t] = (dot(wq[...], first[:, t], 0, 0) * SCALE).astype(BF16)
        if j == 0:
            latents_on()
    load_c.wait()
    load_wd.wait()
    for t in tiles:
        gout[:, t] = (stats[0:1, t] * cin[t, :].T.astype(F32)).astype(BF16)
        gup[:, t] = dot(wd[...], gout[:, t], 1, 0).astype(BF16)

    early.wait(1, lat.at[pl.ds(0, 3)])
    all_latents = lat[...].reshape(LAT, DL)
    load_wk.wait()
    keys[...] = dot(all_latents, wk[...], 1, 0).astype(BF16).T
    load_wv.wait()
    values[...] = dot(all_latents, wv[...], 1, 0).astype(BF16).T
    load_wo.wait()
    load_wu.wait()

    def mix(h):
        r = pl.ds(HEAD * h, HEAD)
        mixed[r, :] = dot(values[r, :], att[pl.ds(LAT * h, LAT), :], 1, 0).astype(BF16)

    for h in range(HEADS):
        r = pl.ds(HEAD * h, HEAD)
        for t in tiles:
            s = dot(keys[r, :], query[r, t], 0, 0)
            e = jnp.exp(s - jnp.max(s, axis=0, keepdims=True))
            att[pl.ds(LAT * h, LAT), t] = (e * (1.0 / jnp.sum(e, axis=0, keepdims=True))).astype(BF16)
        if h > 0:
            mix(h - 1)
    mix(HEADS - 1)
    for t in tiles:
        x = resid[:, t] + dot(wo[...], mixed[:, t], 0, 0)
        resid[:, t] = x
        mu = jnp.mean(x, axis=0, keepdims=True)
        center = x - mu
        rstd = lax.rsqrt(jnp.mean(center * center, axis=0, keepdims=True) + EPS)
        stats[1:2, t] = mu
        stats[2:3, t] = rstd
        second[:, t] = (center * rstd * col2).astype(BF16)
        up = dot(wu[...], second[:, t], 0, 0)
        cdf = 0.5 * (1.0 + lax.erf(up * (0.5**0.5)))
        act[:, t] = (up * cdf).astype(BF16)
        slope = cdf + up * (jnp.exp(-0.5 * up * up) * 0.3989422804014327)
        gup[:, t] = (slope * gup[:, t].astype(F32)).astype(BF16)

    part_o = wk.at[:, pl.ds(0, D)]
    du = SumSession(
        p,
        Rounds(p, du_send, du_recv),
        local,
        "rows",
        ORDERS["du"],
        1536,
        part_du,
        rcore_du,
        relay_du,
        ra_du,
        rb_du,
        rc_du,
        fin_du,
        g_du,
    )
    so = SumSession(
        p,
        Rounds(p, o_send, o_recv),
        local,
        "cols",
        ORDERS["o"],
        D,
        part_o,
        rcore_o,
        relay_o,
        ra_o,
        rb_o,
        rc_o,
        fin_o,
        g_o,
    )
    sq = SumSession(
        p,
        Rounds(p, q_send, q_recv),
        local,
        "rows",
        ORDERS["q"],
        DL,
        part_q,
        rcore_q,
        relay_q,
        ra_q,
        rb_q,
        rc_q,
        fin_q,
        g_q,
    )
    sk = LatentSession(
        p,
        Rounds(p, k_send, k_recv),
        local,
        "y",
        "z",
        part_k,
        slots_k,
        sums_k,
        slots2_k,
        turned,
        0,
        lat,
        buffers_k,
        g_k,
    )
    sv = LatentSession(
        p,
        Rounds(p, v_send, v_recv),
        local,
        "z",
        "y",
        part_v,
        slots_v,
        sums_v,
        slots2_v,
        turned,
        128,
        lat,
        buffers_v,
        g_v,
    )
    gal = second
    gm = wv.at[:, pl.ds(0, ROWS)]
    stores = []

    def heads_of(axis, j):
        for i in range(2):
            h = 2 * p.shifted(axis, j) + i
            yield pl.ds(pl.multiple_of(h * HEAD, 32), HEAD), pl.ds(pl.multiple_of(h * LAT, 256), LAT)

    def mlp_back(j):
        t = tiles[j]
        gg = dot(wu[...], gup[:, t], 1, 0) * col2
        rstd = stats[2:3, t]
        n = (resid[:, t] - stats[1:2, t]) * rstd
        mean_gg = jnp.mean(gg, axis=0, keepdims=True)
        mean_ggn = jnp.mean(gg * n, axis=0, keepdims=True)
        gal[:, t] = (gout[:, t].astype(F32) + rstd * (gg - mean_gg - n * mean_ggn)).astype(BF16)

    def mixed_back(j):
        gm[:, tiles[j]] = dot(wo[...], gal[:, tiles[j]], 1, 0).astype(BF16)

    def value_heads(j):
        for r, l in heads_of("z", j):
            part_v[r, :] = dot(gm[r, :], att[l, :], 1, 1).astype(BF16)
        sv.send(j)

    def key_heads(j):
        for r, l in heads_of("y", j):
            for t in tiles:
                ga = dot(values[r, :], gm[r, t], 0, 0)
                a = att[l, t].astype(F32)
                att[l, t] = (a * (ga - jnp.sum(ga * a, axis=0, keepdims=True))).astype(BF16)
            part_k[r, :] = dot(query[r, :], att[l, :], 1, 1).astype(BF16)
        sk.send(j)

    def query_back(j):
        for h in range(4 * j, 4 * j + 4):
            r = pl.ds(h * HEAD, HEAD)
            gm[r, :] = dot(keys[r, :], att[pl.ds(h * LAT, LAT), :], 1, 0).astype(BF16)

    def query_weight(j):
        c = pl.ds(640 * j, 640)
        part_q[:, c] = (dot(first[...], gm[c, :], 1, 1) * SCALE).astype(BF16)

    def out_weight(j):
        c = pl.ds(640 * j, 640)
        wk[c, 0:D] = dot(mixed[c, :], gal[...], 1, 1).astype(BF16)

    def query_out(j):
        t = tiles[j]
        gg = dot(wq[...], gm[:, t], 1, 0) * (col1 * SCALE)
        n, rstd = normalized(qin[t, :].T.astype(F32))
        mean_gg = jnp.mean(gg, axis=0, keepdims=True)
        mean_ggn = jnp.mean(gg * n, axis=0, keepdims=True)
        total = gal[:, t].astype(F32) + rstd * (gg - mean_gg - n * mean_ggn)
        qin[t, :] = total.astype(BF16).T
        stores.append(local.start(qin.at[t], query_grad.at[t]))

    def block(j):
        t = tiles[j]
        out = stats[0:1, t] * (resid[:, t] + dot(wd[...], act[:, t], 0, 0))
        cin[t, :] = out.astype(BF16).T
        stores.append(local.start(cin.at[t], block_out.at[t]))

    def turn_send(j):
        turned_low[...] = turned[...].astype(BF16)
        for k in range(1, 16):
            who = lax.rem(seq + k, 16)
            mine = turned_low.at[pl.ds(pl.multiple_of(who * 16, 16), 16)]
            early.start(2, mine, rturned.at[seq], p.in_seq(who))
        rturned[pl.ds(seq, 1)] = turned_low[pl.ds(pl.multiple_of(seq * 16, 16), 16), :][None]

    reload = []

    def load_again(j):
        so.r.drain((0, 1, 2, 3))
        reload.append(local.start(k_w, wk))
        reload.append(local.start(v_w, wv))

    def latent_back(j):
        early.wait(2, rturned.at[pl.ds(0, 15)])
        for i in range(16):
            piece = rturned[i].astype(F32).T
            gathered_k[pl.ds(80 * (4 * (i % 4) + i // 4), 80), :] = piece[0:80, :]
            gathered_v[pl.ds(80 * i, 80), :] = piece[128:208, :]
        for load in reload:
            load.wait()
        latent_grad[...] = dot(gathered_k[...].T.astype(BF16), wk[...], 1, 1) + dot(
            gathered_v[...].T.astype(BF16), wv[...], 1, 1
        )

    def down_up(j):
        part_du[:, 0:D] = dot(act[...], gout[...], 1, 1).astype(BF16)
        part_du[:, D:] = dot(second[...], gup[...], 1, 1).astype(BF16)

    parts = {
        "w": down_up,
        "b": mlp_back,
        "m": mixed_back,
        "V": value_heads,
        "K": key_heads,
        "g": query_back,
        "Q": query_weight,
        "O": out_weight,
        "x": query_out,
        "B": block,
        "T": turn_send,
        "R": load_again,
        "L": latent_back,
    }
    sessions = {"d": du, "o": so, "q": sq, "k": sk, "v": sv}
    for item in PLAN:
        if item in sessions:
            sessions[item].step()
        else:
            parts[item[0]](int(item[1]))
    for copy in stores:
        copy.wait()
    early.drain()
    for session in (du, so, sq, sk, sv):
        session.r.drain()
    assert [s.step_done for s in (du, so, sq, sk, sv)] == [10, 10, 10, 11, 11]


def convert_kernel(
    gain1,
    gain2,
    du,
    o,
    q,
    k,
    v,
    u_w,
    q_w,
    block,
    query,
    out_q,
    out_k,
    out_v,
    out_o,
    out_u,
    out_d,
    out_block,
    out_query,
    out_g1,
    out_g2,
):
    high = out_q.shape[0]
    at = pl.ds(pl.multiple_of(pl.program_id(0) * high, 128), high)

    def per_row(product, gain):
        total = jnp.sum(product, axis=1, keepdims=True)
        return (jnp.broadcast_to(total, (high, 128)).T[0:1, :] / gain.reshape(1, high)).reshape(high)

    out_d[...] = du[:, 0:D].astype(F32)
    up = du[:, D:].astype(F32)
    out_u[...] = up
    out_g2[at] = per_row(up * u_w[...].astype(F32), gain2[at])
    value = q[...].astype(F32)
    out_q[...] = value
    out_g1[at] = per_row(value * q_w[...].astype(F32), gain1[at])
    out_o[...] = o[...].astype(F32)
    out_k[...] = k[...].T.astype(F32)
    out_v[...] = v[...].T.astype(F32)
    out_block[...] = block[...]
    out_query[...] = query[...].astype(F32)


def vm(shape, dtype=BF16):
    return pltpu.VMEM(shape, dtype)


def on_device(queries, latents, lengths, q_w, k_w, v_w, o_w, u_w, d_w, gain1, gain2, cotangent):
    any_spec = pl.BlockSpec(memory_space=pl.ANY)
    vmem_spec = pl.BlockSpec(memory_space=pltpu.VMEM)
    dma = pltpu.SemaphoreType.DMA
    sds = jax.ShapeDtypeStruct
    outs = pl.pallas_call(
        main_kernel,
        out_shape=(
            sds((ROWS, D), BF16),
            sds((ROWS, D), BF16),
            sds((16, DL), F32),
            sds((D, 1536), BF16),
            sds((DL, D), BF16),
            sds((D, DL), BF16),
            sds((4, 4, 80, DL), BF16),
            sds((4, 4, 80, DL), BF16),
        ),
        in_specs=[pl.BlockSpec(memory_space=pltpu.SMEM), vmem_spec, vmem_spec] + [any_spec] * 9,
        out_specs=(any_spec, any_spec, vmem_spec) + (any_spec,) * 5,
        scratch_shapes=[
            vm((ROWS, D)),
            vm((ROWS, D)),
            vm((4, 4, 16, DL)),
            vm((D, DL)),
            vm((DL, DL)),
            vm((DL, DL)),
            vm((DL, D)),
            vm((D, D)),
            vm((D, D)),
            vm((D, ROWS)),
            vm((DL, ROWS)),
            vm((DL, LAT)),
            vm((DL, LAT)),
            vm((HEADS * LAT, ROWS)),
            vm((DL, ROWS)),
            vm((D, ROWS), F32),
            vm((D, ROWS)),
            vm((D, ROWS)),
            vm((D, ROWS)),
            vm((D, ROWS)),
            vm((8, ROWS), F32),
            vm((2, D, 128), F32),
            vm((D, 1536)),
            vm((D, DL)),
            vm((DL, LAT)),
            vm((DL, LAT)),
            vm((3, 128, 1536)),
            vm((3, 640, 256)),
            vm((3, 128, DL)),
            vm((3, 2, 16, 1536)),
            vm((3, 2, 80, 256)),
            vm((3, 2, 16, DL)),
            vm((3, 4, 16, 1536)),
            vm((3, 4, 80, 256)),
            vm((3, 4, 16, DL)),
            vm((3, 3, 16, 768)),
            vm((3, 3, 80, 128)),
            vm((3, 3, 16, 640)),
            vm((3, 4, 16, 768)),
            vm((3, 4, 80, 128)),
            vm((3, 4, 16, 640)),
            vm((3, 16, 768)),
            vm((3, 80, 128)),
            vm((3, 16, 640)),
            vm((3, 320, LAT)),
            vm((3, 320, LAT)),
            vm((4, 80, LAT)),
            vm((4, 80, LAT)),
            vm((3, 80, LAT)),
            vm((3, 80, LAT)),
        ]
        + [
            vm((2, 80, 640)),
            vm((80, 640)),
            vm((3, 16, 256)),
            vm((4, 64, 256)),
            vm((4, 64, 128)),
            vm((4, 16, 640)),
            vm((16, 256)),
            vm((64, 256)),
            vm((64, 128)),
            vm((16, 640)),
        ]
        * 2
        + [
            vm((LAT, 256), F32),
            vm((LAT, 256)),
            vm((16, 16, 256)),
            vm((DL, 16), F32),
            vm((DL, 16), F32),
        ]
        + [dma((SUM_ROUNDS,))] * 6
        + [dma((LATENT_ROUNDS,))] * 4
        + [dma((3,)), dma((3,)), dma((N_LOCAL,))],
        compiler_params=pltpu.CompilerParams(
            collective_id=0, has_side_effects=True, vmem_limit_bytes=VMEM_LIMIT
        ),
        name="decoder_block",
    )(lengths, gain1, gain2, queries[0], cotangent[0], latents[0], q_w, k_w, v_w, o_w, u_w, d_w)
    block_out, query_grad, latent_grad, g_du, g_o, g_q, g_k, g_v = outs

    def by_rows(rows, columns):
        return pl.BlockSpec((rows // 2, columns), lambda i: (i, 0))

    by_columns = pl.BlockSpec((DL, DL // 2), lambda i: (0, i))
    whole = pl.BlockSpec((D,), lambda i: (0,))
    conv = pl.pallas_call(
        convert_kernel,
        out_shape=(
            sds((D, DL), F32),
            sds((DL, DL), F32),
            sds((DL, DL), F32),
            sds((DL, D), F32),
            sds((D, D), F32),
            sds((D, D), F32),
            sds((ROWS, D), BF16),
            sds((ROWS, D), F32),
            sds((D,), F32),
            sds((D,), F32),
        ),
        grid=(2,),
        in_specs=[whole, whole]
        + [by_rows(*shape) for shape in ((D, 1536), (DL, D), (D, DL))]
        + [by_columns, by_columns]
        + [by_rows(*shape) for shape in ((D, D), (D, DL), (ROWS, D), (ROWS, D))],
        out_specs=tuple(
            by_rows(*shape)
            for shape in ((D, DL), (DL, DL), (DL, DL), (DL, D), (D, D), (D, D), (ROWS, D), (ROWS, D))
        )
        + (whole, whole),
        compiler_params=pltpu.CompilerParams(vmem_limit_bytes=VMEM_LIMIT),
        name="to_float32",
    )(
        gain1,
        gain2,
        g_du,
        g_o,
        g_q,
        g_k.reshape(DL, DL),
        g_v.reshape(DL, DL),
        u_w,
        q_w,
        block_out,
        query_grad,
    )
    q_grad, k_grad, v_grad, o_grad, u_grad, d_grad, block_out, query_grad, g1_grad, g2_grad = conv
    return (
        block_out[None],
        query_grad[None],
        latent_grad[None],
        q_grad,
        k_grad,
        v_grad,
        o_grad,
        u_grad,
        d_grad,
        g1_grad,
        g2_grad,
    )


def solution(mesh):
    rows = P("dp", "seq", None)
    in_specs = (rows, rows, P("dp", None)) + (P(),) * 8 + (rows,)
    out_specs = (rows, rows, rows) + (P(),) * 8
    return jax.shard_map(on_device, mesh=mesh, in_specs=in_specs, out_specs=out_specs, check_vma=False)
```

```python
import functools

import jax
import jax.numpy as jnp
from jax import lax
from jax.experimental import pallas as pl
from jax.experimental.pallas import tpu as pltpu
from jax.sharding import PartitionSpec as P

MESH = pl.DeviceIdType.MESH
F32 = jnp.float32
BF16 = jnp.bfloat16
HEADS = 8
HEAD = 160
LAT = 256
ROWS = 1024
TILE = 512
D = 768
DL = 1280
SCALE = HEAD ** (-0.5)
EPS = 1e-5
VMEM_LIMIT = 63 * 2**20
ORDERS = {
    "du": ("xyz", "yzx", "zxy"),
    "o": ("xyz", "yzx", "zxy"),
    "q": ("xyz", "yzx", "zxy"),
}
PLAN = (
    "w0", "d", "b0", "b1", "m0", "d", "m1", "V0", "V1", "V2", "V3", "K0",
    "d", "K1", "K2", "K3", "O0", "O1", "o", "v", "d", "g0", "g1", "Q0",
    "o", "Q1", "v", "d", "q", "k", "o", "v", "d", "q", "k", "T0",
    "o", "v", "d", "q", "x0", "k", "v", "x1", "q", "o", "v", "R0",
    "k", "B0", "d", "q", "o", "k", "q", "d", "o", "v", "B1", "k",
    "L0", "v", "q", "o", "k", "k", "d", "q", "v", "o", "v", "k",
    "k", "q", "o", "k", "v", "q",
)


def dot(left, right, left_dim, right_dim):
    return lax.dot_general(
        left, right, (((left_dim,), (right_dim,)), ((), ())), preferred_element_type=F32
    )


class Place:
    def __init__(self):
        dp = lax.axis_index("dp")
        sq = lax.axis_index("seq")
        self.seq = sq
        self.dp = dp
        self.core = lax.rem(dp, 2)
        self.at = {"x": lax.div(dp, 2), "y": lax.rem(sq, 4), "z": lax.div(sq, 4)}

    def shifted(self, axis, step):
        return lax.rem(self.at[axis] + step, 4)

    def neighbour(self, axis, step):
        to = dict(self.at)
        to[axis] = self.shifted(axis, step)
        return (to["x"] * 2 + self.core, to["z"] * 4 + to["y"])

    def sibling(self):
        return (self.dp + 1 - 2 * self.core, self.seq)

    def in_seq(self, index):
        return (self.dp, index)


class Rounds:
    def __init__(self, place, send, recv):
        self.place, self.send, self.recv, self.size = place, send, recv, {}

    def copy(self, index, src, dst, device):
        return pltpu.make_async_remote_copy(
            src_ref=src,
            dst_ref=dst,
            send_sem=self.send.at[index],
            recv_sem=self.recv.at[index],
            device_id=device,
            device_id_type=MESH,
        )

    def start(self, index, src, dst, device):
        self.copy(index, src, dst, device).start()

    def wait(self, index, same_size):
        self.size[index] = same_size
        self.copy(index, same_size, same_size, self.place.sibling()).wait_recv()

    def drain(self, only=None):
        for index in list(self.size) if only is None else only:
            same_size = self.size.pop(index)
            self.copy(index, same_size, same_size, self.place.sibling()).wait_send()


class Locals:
    def __init__(self, sems):
        self.sems, self.used = sems, 0

    def start(self, src, dst):
        copy = pltpu.make_async_copy(src, dst, self.sems.at[self.used])
        self.used += 1
        copy.start()
        return copy


class SumSession:
    def __init__(self, place, rounds, local, kind, orders, width, part, rcore, relay, ra, rb, rc, fin, out):
        self.p, self.r, self.local = place, rounds, local
        self.kind, self.orders, self.width = kind, orders, width
        self.part, self.rcore, self.relay, self.ra, self.rb, self.rc = part, rcore, relay, ra, rb, rc
        self.fin, self.out = fin, out
        self.step_done = 0

    def region(self, i, c, a=None, b=None, half=None):
        if self.kind == "rows":
            row, high, col, wide = 256 * i + 128 * c, 128, 0, self.width
            if a is not None:
                row, high = row + 32 * a, 32
            if half is not None:
                row, high = row + 16 * half, 16
            if b is not None:
                row, high = row + 16 * lax.div(b, 2), 16
                wide = self.width // 2
                col = pl.multiple_of(lax.rem(b, 2) * wide, 128)
        else:
            row, high, col, wide = 640 * c, 640, 256 * i, 256
            if a is not None:
                row, high = row + 160 * a, 160
            if half is not None:
                row, high = row + 80 * half, 80
            if b is not None:
                row, high = row + 80 * lax.div(b, 2), 80
                wide = 128
                col = pl.multiple_of(256 * i + 128 * lax.rem(b, 2), 128)
        return pl.ds(pl.multiple_of(row, 16), high), pl.ds(col, wide)

    def here(self, i, *rest):
        return self.region(i, self.p.core, *rest)

    def axes(self, i):
        return self.orders[i]

    def s0(self):
        for i in range(3):
            self.r.start(0, self.part.at[self.region(i, 1 - self.p.core)], self.rcore.at[i], self.p.sibling())

    def s1(self):
        self.r.wait(0, self.rcore)
        for i in range(3):
            here = self.here(i)
            self.part[here] = self.part[here] + self.rcore[i]
        for i in range(3):
            axis = self.axes(i)[0]
            up, down = self.p.neighbour(axis, 1), self.p.neighbour(axis, 3)
            at = [self.p.shifted(axis, k) for k in range(4)]
            self.r.start(1, self.part.at[self.here(i, at[2], None, 0)], self.relay.at[i, 0], down)
            self.r.start(1, self.part.at[self.here(i, at[2], None, 1)], self.relay.at[i, 1], up)
            self.r.start(2, self.part.at[self.here(i, at[1], None, 0)], self.ra.at[i, 0], up)
            self.r.start(2, self.part.at[self.here(i, at[3], None, 1)], self.ra.at[i, 1], down)

    def s2(self):
        self.r.wait(1, self.relay)
        for i in range(3):
            axis = self.axes(i)[0]
            for half, k in ((0, 3), (1, 1)):
                there = self.here(i, self.p.shifted(axis, k), None, half)
                self.part[there] = self.part[there] + self.relay[i, half]
                self.r.start(2, self.part.at[there], self.ra.at[i, 2 + half], self.p.neighbour(axis, k))

    def s3(self):
        self.r.wait(2, self.ra)
        for i in range(3):
            a = self.p.at[self.axes(i)[0]]
            for half in range(2):
                here = self.here(i, a, None, half)
                total = self.part[here].astype(F32) + self.ra[i, half].astype(F32) + self.ra[i, 2 + half].astype(F32)
                self.part[here] = total.astype(BF16)
        for i in range(3):
            a_axis, b_axis, _ = self.axes(i)
            for k in range(3):
                to = self.p.shifted(b_axis, k + 1)
                self.r.start(
                    3,
                    self.part.at[self.here(i, self.p.at[a_axis], to)],
                    self.rb.at[i, k],
                    self.p.neighbour(b_axis, k + 1),
                )

    def s4(self):
        self.r.wait(3, self.rb)
        for i in range(3):
            a_axis, b_axis, c_axis = self.axes(i)
            total = self.part[self.here(i, self.p.at[a_axis], self.p.at[b_axis])].astype(F32)
            for k in range(3):
                total = total + self.rb[i, k].astype(F32)
            self.rc[i, pl.ds(self.p.at[c_axis], 1)] = total.astype(BF16)[None]
        for i in range(3):
            c_axis = self.axes(i)[2]
            slot = self.rc.at[i, self.p.at[c_axis]]
            for k in range(3):
                self.r.start(4, slot, slot, self.p.neighbour(c_axis, k + 1))

    def s5(self):
        self.r.wait(4, self.rb)
        self.own = []
        for i in range(3):
            total = self.rc[i, 0].astype(F32)
            for k in range(1, 4):
                total = total + self.rc[i, k].astype(F32)
            self.fin[i] = total.astype(BF16)
        for i in range(3):
            a_axis, b_axis, _ = self.axes(i)
            there = self.out.at[self.here(i, self.p.at[a_axis], self.p.at[b_axis])]
            self.own.append(self.local.start(self.fin.at[i], there))
            for k in range(3):
                self.r.start(5, self.fin.at[i], there, self.p.neighbour(b_axis, k + 1))

    def s6(self):
        self.r.wait(5, self.rb)
        for copy in self.own:
            copy.wait()
        for i in range(3):
            axis = self.axes(i)[0]
            there = self.out.at[self.here(i, self.p.at[axis])]
            for k in (1, 3):
                self.r.start(6, there, there, self.p.neighbour(axis, k))

    def s7(self):
        self.r.wait(6, self.ra)
        for i in range(3):
            axis = self.axes(i)[0]
            for half, k in ((0, 3), (1, 1)):
                there = self.out.at[self.here(i, self.p.shifted(axis, k), None, half)]
                self.r.start(7, there, there, self.p.neighbour(axis, 4 - k))
        self.to_sibling(8, (0, 1, 3))

    def to_sibling(self, index, steps):
        for i in range(3):
            for k in steps:
                there = self.out.at[self.here(i, self.p.shifted(self.axes(i)[0], k))]
                self.r.start(index, there, there, self.p.sibling())

    def s8(self):
        self.r.wait(7, self.relay)
        self.to_sibling(9, (2,))

    def s9(self):
        quarter = self.rcore.shape[1] // 4
        self.r.wait(8, self.rcore.at[:, pl.ds(0, 3 * quarter)])
        self.r.wait(9, self.rcore.at[:, pl.ds(0, quarter)])

    def step(self):
        getattr(self, "s%d" % self.step_done)()
        self.step_done += 1


class LatentSession:
    def __init__(self, place, rounds, local, first, other, part, slots, sums, slots2, turned, turned_at, lat, buffers, out):
        self.p, self.r, self.local, self.first, self.other = place, rounds, local, first, other
        self.part, self.slots, self.sums, self.slots2 = part, slots, sums, slots2
        self.turned, self.turned_at, self.lat, self.out = turned, turned_at, lat, out
        self.half, self.rhalf, self.ra, self.rb, self.rc, self.rd, self.fa, self.fb, self.fc, self.fd = buffers
        self.f, self.g = place.at[first], place.at[other]
        self.step_done = 0

    def rows(self, step):
        return pl.ds(pl.multiple_of(320 * self.p.shifted(self.first, step), 64), 320)

    def send(self, step):
        if step > 0:
            self.r.start(0, self.part.at[self.rows(step)], self.slots.at[step - 1], self.p.neighbour(self.first, step))

    def s0(self):
        self.r.wait(0, self.slots)
        total = self.part[self.rows(0)].astype(F32)
        for k in range(3):
            total = total + self.slots[k].astype(F32)
        for k in range(4):
            self.sums[k] = total[80 * k : 80 * k + 80].astype(BF16)
        for k in range(1, 4):
            to = self.p.shifted(self.other, k)
            self.r.start(1, self.sums.at[to], self.slots2.at[k - 1], self.p.neighbour(self.other, k))

    def s1(self):
        self.r.wait(1, self.slots2)
        total = self.sums[self.g].astype(F32)
        for k in range(3):
            total = total + self.slots2[k].astype(F32)
        product = dot(total.astype(BF16), self.lat[...].reshape(LAT, DL), 1, 0).astype(BF16)
        self.half[0] = product[:, :640]
        self.half[1] = product[:, 640:]
        self.r.start(2, self.half.at[1 - self.p.core], self.rhalf, self.p.sibling())
        self.turned[:, self.turned_at : self.turned_at + 80] = total.T

    def s2(self):
        self.r.wait(2, self.rhalf)
        x = self.p.at["x"]
        total = self.half[self.p.core] + self.rhalf[...]
        self.half[self.p.core] = total
        self.rb[pl.ds(x, 1)] = total[0:64, 256:512][None]
        self.rc[pl.ds(x, 1)] = total[0:64, 512:][None]
        self.rd[pl.ds(x, 1)] = total[64:80][None]
        for k in range(1, 4):
            rows = pl.ds(pl.multiple_of(16 * self.p.shifted("x", k), 16), 16)
            self.r.start(
                3, self.half.at[self.p.core, rows, pl.ds(0, 256)], self.ra.at[k - 1], self.p.neighbour("x", k)
            )
        for k in range(1, 4):
            for index, buf in ((4, self.rb), (5, self.rc), (6, self.rd)):
                self.r.start(index, buf.at[x], buf.at[x], self.p.neighbour("x", k))

    def columns(self, start, size):
        return pl.ds(pl.multiple_of(640 * self.p.core + start, 128), size)

    def a_part(self):
        return pl.ds(pl.multiple_of(16 * self.p.at["x"], 16), 16), self.columns(0, 256)

    def b_part(self):
        return pl.ds(0, 64), self.columns(256, 256)

    def c_part(self):
        return pl.ds(0, 64), self.columns(512, 128)

    def d_part(self):
        return pl.ds(64, 16), self.columns(0, 640)

    def same(self, index, *lead):
        rows, cols = ((16, 256), (64, 256), (64, 128), (16, 640))[index]
        return self.out.at[lead + (pl.ds(0, rows), pl.ds(0, cols))]

    def s3(self):
        three = pl.ds(0, 3)
        self.r.wait(3, self.ra)
        total = self.half[self.p.core, self.a_part()[0], 0:256].astype(F32)
        for k in range(3):
            total = total + self.ra[k].astype(F32)
        self.fa[...] = total.astype(BF16)
        for index, buf, fin in ((4, self.rb, self.fb), (5, self.rc, self.fc), (6, self.rd, self.fd)):
            self.r.wait(index, buf.at[three])
            total = buf[0].astype(F32)
            for k in range(1, 4):
                total = total + buf[k].astype(F32)
            fin[...] = total.astype(BF16)
        block = self.out.at[self.f, self.g]
        self.own = []
        for index, fin, part, axis in (
            (7, self.fa, self.a_part(), self.first),
            (9, self.fc, self.c_part(), self.other),
            (10, self.fd, self.d_part(), self.other),
            (8, self.fb, self.b_part(), self.first),
        ):
            there = block.at[part]
            self.own.append(self.local.start(fin, there))
            for k in range(1, 4):
                self.r.start(index, fin, there, self.p.neighbour(axis, k))

    def s4(self):
        three, every = pl.ds(0, 3), slice(None)
        for index in range(4):
            self.r.wait(7 + index, self.same(index, 0, three))
        for copy in self.own:
            copy.wait()
        there = self.out.at[(every, self.g) + self.a_part()]
        for k in range(1, 4):
            self.r.start(11, there, there, self.p.neighbour(self.other, k))
        for index, part in ((13, self.c_part()), (14, self.d_part())):
            there = self.out.at[(self.f, every) + part]
            for k in (1, 3):
                self.r.start(index, there, there, self.p.neighbour(self.first, k))
        there = self.out.at[(every, self.g) + self.b_part()]
        for k in (1, 3):
            self.r.start(12, there, there, self.p.neighbour(self.other, k))

    def s5(self):
        every = slice(None)
        self.r.wait(11, self.same(0, pl.ds(0, 3), every))
        there = self.out.at[(every, every) + self.a_part()]
        for k in (1, 3):
            self.r.start(15, there, there, self.p.neighbour("x", k))

    def x_rows(self, k):
        return pl.ds(pl.multiple_of(16 * self.p.shifted("x", k), 16), 16)

    def to_sibling(self, index, steps):
        every = slice(None)
        for k in steps:
            f, g = self.p.shifted(self.first, k), self.p.shifted(self.other, k)
            for i, where in ((0, (every, g) + self.b_part()), (1, (f, every) + self.c_part()), (2, (f, every) + self.d_part())):
                there = self.out.at[where]
                self.r.start(index + i, there, there, self.p.sibling())

    def a_to_sibling(self, index, steps):
        for k in steps:
            there = self.out.at[:, :, self.x_rows(k), self.columns(0, 256)]
            self.r.start(index, there, there, self.p.sibling())

    def s6(self):
        two, every = pl.ds(0, 2), slice(None)
        self.r.wait(13, self.same(2, two, every))
        self.r.wait(14, self.same(3, two, every))
        for index, part in ((21, self.c_part()), (22, self.d_part())):
            for low, k in ((0, 3), (2, 1)):
                there = self.out.at[(self.p.shifted(self.first, k), pl.ds(low, 2)) + part]
                self.r.start(index, there, there, self.p.neighbour(self.first, 4 - k))
        self.r.wait(12, self.same(1, two, every))
        for low, k in ((0, 3), (2, 1)):
            there = self.out.at[(pl.ds(low, 2), self.p.shifted(self.other, k)) + self.b_part()]
            self.r.start(20, there, there, self.p.neighbour(self.other, 4 - k))
        self.to_sibling(16, (0, 1, 3))

    def s7(self):
        self.r.wait(15, self.out.at[:, :, pl.ds(0, 32), pl.ds(0, 256)])
        for low, k in ((0, 3), (2, 1)):
            there = self.out.at[pl.ds(low, 2), :, self.x_rows(k), self.columns(0, 256)]
            self.r.start(23, there, there, self.p.neighbour("x", 4 - k))
        self.a_to_sibling(19, (0, 1, 3))

    def s8(self):
        for index in (1, 2, 3):
            self.r.wait(19 + index, self.same(index, 0, slice(None)))
        self.to_sibling(24, (2,))

    def s9(self):
        self.r.wait(23, self.same(0, slice(None), slice(None)))
        self.a_to_sibling(27, (2,))

    def s10(self):
        three, every = pl.ds(0, 3), slice(None)
        for index in (1, 2, 3):
            self.r.wait(15 + index, self.same(index, three, every))
            self.r.wait(23 + index, self.same(index, 0, every))
        self.r.wait(19, self.out.at[:, :, pl.ds(0, 48), pl.ds(0, 256)])
        self.r.wait(27, self.same(0, every, every))

    def step(self):
        getattr(self, "s%d" % self.step_done)()
        self.step_done += 1


SUM_ROUNDS = 10
LATENT_ROUNDS = 28
N_LOCAL = 40


def main_kernel(
    lengths,
    gain1,
    gain2,
    queries,
    cotangent,
    latents,
    q_w,
    k_w,
    v_w,
    o_w,
    u_w,
    d_w,
    block_out,
    query_grad,
    latent_grad,
    g_du,
    g_o,
    g_q,
    g_k,
    g_v,
    qin,
    cin,
    lat,
    wq,
    wk,
    wv,
    wo,
    wu,
    wd,
    first,
    query,
    keys,
    values,
    att,
    mixed,
    resid,
    second,
    act,
    gup,
    gout,
    stats,
    gcol,
    part_du,
    part_q,
    part_k,
    part_v,
    rcore_du,
    rcore_o,
    rcore_q,
    relay_du,
    relay_o,
    relay_q,
    ra_du,
    ra_o,
    ra_q,
    rb_du,
    rb_o,
    rb_q,
    rc_du,
    rc_o,
    rc_q,
    fin_du,
    fin_o,
    fin_q,
    slots_k,
    slots_v,
    sums_k,
    sums_v,
    slots2_k,
    slots2_v,
    *rest,
):
    buffers_k, buffers_v = rest[0:10], rest[10:20]
    (
        turned,
        turned_low,
        rturned,
        gathered_k,
        gathered_v,
        du_send,
        du_recv,
        o_send,
        o_recv,
        q_send,
        q_recv,
        k_send,
        k_recv,
        v_send,
        v_recv,
        a_send,
        a_recv,
        local_sem,
    ) = rest[20:]
    p = Place()
    local = Locals(local_sem)
    load_q = [local.start(queries.at[pl.ds(TILE * j, TILE)], qin.at[pl.ds(TILE * j, TILE)]) for j in range(2)]
    z, y = p.at["z"], p.at["y"]
    load_own = local.start(latents, lat.at[z, y])
    load_wq = local.start(q_w, wq)

    barrier = pltpu.get_barrier_semaphore()
    for k in range(1, 16):
        pl.semaphore_signal(barrier, inc=1, device_id=p.in_seq(lax.rem(p.seq + k, 16)), device_id_type=MESH)
    for k in range(1, 4):
        pl.semaphore_signal(barrier, inc=1, device_id=p.neighbour("x", k), device_id_type=MESH)
    pl.semaphore_signal(barrier, inc=1, device_id=p.sibling(), device_id_type=MESH)

    seq = p.seq
    is_long = (seq < 8).astype(jnp.int32)
    lane = lax.broadcasted_iota(jnp.int32, (1, 128), 1)
    for j in range(8):
        item = is_long * lax.div(seq, 2) + (1 - is_long) * (4 + (seq - 8) * 8 + j)
        offset = is_long * (lax.rem(seq, 2) * 1024 + 128 * j)
        stats[0:1, 128 * j : 128 * j + 128] = jnp.where(lane + offset < lengths[0, item], 1.0, 0.0).astype(F32)

    gcol[0] = jnp.broadcast_to(gain1[...].reshape(1, D), (128, D)).T
    gcol[1] = jnp.broadcast_to(gain2[...].reshape(1, D), (128, D)).T
    col1 = gcol[0][:, 0:1]
    col2 = gcol[1][:, 0:1]
    turned[...] = jnp.zeros_like(turned)

    def normalized(x):
        center = x - jnp.mean(x, axis=0, keepdims=True)
        rstd = lax.rsqrt(jnp.mean(center * center, axis=0, keepdims=True) + EPS)
        return center * rstd, rstd

    tiles = [pl.ds(TILE * j, TILE) for j in range(2)]

    def first_part(j):
        t = tiles[j]
        load_q[j].wait()
        x = qin[t, :].T.astype(F32)
        resid[:, t] = x
        n, _ = normalized(x)
        first[:, t] = (n * col1).astype(BF16)

    load_c = local.start(cotangent, cin)
    load_wd = local.start(d_w, wd)
    load_wk = local.start(k_w, wk)
    load_wv = local.start(v_w, wv)
    load_wo = local.start(o_w, wo)
    load_wu = local.start(u_w, wu)
    first_part(0)
    load_own.wait()
    pl.semaphore_wait(barrier, 19)

    early = Rounds(p, a_send, a_recv)
    left, right = pl.ds(0, 640), pl.ds(640, 640)
    for k in range(1, 4):
        early.start(0, lat.at[z, y, :, left], lat.at[z, y, :, left], p.neighbour("y", k))
        early.start(0, lat.at[z, y, :, right], lat.at[z, y, :, right], p.neighbour("z", k))

    def latents_on():
        early.wait(0, lat.at[0, pl.ds(0, 3)])
        for k in range(1, 4):
            early.start(1, lat.at[z, :, :, left], lat.at[z, :, :, left], p.neighbour("z", k))
            early.start(1, lat.at[:, y, :, right], lat.at[:, y, :, right], p.neighbour("y", k))

    first_part(1)
    load_wq.wait()
    for j, t in enumerate(tiles):
        query[:, t] = (dot(wq[...], first[:, t], 0, 0) * SCALE).astype(BF16)
        if j == 0:
            latents_on()
    load_c.wait()
    load_wd.wait()
    for t in tiles:
        gout[:, t] = (stats[0:1, t] * cin[t, :].T.astype(F32)).astype(BF16)
        gup[:, t] = dot(wd[...], gout[:, t], 1, 0).astype(BF16)

    early.wait(1, lat.at[pl.ds(0, 3)])
    all_latents = lat[...].reshape(LAT, DL)
    load_wk.wait()
    keys[...] = dot(all_latents, wk[...], 1, 0).astype(BF16).T
    load_wv.wait()
    values[...] = dot(all_latents, wv[...], 1, 0).astype(BF16).T
    load_wo.wait()
    load_wu.wait()

    def mix(h):
        r = pl.ds(HEAD * h, HEAD)
        mixed[r, :] = dot(values[r, :], att[pl.ds(LAT * h, LAT), :], 1, 0).astype(BF16)

    for h in range(HEADS):
        r = pl.ds(HEAD * h, HEAD)
        for t in tiles:
            s = dot(keys[r, :], query[r, t], 0, 0)
            e = jnp.exp(s - jnp.max(s, axis=0, keepdims=True))
            att[pl.ds(LAT * h, LAT), t] = (e * (1.0 / jnp.sum(e, axis=0, keepdims=True))).astype(BF16)
        if h > 0:
            mix(h - 1)
    mix(HEADS - 1)
    attn_out = [dot(wo[...], mixed[:, t], 0, 0) for t in tiles]
    for j, t in enumerate(tiles):
        x = resid[:, t] + attn_out[j]
        resid[:, t] = x
        mu = jnp.mean(x, axis=0, keepdims=True)
        center = x - mu
        rstd = lax.rsqrt(jnp.mean(center * center, axis=0, keepdims=True) + EPS)
        stats[1:2, t] = mu
        stats[2:3, t] = rstd
        second[:, t] = (center * rstd * col2).astype(BF16)
        up = dot(wu[...], second[:, t], 0, 0)
        cdf = 0.5 * (1.0 + lax.erf(up * (0.5**0.5)))
        act[:, t] = (up * cdf).astype(BF16)
        slope = cdf + up * (jnp.exp(-0.5 * up * up) * 0.3989422804014327)
        gup[:, t] = (slope * gup[:, t].astype(F32)).astype(BF16)

    part_o = wk.at[:, pl.ds(0, D)]
    du = SumSession(
        p,
        Rounds(p, du_send, du_recv),
        local,
        "rows",
        ORDERS["du"],
        1536,
        part_du,
        rcore_du,
        relay_du,
        ra_du,
        rb_du,
        rc_du,
        fin_du,
        g_du,
    )
    so = SumSession(
        p,
        Rounds(p, o_send, o_recv),
        local,
        "cols",
        ORDERS["o"],
        D,
        part_o,
        rcore_o,
        relay_o,
        ra_o,
        rb_o,
        rc_o,
        fin_o,
        g_o,
    )
    sq = SumSession(
        p,
        Rounds(p, q_send, q_recv),
        local,
        "rows",
        ORDERS["q"],
        DL,
        part_q,
        rcore_q,
        relay_q,
        ra_q,
        rb_q,
        rc_q,
        fin_q,
        g_q,
    )
    sk = LatentSession(
        p,
        Rounds(p, k_send, k_recv),
        local,
        "y",
        "z",
        part_k,
        slots_k,
        sums_k,
        slots2_k,
        turned,
        0,
        lat,
        buffers_k,
        g_k,
    )
    sv = LatentSession(
        p,
        Rounds(p, v_send, v_recv),
        local,
        "z",
        "y",
        part_v,
        slots_v,
        sums_v,
        slots2_v,
        turned,
        128,
        lat,
        buffers_v,
        g_v,
    )
    gal = second
    gm = wv.at[:, pl.ds(0, ROWS)]
    stores = []

    def heads_of(axis, j):
        for i in range(2):
            h = 2 * p.shifted(axis, j) + i
            yield pl.ds(pl.multiple_of(h * HEAD, 32), HEAD), pl.ds(pl.multiple_of(h * LAT, 256), LAT)

    def mlp_back(j):
        t = tiles[j]
        gg = dot(wu[...], gup[:, t], 1, 0) * col2
        rstd = stats[2:3, t]
        n = (resid[:, t] - stats[1:2, t]) * rstd
        mean_gg = jnp.mean(gg, axis=0, keepdims=True)
        mean_ggn = jnp.mean(gg * n, axis=0, keepdims=True)
        gal[:, t] = (gout[:, t].astype(F32) + rstd * (gg - mean_gg - n * mean_ggn)).astype(BF16)

    def mixed_back(j):
        gm[:, tiles[j]] = dot(wo[...], gal[:, tiles[j]], 1, 0).astype(BF16)

    def value_heads(j):
        for r, l in heads_of("z", j):
            part_v[r, :] = dot(gm[r, :], att[l, :], 1, 1).astype(BF16)
        sv.send(j)

    def key_heads(j):
        for r, l in heads_of("y", j):
            for t in tiles:
                ga = dot(values[r, :], gm[r, t], 0, 0)
                a = att[l, t].astype(F32)
                att[l, t] = (a * (ga - jnp.sum(ga * a, axis=0, keepdims=True))).astype(BF16)
            part_k[r, :] = dot(query[r, :], att[l, :], 1, 1).astype(BF16)
        sk.send(j)

    def query_back(j):
        for h in range(4 * j, 4 * j + 4):
            r = pl.ds(h * HEAD, HEAD)
            gm[r, :] = dot(keys[r, :], att[pl.ds(h * LAT, LAT), :], 1, 0).astype(BF16)

    def query_weight(j):
        c = pl.ds(640 * j, 640)
        part_q[:, c] = (dot(first[...], gm[c, :], 1, 1) * SCALE).astype(BF16)

    def out_weight(j):
        c = pl.ds(640 * j, 640)
        wk[c, 0:D] = dot(mixed[c, :], gal[...], 1, 1).astype(BF16)

    def query_out(j):
        t = tiles[j]
        gg = dot(wq[...], gm[:, t], 1, 0) * (col1 * SCALE)
        n, rstd = normalized(qin[t, :].T.astype(F32))
        mean_gg = jnp.mean(gg, axis=0, keepdims=True)
        mean_ggn = jnp.mean(gg * n, axis=0, keepdims=True)
        total = gal[:, t].astype(F32) + rstd * (gg - mean_gg - n * mean_ggn)
        qin[t, :] = total.astype(BF16).T
        stores.append(local.start(qin.at[t], query_grad.at[t]))

    def block(j):
        t = tiles[j]
        out = stats[0:1, t] * (resid[:, t] + dot(wd[...], act[:, t], 0, 0))
        cin[t, :] = out.astype(BF16).T
        stores.append(local.start(cin.at[t], block_out.at[t]))

    def turn_send(j):
        turned_low[...] = turned[...].astype(BF16)
        for k in range(1, 16):
            who = lax.rem(seq + k, 16)
            mine = turned_low.at[pl.ds(pl.multiple_of(who * 16, 16), 16)]
            early.start(2, mine, rturned.at[seq], p.in_seq(who))
        rturned[pl.ds(seq, 1)] = turned_low[pl.ds(pl.multiple_of(seq * 16, 16), 16), :][None]

    reload = []

    def load_again(j):
        so.r.drain((0, 1, 2, 3))
        reload.append(local.start(k_w, wk))
        reload.append(local.start(v_w, wv))

    def latent_back(j):
        early.wait(2, rturned.at[pl.ds(0, 15)])
        for i in range(16):
            piece = rturned[i].astype(F32).T
            gathered_k[pl.ds(80 * (4 * (i % 4) + i // 4), 80), :] = piece[0:80, :]
            gathered_v[pl.ds(80 * i, 80), :] = piece[128:208, :]
        for load in reload:
            load.wait()
        latent_grad[...] = dot(gathered_k[...].T.astype(BF16), wk[...], 1, 1) + dot(
            gathered_v[...].T.astype(BF16), wv[...], 1, 1
        )

    def down_up(j):
        part_du[:, 0:D] = dot(act[...], gout[...], 1, 1).astype(BF16)
        part_du[:, D:] = dot(second[...], gup[...], 1, 1).astype(BF16)

    parts = {
        "w": down_up,
        "b": mlp_back,
        "m": mixed_back,
        "V": value_heads,
        "K": key_heads,
        "g": query_back,
        "Q": query_weight,
        "O": out_weight,
        "x": query_out,
        "B": block,
        "T": turn_send,
        "R": load_again,
        "L": latent_back,
    }
    sessions = {"d": du, "o": so, "q": sq, "k": sk, "v": sv}
    for item in PLAN:
        if item in sessions:
            sessions[item].step()
        else:
            parts[item[0]](int(item[1]))
    for copy in stores:
        copy.wait()
    early.drain()
    for session in (du, so, sq, sk, sv):
        session.r.drain()
    assert [s.step_done for s in (du, so, sq, sk, sv)] == [10, 10, 10, 11, 11]


def convert_kernel(
    gain1,
    gain2,
    du,
    o,
    q,
    k,
    v,
    u_w,
    q_w,
    block,
    query,
    latent,
    out_q,
    out_k,
    out_v,
    out_o,
    out_u,
    out_d,
    out_block,
    out_query,
    out_latent,
    out_g1,
    out_g2,
):
    high = out_q.shape[0]
    at = pl.ds(pl.multiple_of(pl.program_id(0) * high, 128), high)

    def per_row(product, gain):
        total = jnp.sum(product, axis=1, keepdims=True)
        return (jnp.broadcast_to(total, (high, 128)).T[0:1, :] / gain.reshape(1, high)).reshape(high)

    out_d[...] = du[:, 0:D].astype(F32)
    up = du[:, D:].astype(F32)
    out_u[...] = up
    out_g2[at] = per_row(up * u_w[...].astype(F32), gain2[at])
    value = q[...].astype(F32)
    out_q[...] = value
    out_g1[at] = per_row(value * q_w[...].astype(F32), gain1[at])
    out_o[...] = o[...].astype(F32)
    out_k[...] = k[...].T.astype(F32)
    out_v[...] = v[...].T.astype(F32)
    out_block[...] = block[...]
    out_query[...] = query[...].astype(F32)
    out_latent[...] = latent[...]


def vm(shape, dtype=BF16):
    return pltpu.VMEM(shape, dtype)


def on_device(queries, latents, lengths, q_w, k_w, v_w, o_w, u_w, d_w, gain1, gain2, cotangent):
    any_spec = pl.BlockSpec(memory_space=pl.ANY)
    vmem_spec = pl.BlockSpec(memory_space=pltpu.VMEM)
    dma = pltpu.SemaphoreType.DMA
    sds = jax.ShapeDtypeStruct
    outs = pl.pallas_call(
        main_kernel,
        out_shape=(
            sds((ROWS, D), BF16),
            sds((ROWS, D), BF16),
            sds((16, DL), F32),
            sds((D, 1536), BF16),
            sds((DL, D), BF16),
            sds((D, DL), BF16),
            sds((4, 4, 80, DL), BF16),
            sds((4, 4, 80, DL), BF16),
        ),
        in_specs=[pl.BlockSpec(memory_space=pltpu.SMEM), vmem_spec, vmem_spec] + [any_spec] * 9,
        out_specs=(any_spec, any_spec, vmem_spec) + (any_spec,) * 5,
        scratch_shapes=[
            vm((ROWS, D)),
            vm((ROWS, D)),
            vm((4, 4, 16, DL)),
            vm((D, DL)),
            vm((DL, DL)),
            vm((DL, DL)),
            vm((DL, D)),
            vm((D, D)),
            vm((D, D)),
            vm((D, ROWS)),
            vm((DL, ROWS)),
            vm((DL, LAT)),
            vm((DL, LAT)),
            vm((HEADS * LAT, ROWS)),
            vm((DL, ROWS)),
            vm((D, ROWS), F32),
            vm((D, ROWS)),
            vm((D, ROWS)),
            vm((D, ROWS)),
            vm((D, ROWS)),
            vm((8, ROWS), F32),
            vm((2, D, 128), F32),
            vm((D, 1536)),
            vm((D, DL)),
            vm((DL, LAT)),
            vm((DL, LAT)),
            vm((3, 128, 1536)),
            vm((3, 640, 256)),
            vm((3, 128, DL)),
            vm((3, 2, 16, 1536)),
            vm((3, 2, 80, 256)),
            vm((3, 2, 16, DL)),
            vm((3, 4, 16, 1536)),
            vm((3, 4, 80, 256)),
            vm((3, 4, 16, DL)),
            vm((3, 3, 16, 768)),
            vm((3, 3, 80, 128)),
            vm((3, 3, 16, 640)),
            vm((3, 4, 16, 768)),
            vm((3, 4, 80, 128)),
            vm((3, 4, 16, 640)),
            vm((3, 16, 768)),
            vm((3, 80, 128)),
            vm((3, 16, 640)),
            vm((3, 320, LAT)),
            vm((3, 320, LAT)),
            vm((4, 80, LAT)),
            vm((4, 80, LAT)),
            vm((3, 80, LAT)),
            vm((3, 80, LAT)),
        ]
        + [
            vm((2, 80, 640)),
            vm((80, 640)),
            vm((3, 16, 256)),
            vm((4, 64, 256)),
            vm((4, 64, 128)),
            vm((4, 16, 640)),
            vm((16, 256)),
            vm((64, 256)),
            vm((64, 128)),
            vm((16, 640)),
        ]
        * 2
        + [
            vm((LAT, 256), F32),
            vm((LAT, 256)),
            vm((16, 16, 256)),
            vm((DL, 16), F32),
            vm((DL, 16), F32),
        ]
        + [dma((SUM_ROUNDS,))] * 6
        + [dma((LATENT_ROUNDS,))] * 4
        + [dma((3,)), dma((3,)), dma((N_LOCAL,))],
        compiler_params=pltpu.CompilerParams(
            collective_id=0, has_side_effects=True, vmem_limit_bytes=VMEM_LIMIT
        ),
        name="decoder_block",
    )(lengths, gain1, gain2, queries[0], cotangent[0], latents[0], q_w, k_w, v_w, o_w, u_w, d_w)
    block_out, query_grad, latent_grad, g_du, g_o, g_q, g_k, g_v = outs

    def by_rows(rows, columns):
        return pl.BlockSpec((rows // 2, columns), lambda i: (i, 0))

    by_columns = pl.BlockSpec((DL, DL // 2), lambda i: (0, i))
    whole = pl.BlockSpec((D,), lambda i: (0,))
    latent_spec = pl.BlockSpec((16, DL), lambda i: (0, 0))
    conv = pl.pallas_call(
        convert_kernel,
        out_shape=(
            sds((D, DL), F32),
            sds((DL, DL), F32),
            sds((DL, DL), F32),
            sds((DL, D), F32),
            sds((D, D), F32),
            sds((D, D), F32),
            sds((ROWS, D), BF16),
            sds((ROWS, D), F32),
            sds((16, DL), F32),
            sds((D,), F32),
            sds((D,), F32),
        ),
        grid=(2,),
        in_specs=[whole, whole]
        + [by_rows(*shape) for shape in ((D, 1536), (DL, D), (D, DL))]
        + [by_columns, by_columns]
        + [by_rows(*shape) for shape in ((D, D), (D, DL), (ROWS, D), (ROWS, D))]
        + [latent_spec],
        out_specs=tuple(
            by_rows(*shape)
            for shape in ((D, DL), (DL, DL), (DL, DL), (DL, D), (D, D), (D, D), (ROWS, D), (ROWS, D))
        )
        + (latent_spec, whole, whole),
        compiler_params=pltpu.CompilerParams(vmem_limit_bytes=VMEM_LIMIT),
        name="to_float32",
    )(
        gain1,
        gain2,
        g_du,
        g_o,
        g_q,
        g_k.reshape(DL, DL),
        g_v.reshape(DL, DL),
        u_w,
        q_w,
        block_out,
        query_grad,
        latent_grad,
    )
    q_grad, k_grad, v_grad, o_grad, u_grad, d_grad, block_out, query_grad, latent_grad, g1_grad, g2_grad = conv
    return (
        block_out[None],
        query_grad[None],
        latent_grad[None],
        q_grad,
        k_grad,
        v_grad,
        o_grad,
        u_grad,
        d_grad,
        g1_grad,
        g2_grad,
    )


def solution(mesh):
    rows = P("dp", "seq", None)
    in_specs = (rows, rows, P("dp", None)) + (P(),) * 8 + (rows,)
    out_specs = (rows, rows, rows) + (P(),) * 8
    return jax.shard_map(on_device, mesh=mesh, in_specs=in_specs, out_specs=out_specs, check_vma=False)
```

```python
import functools

import jax
import jax.numpy as jnp
from jax import lax
from jax.experimental import pallas as pl
from jax.experimental.pallas import tpu as pltpu
from jax.sharding import PartitionSpec as P

MESH = pl.DeviceIdType.MESH
F32 = jnp.float32
BF16 = jnp.bfloat16
HEADS = 8
HEAD = 160
LAT = 256
ROWS = 1024
TILE = 512
D = 768
DL = 1280
SCALE = HEAD ** (-0.5)
EPS = 1e-5
VMEM_LIMIT = 63 * 2**20
ORDERS = {
    "du": ("xyz", "yzx", "zxy"),
    "o": ("xyz", "yzx", "zxy"),
    "q": ("xyz", "yzx", "zxy"),
}
PLAN = (
    "w0", "b0", "d", "b1", "m0", "m1", "V0", "V1", "V2", "d", "V3", "K0",
    "K1", "K2", "O0", "O1", "o", "K3", "v", "g0", "g1", "d", "Q0", "o",
    "Q1", "v", "d", "q", "o", "k", "v", "q", "o", "d", "k", "v",
    "q", "k", "T0", "o", "B0", "d", "q", "v", "x0", "k", "o", "v",
    "B1", "q", "d", "k", "q", "v", "v", "k", "x1", "o", "R0", "q",
    "k", "d", "k", "v", "L0", "v", "q", "o", "k", "d", "k", "v",
    "q", "o", "k", "q", "d", "o",
)


def dot(left, right, left_dim, right_dim):
    return lax.dot_general(
        left, right, (((left_dim,), (right_dim,)), ((), ())), preferred_element_type=F32
    )


class Place:
    def __init__(self):
        dp = lax.axis_index("dp")
        sq = lax.axis_index("seq")
        self.seq = sq
        self.dp = dp
        self.core = lax.rem(dp, 2)
        self.at = {"x": lax.div(dp, 2), "y": lax.rem(sq, 4), "z": lax.div(sq, 4)}

    def shifted(self, axis, step):
        return lax.rem(self.at[axis] + step, 4)

    def neighbour(self, axis, step):
        to = dict(self.at)
        to[axis] = self.shifted(axis, step)
        return (to["x"] * 2 + self.core, to["z"] * 4 + to["y"])

    def sibling(self):
        return (self.dp + 1 - 2 * self.core, self.seq)

    def in_seq(self, index):
        return (self.dp, index)


class Rounds:
    def __init__(self, place, send, recv):
        self.place, self.send, self.recv, self.size = place, send, recv, {}

    def copy(self, index, src, dst, device):
        return pltpu.make_async_remote_copy(
            src_ref=src,
            dst_ref=dst,
            send_sem=self.send.at[index],
            recv_sem=self.recv.at[index],
            device_id=device,
            device_id_type=MESH,
        )

    def start(self, index, src, dst, device):
        self.copy(index, src, dst, device).start()

    def wait(self, index, same_size):
        self.size[index] = same_size
        self.copy(index, same_size, same_size, self.place.sibling()).wait_recv()

    def drain(self, only=None):
        for index in list(self.size) if only is None else only:
            same_size = self.size.pop(index)
            self.copy(index, same_size, same_size, self.place.sibling()).wait_send()


class Locals:
    def __init__(self, sems):
        self.sems, self.used = sems, 0

    def start(self, src, dst):
        copy = pltpu.make_async_copy(src, dst, self.sems.at[self.used])
        self.used += 1
        copy.start()
        return copy


class SumSession:
    def __init__(self, place, rounds, local, kind, orders, width, part, rcore, relay, ra, rb, rc, fin, out):
        self.p, self.r, self.local = place, rounds, local
        self.kind, self.orders, self.width = kind, orders, width
        self.part, self.rcore, self.relay, self.ra, self.rb, self.rc = part, rcore, relay, ra, rb, rc
        self.fin, self.out = fin, out
        self.step_done = 0

    def region(self, i, c, a=None, b=None, half=None):
        if self.kind == "rows":
            row, high, col, wide = 256 * i + 128 * c, 128, 0, self.width
            if a is not None:
                row, high = row + 32 * a, 32
            if half is not None:
                row, high = row + 16 * half, 16
            if b is not None:
                row, high = row + 16 * lax.div(b, 2), 16
                wide = self.width // 2
                col = pl.multiple_of(lax.rem(b, 2) * wide, 128)
        else:
            row, high, col, wide = 640 * c, 640, 256 * i, 256
            if a is not None:
                row, high = row + 160 * a, 160
            if half is not None:
                row, high = row + 80 * half, 80
            if b is not None:
                row, high = row + 80 * lax.div(b, 2), 80
                wide = 128
                col = pl.multiple_of(256 * i + 128 * lax.rem(b, 2), 128)
        return pl.ds(pl.multiple_of(row, 16), high), pl.ds(col, wide)

    def here(self, i, *rest):
        return self.region(i, self.p.core, *rest)

    def axes(self, i):
        return self.orders[i]

    def s0(self):
        for i in range(3):
            self.r.start(0, self.part.at[self.region(i, 1 - self.p.core)], self.rcore.at[i], self.p.sibling())

    def s1(self):
        self.r.wait(0, self.rcore)
        for i in range(3):
            here = self.here(i)
            self.part[here] = self.part[here] + self.rcore[i]
        for i in range(3):
            axis = self.axes(i)[0]
            up, down = self.p.neighbour(axis, 1), self.p.neighbour(axis, 3)
            at = [self.p.shifted(axis, k) for k in range(4)]
            self.r.start(1, self.part.at[self.here(i, at[2], None, 0)], self.relay.at[i, 0], down)
            self.r.start(1, self.part.at[self.here(i, at[2], None, 1)], self.relay.at[i, 1], up)
            self.r.start(2, self.part.at[self.here(i, at[1], None, 0)], self.ra.at[i, 0], up)
            self.r.start(2, self.part.at[self.here(i, at[3], None, 1)], self.ra.at[i, 1], down)

    def s2(self):
        self.r.wait(1, self.relay)
        for i in range(3):
            axis = self.axes(i)[0]
            for half, k in ((0, 3), (1, 1)):
                there = self.here(i, self.p.shifted(axis, k), None, half)
                self.part[there] = self.part[there] + self.relay[i, half]
                self.r.start(2, self.part.at[there], self.ra.at[i, 2 + half], self.p.neighbour(axis, k))

    def s3(self):
        self.r.wait(2, self.ra)
        for i in range(3):
            a = self.p.at[self.axes(i)[0]]
            for half in range(2):
                here = self.here(i, a, None, half)
                total = self.part[here].astype(F32) + self.ra[i, half].astype(F32) + self.ra[i, 2 + half].astype(F32)
                self.part[here] = total.astype(BF16)
        for i in range(3):
            a_axis, b_axis, _ = self.axes(i)
            for k in range(3):
                to = self.p.shifted(b_axis, k + 1)
                self.r.start(
                    3,
                    self.part.at[self.here(i, self.p.at[a_axis], to)],
                    self.rb.at[i, k],
                    self.p.neighbour(b_axis, k + 1),
                )

    def s4(self):
        self.r.wait(3, self.rb)
        for i in range(3):
            a_axis, b_axis, c_axis = self.axes(i)
            total = self.part[self.here(i, self.p.at[a_axis], self.p.at[b_axis])].astype(F32)
            for k in range(3):
                total = total + self.rb[i, k].astype(F32)
            self.rc[i, pl.ds(self.p.at[c_axis], 1)] = total.astype(BF16)[None]
        for i in range(3):
            c_axis = self.axes(i)[2]
            slot = self.rc.at[i, self.p.at[c_axis]]
            for k in range(3):
                self.r.start(4, slot, slot, self.p.neighbour(c_axis, k + 1))

    def s5(self):
        self.r.wait(4, self.rb)
        self.own = []
        for i in range(3):
            total = self.rc[i, 0].astype(F32)
            for k in range(1, 4):
                total = total + self.rc[i, k].astype(F32)
            self.fin[i] = total.astype(BF16)
        for i in range(3):
            a_axis, b_axis, _ = self.axes(i)
            there = self.out.at[self.here(i, self.p.at[a_axis], self.p.at[b_axis])]
            self.own.append(self.local.start(self.fin.at[i], there))
            for k in range(3):
                self.r.start(5, self.fin.at[i], there, self.p.neighbour(b_axis, k + 1))

    def s6(self):
        self.r.wait(5, self.rb)
        for copy in self.own:
            copy.wait()
        for i in range(3):
            axis = self.axes(i)[0]
            there = self.out.at[self.here(i, self.p.at[axis])]
            for k in (1, 3):
                self.r.start(6, there, there, self.p.neighbour(axis, k))

    def s7(self):
        self.r.wait(6, self.ra)
        for i in range(3):
            axis = self.axes(i)[0]
            for half, k in ((0, 3), (1, 1)):
                there = self.out.at[self.here(i, self.p.shifted(axis, k), None, half)]
                self.r.start(7, there, there, self.p.neighbour(axis, 4 - k))
        self.to_sibling(8, (0, 1, 3))

    def to_sibling(self, index, steps):
        for i in range(3):
            for k in steps:
                there = self.out.at[self.here(i, self.p.shifted(self.axes(i)[0], k))]
                self.r.start(index, there, there, self.p.sibling())

    def s8(self):
        self.r.wait(7, self.relay)
        self.to_sibling(9, (2,))

    def s9(self):
        quarter = self.rcore.shape[1] // 4
        self.r.wait(8, self.rcore.at[:, pl.ds(0, 3 * quarter)])
        self.r.wait(9, self.rcore.at[:, pl.ds(0, quarter)])

    def step(self):
        getattr(self, "s%d" % self.step_done)()
        self.step_done += 1


class LatentSession:
    def __init__(self, place, rounds, local, first, other, part, slots, sums, slots2, turned, turned_at, lat, buffers, out):
        self.p, self.r, self.local, self.first, self.other = place, rounds, local, first, other
        self.part, self.slots, self.sums, self.slots2 = part, slots, sums, slots2
        self.turned, self.turned_at, self.lat, self.out = turned, turned_at, lat, out
        self.half, self.rhalf, self.ra, self.rb, self.rc, self.rd, self.fa, self.fb, self.fc, self.fd = buffers
        self.f, self.g = place.at[first], place.at[other]
        self.step_done = 0

    def rows(self, step):
        return pl.ds(pl.multiple_of(320 * self.p.shifted(self.first, step), 64), 320)

    def send(self, step):
        if step > 0:
            self.r.start(0, self.part.at[self.rows(step)], self.slots.at[step - 1], self.p.neighbour(self.first, step))

    def s0(self):
        self.r.wait(0, self.slots)
        total = self.part[self.rows(0)].astype(F32)
        for k in range(3):
            total = total + self.slots[k].astype(F32)
        for k in range(4):
            self.sums[k] = total[80 * k : 80 * k + 80].astype(BF16)
        for k in range(1, 4):
            to = self.p.shifted(self.other, k)
            self.r.start(1, self.sums.at[to], self.slots2.at[k - 1], self.p.neighbour(self.other, k))

    def s1(self):
        self.r.wait(1, self.slots2)
        total = self.sums[self.g].astype(F32)
        for k in range(3):
            total = total + self.slots2[k].astype(F32)
        product = dot(total.astype(BF16), self.lat[...].reshape(LAT, DL), 1, 0).astype(BF16)
        self.half[0] = product[:, :640]
        self.half[1] = product[:, 640:]
        self.r.start(2, self.half.at[1 - self.p.core], self.rhalf, self.p.sibling())
        self.turned[:, self.turned_at : self.turned_at + 80] = total.T

    def s2(self):
        self.r.wait(2, self.rhalf)
        x = self.p.at["x"]
        total = self.half[self.p.core] + self.rhalf[...]
        self.half[self.p.core] = total
        self.rb[pl.ds(x, 1)] = total[0:64, 256:512][None]
        self.rc[pl.ds(x, 1)] = total[0:64, 512:][None]
        self.rd[pl.ds(x, 1)] = total[64:80][None]
        for k in range(1, 4):
            rows = pl.ds(pl.multiple_of(16 * self.p.shifted("x", k), 16), 16)
            self.r.start(
                3, self.half.at[self.p.core, rows, pl.ds(0, 256)], self.ra.at[k - 1], self.p.neighbour("x", k)
            )
        for k in range(1, 4):
            for index, buf in ((4, self.rb), (5, self.rc), (6, self.rd)):
                self.r.start(index, buf.at[x], buf.at[x], self.p.neighbour("x", k))

    def columns(self, start, size):
        return pl.ds(pl.multiple_of(640 * self.p.core + start, 128), size)

    def a_part(self):
        return pl.ds(pl.multiple_of(16 * self.p.at["x"], 16), 16), self.columns(0, 256)

    def b_part(self):
        return pl.ds(0, 64), self.columns(256, 256)

    def c_part(self):
        return pl.ds(0, 64), self.columns(512, 128)

    def d_part(self):
        return pl.ds(64, 16), self.columns(0, 640)

    def same(self, index, *lead):
        rows, cols = ((16, 256), (64, 256), (64, 128), (16, 640))[index]
        return self.out.at[lead + (pl.ds(0, rows), pl.ds(0, cols))]

    def s3(self):
        three = pl.ds(0, 3)
        self.r.wait(3, self.ra)
        total = self.half[self.p.core, self.a_part()[0], 0:256].astype(F32)
        for k in range(3):
            total = total + self.ra[k].astype(F32)
        self.fa[...] = total.astype(BF16)
        for index, buf, fin in ((4, self.rb, self.fb), (5, self.rc, self.fc), (6, self.rd, self.fd)):
            self.r.wait(index, buf.at[three])
            total = buf[0].astype(F32)
            for k in range(1, 4):
                total = total + buf[k].astype(F32)
            fin[...] = total.astype(BF16)
        block = self.out.at[self.f, self.g]
        self.own = []
        for index, fin, part, axis in (
            (7, self.fa, self.a_part(), self.first),
            (9, self.fc, self.c_part(), self.other),
            (10, self.fd, self.d_part(), self.other),
            (8, self.fb, self.b_part(), self.first),
        ):
            there = block.at[part]
            self.own.append(self.local.start(fin, there))
            for k in range(1, 4):
                self.r.start(index, fin, there, self.p.neighbour(axis, k))

    def s4(self):
        three, every = pl.ds(0, 3), slice(None)
        for index in range(4):
            self.r.wait(7 + index, self.same(index, 0, three))
        for copy in self.own:
            copy.wait()
        there = self.out.at[(every, self.g) + self.a_part()]
        for k in range(1, 4):
            self.r.start(11, there, there, self.p.neighbour(self.other, k))
        for index, part in ((13, self.c_part()), (14, self.d_part())):
            there = self.out.at[(self.f, every) + part]
            for k in (1, 3):
                self.r.start(index, there, there, self.p.neighbour(self.first, k))
        there = self.out.at[(every, self.g) + self.b_part()]
        for k in (1, 3):
            self.r.start(12, there, there, self.p.neighbour(self.other, k))

    def s5(self):
        every = slice(None)
        self.r.wait(11, self.same(0, pl.ds(0, 3), every))
        there = self.out.at[(every, every) + self.a_part()]
        for k in (1, 3):
            self.r.start(15, there, there, self.p.neighbour("x", k))

    def x_rows(self, k):
        return pl.ds(pl.multiple_of(16 * self.p.shifted("x", k), 16), 16)

    def to_sibling(self, index, steps):
        every = slice(None)
        for k in steps:
            f, g = self.p.shifted(self.first, k), self.p.shifted(self.other, k)
            for i, where in ((0, (every, g) + self.b_part()), (1, (f, every) + self.c_part()), (2, (f, every) + self.d_part())):
                there = self.out.at[where]
                self.r.start(index + i, there, there, self.p.sibling())

    def a_to_sibling(self, index, steps):
        for k in steps:
            there = self.out.at[:, :, self.x_rows(k), self.columns(0, 256)]
            self.r.start(index, there, there, self.p.sibling())

    def s6(self):
        two, every = pl.ds(0, 2), slice(None)
        self.r.wait(13, self.same(2, two, every))
        self.r.wait(14, self.same(3, two, every))
        for index, part in ((21, self.c_part()), (22, self.d_part())):
            for low, k in ((0, 3), (2, 1)):
                there = self.out.at[(self.p.shifted(self.first, k), pl.ds(low, 2)) + part]
                self.r.start(index, there, there, self.p.neighbour(self.first, 4 - k))
        self.r.wait(12, self.same(1, two, every))
        for low, k in ((0, 3), (2, 1)):
            there = self.out.at[(pl.ds(low, 2), self.p.shifted(self.other, k)) + self.b_part()]
            self.r.start(20, there, there, self.p.neighbour(self.other, 4 - k))
        self.to_sibling(16, (0, 1, 3))

    def s7(self):
        self.r.wait(15, self.out.at[:, :, pl.ds(0, 32), pl.ds(0, 256)])
        for low, k in ((0, 3), (2, 1)):
            there = self.out.at[pl.ds(low, 2), :, self.x_rows(k), self.columns(0, 256)]
            self.r.start(23, there, there, self.p.neighbour("x", 4 - k))
        self.a_to_sibling(19, (0, 1, 3))

    def s8(self):
        for index in (1, 2, 3):
            self.r.wait(19 + index, self.same(index, 0, slice(None)))
        self.to_sibling(24, (2,))

    def s9(self):
        self.r.wait(23, self.same(0, slice(None), slice(None)))
        self.a_to_sibling(27, (2,))

    def s10(self):
        three, every = pl.ds(0, 3), slice(None)
        for index in (1, 2, 3):
            self.r.wait(15 + index, self.same(index, three, every))
            self.r.wait(23 + index, self.same(index, 0, every))
        self.r.wait(19, self.out.at[:, :, pl.ds(0, 48), pl.ds(0, 256)])
        self.r.wait(27, self.same(0, every, every))

    def step(self):
        getattr(self, "s%d" % self.step_done)()
        self.step_done += 1


SUM_ROUNDS = 10
LATENT_ROUNDS = 28
N_LOCAL = 36


def main_kernel(
    lengths,
    gain1_in,
    gain2_in,
    queries,
    cotangent,
    latents,
    q_w,
    k_w,
    v_w,
    o_w,
    u_w,
    d_w,
    block_out,
    query_grad,
    latent_grad,
    g_du,
    g_o,
    g_q,
    g_k,
    g_v,
    qin,
    cin,
    lat,
    wq,
    wk,
    wv,
    wo,
    wu,
    wd,
    first,
    query,
    keys,
    values,
    att,
    mixed,
    resid,
    second,
    act,
    gup,
    gout,
    stats,
    gcol,
    part_du,
    part_q,
    part_k,
    part_v,
    rcore_du,
    rcore_o,
    rcore_q,
    relay_du,
    relay_o,
    relay_q,
    ra_du,
    ra_o,
    ra_q,
    rb_du,
    rb_o,
    rb_q,
    rc_du,
    rc_o,
    rc_q,
    fin_du,
    fin_o,
    fin_q,
    slots_k,
    slots_v,
    sums_k,
    sums_v,
    slots2_k,
    slots2_v,
    *rest,
):
    buffers_k, buffers_v = rest[0:10], rest[10:20]
    (
        turned,
        turned_low,
        rturned,
        gathered_k,
        gathered_v,
        latent_sum,
        gain1,
        gain2,
        du_send,
        du_recv,
        o_send,
        o_recv,
        q_send,
        q_recv,
        k_send,
        k_recv,
        v_send,
        v_recv,
        a_send,
        a_recv,
        local_sem,
    ) = rest[20:]
    p = Place()
    local = Locals(local_sem)
    load_q = [local.start(queries.at[pl.ds(TILE * j, TILE)], qin.at[pl.ds(TILE * j, TILE)]) for j in range(2)]
    z, y = p.at["z"], p.at["y"]
    load_own = local.start(latents, lat.at[z, y])
    load_g = [local.start(gain1_in, gain1), local.start(gain2_in, gain2)]
    load_wq = local.start(q_w, wq)

    barrier = pltpu.get_barrier_semaphore()
    for k in range(1, 16):
        pl.semaphore_signal(barrier, inc=1, device_id=p.in_seq(lax.rem(p.seq + k, 16)), device_id_type=MESH)
    for k in range(1, 4):
        pl.semaphore_signal(barrier, inc=1, device_id=p.neighbour("x", k), device_id_type=MESH)
    pl.semaphore_signal(barrier, inc=1, device_id=p.sibling(), device_id_type=MESH)

    seq = p.seq
    is_long = (seq < 8).astype(jnp.int32)
    lane = lax.broadcasted_iota(jnp.int32, (1, 128), 1)
    for j in range(8):
        item = is_long * lax.div(seq, 2) + (1 - is_long) * (4 + (seq - 8) * 8 + j)
        offset = is_long * (lax.rem(seq, 2) * 1024 + 128 * j)
        stats[0:1, 128 * j : 128 * j + 128] = jnp.where(lane + offset < lengths[0, item], 1.0, 0.0).astype(F32)

    for load in load_g:
        load.wait()
    gcol[0] = jnp.broadcast_to(gain1[...].reshape(1, D), (128, D)).T
    gcol[1] = jnp.broadcast_to(gain2[...].reshape(1, D), (128, D)).T
    col1 = gcol[0][:, 0:1]
    col2 = gcol[1][:, 0:1]
    turned[...] = jnp.zeros_like(turned)

    def normalized(x):
        center = x - jnp.mean(x, axis=0, keepdims=True)
        rstd = lax.rsqrt(jnp.mean(center * center, axis=0, keepdims=True) + EPS)
        return center * rstd, rstd

    tiles = [pl.ds(TILE * j, TILE) for j in range(2)]

    def first_part(j):
        t = tiles[j]
        load_q[j].wait()
        x = qin[t, :].T.astype(F32)
        resid[:, t] = x
        n, _ = normalized(x)
        first[:, t] = (n * col1).astype(BF16)

    load_c = local.start(cotangent, cin)
    load_wd = local.start(d_w, wd)
    load_wk = local.start(k_w, wk)
    load_wv = local.start(v_w, wv)
    load_wo = local.start(o_w, wo)
    load_wu = local.start(u_w, wu)
    first_part(0)
    load_own.wait()
    pl.semaphore_wait(barrier, 19)

    early = Rounds(p, a_send, a_recv)
    left, right = pl.ds(0, 640), pl.ds(640, 640)
    for k in range(1, 4):
        early.start(0, lat.at[z, y, :, left], lat.at[z, y, :, left], p.neighbour("y", k))
        early.start(0, lat.at[z, y, :, right], lat.at[z, y, :, right], p.neighbour("z", k))

    def latents_on():
        early.wait(0, lat.at[0, pl.ds(0, 3)])
        for k in range(1, 4):
            early.start(1, lat.at[z, :, :, left], lat.at[z, :, :, left], p.neighbour("z", k))
            early.start(1, lat.at[:, y, :, right], lat.at[:, y, :, right], p.neighbour("y", k))

    first_part(1)
    load_wq.wait()
    for j, t in enumerate(tiles):
        query[:, t] = (dot(wq[...], first[:, t], 0, 0) * SCALE).astype(BF16)
        if j == 0:
            latents_on()
    load_c.wait()
    load_wd.wait()
    for t in tiles:
        gout[:, t] = (stats[0:1, t] * cin[t, :].T.astype(F32)).astype(BF16)
        gup[:, t] = dot(wd[...], gout[:, t], 1, 0).astype(BF16)

    early.wait(1, lat.at[pl.ds(0, 3)])
    all_latents = lat[...].reshape(LAT, DL)
    load_wk.wait()
    keys[...] = dot(all_latents, wk[...], 1, 0).astype(BF16).T
    load_wv.wait()
    values[...] = dot(all_latents, wv[...], 1, 0).astype(BF16).T
    load_wo.wait()
    load_wu.wait()

    def mix(h):
        r = pl.ds(HEAD * h, HEAD)
        mixed[r, :] = dot(values[r, :], att[pl.ds(LAT * h, LAT), :], 1, 0).astype(BF16)

    for h in range(HEADS):
        r = pl.ds(HEAD * h, HEAD)
        for t in tiles:
            s = dot(keys[r, :], query[r, t], 0, 0)
            e = jnp.exp(s - jnp.max(s, axis=0, keepdims=True))
            att[pl.ds(LAT * h, LAT), t] = (e * (1.0 / jnp.sum(e, axis=0, keepdims=True))).astype(BF16)
        if h > 0:
            mix(h - 1)
    mix(HEADS - 1)
    attn_out = [dot(wo[...], mixed[:, t], 0, 0) for t in tiles]
    for j, t in enumerate(tiles):
        x = resid[:, t] + attn_out[j]
        resid[:, t] = x
        mu = jnp.mean(x, axis=0, keepdims=True)
        center = x - mu
        rstd = lax.rsqrt(jnp.mean(center * center, axis=0, keepdims=True) + EPS)
        stats[1:2, t] = mu
        stats[2:3, t] = rstd
        second[:, t] = (center * rstd * col2).astype(BF16)
        up = dot(wu[...], second[:, t], 0, 0)
        cdf = 0.5 * (1.0 + lax.erf(up * (0.5**0.5)))
        act[:, t] = (up * cdf).astype(BF16)
        slope = cdf + up * (jnp.exp(-0.5 * up * up) * 0.3989422804014327)
        gup[:, t] = (slope * gup[:, t].astype(F32)).astype(BF16)

    part_o = wk.at[:, pl.ds(0, D)]
    du = SumSession(
        p,
        Rounds(p, du_send, du_recv),
        local,
        "rows",
        ORDERS["du"],
        1536,
        part_du,
        rcore_du,
        relay_du,
        ra_du,
        rb_du,
        rc_du,
        fin_du,
        g_du,
    )
    so = SumSession(
        p,
        Rounds(p, o_send, o_recv),
        local,
        "cols",
        ORDERS["o"],
        D,
        part_o,
        rcore_o,
        relay_o,
        ra_o,
        rb_o,
        rc_o,
        fin_o,
        g_o,
    )
    sq = SumSession(
        p,
        Rounds(p, q_send, q_recv),
        local,
        "rows",
        ORDERS["q"],
        DL,
        part_q,
        rcore_q,
        relay_q,
        ra_q,
        rb_q,
        rc_q,
        fin_q,
        g_q,
    )
    sk = LatentSession(
        p,
        Rounds(p, k_send, k_recv),
        local,
        "y",
        "z",
        part_k,
        slots_k,
        sums_k,
        slots2_k,
        turned,
        0,
        lat,
        buffers_k,
        g_k,
    )
    sv = LatentSession(
        p,
        Rounds(p, v_send, v_recv),
        local,
        "z",
        "y",
        part_v,
        slots_v,
        sums_v,
        slots2_v,
        turned,
        128,
        lat,
        buffers_v,
        g_v,
    )
    gal = second
    gm = wv.at[:, pl.ds(0, ROWS)]
    stores = []

    def heads_of(axis, j):
        for i in range(2):
            h = 2 * p.shifted(axis, j) + i
            yield pl.ds(pl.multiple_of(h * HEAD, 32), HEAD), pl.ds(pl.multiple_of(h * LAT, 256), LAT)

    def mlp_back(j):
        t = tiles[j]
        gg = dot(wu[...], gup[:, t], 1, 0) * col2
        rstd = stats[2:3, t]
        n = (resid[:, t] - stats[1:2, t]) * rstd
        mean_gg = jnp.mean(gg, axis=0, keepdims=True)
        mean_ggn = jnp.mean(gg * n, axis=0, keepdims=True)
        gal[:, t] = (gout[:, t].astype(F32) + rstd * (gg - mean_gg - n * mean_ggn)).astype(BF16)

    def mixed_back(j):
        gm[:, tiles[j]] = dot(wo[...], gal[:, tiles[j]], 1, 0).astype(BF16)

    def value_heads(j):
        step = (j + 1) % 4
        for r, l in heads_of("z", step):
            part_v[r, :] = dot(gm[r, :], att[l, :], 1, 1).astype(BF16)
        sv.send(step)

    def key_heads(j):
        step = (j + 1) % 4
        for r, l in heads_of("y", step):
            for t in tiles:
                ga = dot(values[r, :], gm[r, t], 0, 0)
                a = att[l, t].astype(F32)
                att[l, t] = (a * (ga - jnp.sum(ga * a, axis=0, keepdims=True))).astype(BF16)
            part_k[r, :] = dot(query[r, :], att[l, :], 1, 1).astype(BF16)
        sk.send(step)

    def query_back(j):
        for h in range(4 * j, 4 * j + 4):
            r = pl.ds(h * HEAD, HEAD)
            gm[r, :] = dot(keys[r, :], att[pl.ds(h * LAT, LAT), :], 1, 0).astype(BF16)

    def query_weight(j):
        c = pl.ds(640 * j, 640)
        part_q[:, c] = (dot(first[...], gm[c, :], 1, 1) * SCALE).astype(BF16)

    def out_weight(j):
        c = pl.ds(640 * j, 640)
        wk[c, 0:D] = dot(mixed[c, :], gal[...], 1, 1).astype(BF16)

    def query_out(j):
        t = tiles[j]
        gg = dot(wq[...], gm[:, t], 1, 0) * (col1 * SCALE)
        n, rstd = normalized(qin[t, :].T.astype(F32))
        mean_gg = jnp.mean(gg, axis=0, keepdims=True)
        mean_ggn = jnp.mean(gg * n, axis=0, keepdims=True)
        total = gal[:, t].astype(F32) + rstd * (gg - mean_gg - n * mean_ggn)
        qin[t, :] = total.astype(BF16).T
        stores.append(local.start(qin.at[t], query_grad.at[t]))

    def block(j):
        t = tiles[j]
        out = stats[0:1, t] * (resid[:, t] + dot(wd[...], act[:, t], 0, 0))
        cin[t, :] = out.astype(BF16).T
        stores.append(local.start(cin.at[t], block_out.at[t]))

    def turn_send(j):
        turned_low[...] = turned[...].astype(BF16)
        for k in range(1, 16):
            who = lax.rem(seq + k, 16)
            mine = turned_low.at[pl.ds(pl.multiple_of(who * 16, 16), 16)]
            early.start(2, mine, rturned.at[seq], p.in_seq(who))
        rturned[pl.ds(seq, 1)] = turned_low[pl.ds(pl.multiple_of(seq * 16, 16), 16), :][None]

    reload = []

    def load_again(j):
        so.r.drain((0, 1, 2, 3))
        reload.append(local.start(k_w, wk))
        reload.append(local.start(v_w, wv))

    def latent_back(j):
        early.wait(2, rturned.at[pl.ds(0, 15)])
        for i in range(16):
            piece = rturned[i].astype(F32).T
            gathered_k[pl.ds(80 * (4 * (i % 4) + i // 4), 80), :] = piece[0:80, :]
            gathered_v[pl.ds(80 * i, 80), :] = piece[128:208, :]
        for load in reload:
            load.wait()
        latent_sum[...] = dot(gathered_k[...].T.astype(BF16), wk[...], 1, 1) + dot(
            gathered_v[...].T.astype(BF16), wv[...], 1, 1
        )
        stores.append(local.start(latent_sum, latent_grad))

    def down_up(j):
        part_du[:, 0:D] = dot(act[...], gout[...], 1, 1).astype(BF16)
        part_du[:, D:] = dot(second[...], gup[...], 1, 1).astype(BF16)

    parts = {
        "w": down_up,
        "b": mlp_back,
        "m": mixed_back,
        "V": value_heads,
        "K": key_heads,
        "g": query_back,
        "Q": query_weight,
        "O": out_weight,
        "x": query_out,
        "B": block,
        "T": turn_send,
        "R": load_again,
        "L": latent_back,
    }
    sessions = {"d": du, "o": so, "q": sq, "k": sk, "v": sv}
    for item in PLAN:
        if item in sessions:
            sessions[item].step()
        else:
            parts[item[0]](int(item[1]))
    for copy in stores:
        copy.wait()
    early.drain()
    for session in (du, so, sq, sk, sv):
        session.r.drain()
    assert [s.step_done for s in (du, so, sq, sk, sv)] == [10, 10, 10, 11, 11]


def convert_kernel(
    gain1,
    gain2,
    du,
    o,
    q,
    k,
    v,
    u_w,
    q_w,
    block,
    query,
    latent,
    out_q,
    out_k,
    out_v,
    out_o,
    out_u,
    out_d,
    out_block,
    out_query,
    out_latent,
    out_g1,
    out_g2,
):
    high = out_q.shape[0]
    at = pl.ds(pl.multiple_of(pl.program_id(0) * high, 128), high)

    def per_row(product, gain):
        total = jnp.sum(product, axis=1, keepdims=True)
        return (jnp.broadcast_to(total, (high, 128)).T[0:1, :] / gain.reshape(1, high)).reshape(high)

    out_d[...] = du[:, 0:D].astype(F32)
    up = du[:, D:].astype(F32)
    out_u[...] = up
    out_g2[at] = per_row(up * u_w[...].astype(F32), gain2[at])
    value = q[...].astype(F32)
    out_q[...] = value
    out_g1[at] = per_row(value * q_w[...].astype(F32), gain1[at])
    out_o[...] = o[...].astype(F32)
    out_k[...] = k[...].T.astype(F32)
    out_v[...] = v[...].T.astype(F32)
    out_block[...] = block[...]
    out_query[...] = query[...].astype(F32)
    out_latent[...] = latent[...]


def vm(shape, dtype=BF16):
    return pltpu.VMEM(shape, dtype)


def on_device(queries, latents, lengths, q_w, k_w, v_w, o_w, u_w, d_w, gain1, gain2, cotangent):
    any_spec = pl.BlockSpec(memory_space=pl.ANY)
    vmem_spec = pl.BlockSpec(memory_space=pltpu.VMEM)
    dma = pltpu.SemaphoreType.DMA
    sds = jax.ShapeDtypeStruct
    outs = pl.pallas_call(
        main_kernel,
        out_shape=(
            sds((ROWS, D), BF16),
            sds((ROWS, D), BF16),
            sds((16, DL), F32),
            sds((D, 1536), BF16),
            sds((DL, D), BF16),
            sds((D, DL), BF16),
            sds((4, 4, 80, DL), BF16),
            sds((4, 4, 80, DL), BF16),
        ),
        in_specs=[pl.BlockSpec(memory_space=pltpu.SMEM)] + [any_spec] * 11,
        out_specs=(any_spec,) * 8,
        scratch_shapes=[
            vm((ROWS, D)),
            vm((ROWS, D)),
            vm((4, 4, 16, DL)),
            vm((D, DL)),
            vm((DL, DL)),
            vm((DL, DL)),
            vm((DL, D)),
            vm((D, D)),
            vm((D, D)),
            vm((D, ROWS)),
            vm((DL, ROWS)),
            vm((DL, LAT)),
            vm((DL, LAT)),
            vm((HEADS * LAT, ROWS)),
            vm((DL, ROWS)),
            vm((D, ROWS), F32),
            vm((D, ROWS)),
            vm((D, ROWS)),
            vm((D, ROWS)),
            vm((D, ROWS)),
            vm((8, ROWS), F32),
            vm((2, D, 128), F32),
            vm((D, 1536)),
            vm((D, DL)),
            vm((DL, LAT)),
            vm((DL, LAT)),
            vm((3, 128, 1536)),
            vm((3, 640, 256)),
            vm((3, 128, DL)),
            vm((3, 2, 16, 1536)),
            vm((3, 2, 80, 256)),
            vm((3, 2, 16, DL)),
            vm((3, 4, 16, 1536)),
            vm((3, 4, 80, 256)),
            vm((3, 4, 16, DL)),
            vm((3, 3, 16, 768)),
            vm((3, 3, 80, 128)),
            vm((3, 3, 16, 640)),
            vm((3, 4, 16, 768)),
            vm((3, 4, 80, 128)),
            vm((3, 4, 16, 640)),
            vm((3, 16, 768)),
            vm((3, 80, 128)),
            vm((3, 16, 640)),
            vm((3, 320, LAT)),
            vm((3, 320, LAT)),
            vm((4, 80, LAT)),
            vm((4, 80, LAT)),
            vm((3, 80, LAT)),
            vm((3, 80, LAT)),
        ]
        + [
            vm((2, 80, 640)),
            vm((80, 640)),
            vm((3, 16, 256)),
            vm((4, 64, 256)),
            vm((4, 64, 128)),
            vm((4, 16, 640)),
            vm((16, 256)),
            vm((64, 256)),
            vm((64, 128)),
            vm((16, 640)),
        ]
        * 2
        + [
            vm((LAT, 256), F32),
            vm((LAT, 256)),
            vm((16, 16, 256)),
            vm((DL, 16), F32),
            vm((DL, 16), F32),
            vm((16, DL), F32),
            vm((D,), F32),
            vm((D,), F32),
        ]
        + [dma((SUM_ROUNDS,))] * 6
        + [dma((LATENT_ROUNDS,))] * 4
        + [dma((3,)), dma((3,)), dma((N_LOCAL,))],
        compiler_params=pltpu.CompilerParams(
            collective_id=0, has_side_effects=True, vmem_limit_bytes=VMEM_LIMIT
        ),
        name="decoder_block",
    )(lengths, gain1, gain2, queries[0], cotangent[0], latents[0], q_w, k_w, v_w, o_w, u_w, d_w)
    block_out, query_grad, latent_grad, g_du, g_o, g_q, g_k, g_v = outs

    def by_rows(rows, columns):
        return pl.BlockSpec((rows // 2, columns), lambda i: (i, 0))

    by_columns = pl.BlockSpec((DL, DL // 2), lambda i: (0, i))
    whole = pl.BlockSpec((D,), lambda i: (0,))
    latent_spec = pl.BlockSpec((16, DL), lambda i: (0, 0))
    conv = pl.pallas_call(
        convert_kernel,
        out_shape=(
            sds((D, DL), F32),
            sds((DL, DL), F32),
            sds((DL, DL), F32),
            sds((DL, D), F32),
            sds((D, D), F32),
            sds((D, D), F32),
            sds((ROWS, D), BF16),
            sds((ROWS, D), F32),
            sds((16, DL), F32),
            sds((D,), F32),
            sds((D,), F32),
        ),
        grid=(2,),
        in_specs=[whole, whole]
        + [by_rows(*shape) for shape in ((D, 1536), (DL, D), (D, DL))]
        + [by_columns, by_columns]
        + [by_rows(*shape) for shape in ((D, D), (D, DL), (ROWS, D), (ROWS, D))]
        + [latent_spec],
        out_specs=tuple(
            by_rows(*shape)
            for shape in ((D, DL), (DL, DL), (DL, DL), (DL, D), (D, D), (D, D), (ROWS, D), (ROWS, D))
        )
        + (latent_spec, whole, whole),
        compiler_params=pltpu.CompilerParams(vmem_limit_bytes=VMEM_LIMIT),
        name="to_float32",
    )(
        gain1,
        gain2,
        g_du,
        g_o,
        g_q,
        g_k.reshape(DL, DL),
        g_v.reshape(DL, DL),
        u_w,
        q_w,
        block_out,
        query_grad,
        latent_grad,
    )
    q_grad, k_grad, v_grad, o_grad, u_grad, d_grad, block_out, query_grad, latent_grad, g1_grad, g2_grad = conv
    return (
        block_out[None],
        query_grad[None],
        latent_grad[None],
        q_grad,
        k_grad,
        v_grad,
        o_grad,
        u_grad,
        d_grad,
        g1_grad,
        g2_grad,
    )


def solution(mesh):
    rows = P("dp", "seq", None)
    in_specs = (rows, rows, P("dp", None)) + (P(),) * 8 + (rows,)
    out_specs = (rows, rows, rows) + (P(),) * 8
    return jax.shard_map(on_device, mesh=mesh, in_specs=in_specs, out_specs=out_specs, check_vma=False)
```

```python
import functools

import jax
import jax.numpy as jnp
from jax import lax
from jax.experimental import pallas as pl
from jax.experimental.pallas import tpu as pltpu
from jax.sharding import PartitionSpec as P

MESH = pl.DeviceIdType.MESH
F32 = jnp.float32
BF16 = jnp.bfloat16
HEADS = 8
HEAD = 160
LAT = 256
ROWS = 1024
TILE = 512
D = 768
DL = 1280
SCALE = HEAD ** (-0.5)
EPS = 1e-5
VMEM_LIMIT = 63 * 2**20
ORDERS = {
    "du": ("xyz", "yzx", "zxy"),
    "o": ("xyz", "yzx", "zxy"),
    "q": ("xyz", "yzx", "zxy"),
}
PLAN = (
    "w0", "d", "b0", "b1", "m0", "m1", "V0", "V1", "V2", "d", "V3", "K0",
    "K1", "K2", "O0", "O1", "o", "v", "K3", "d", "g0", "g1", "Q0", "o",
    "v", "Q1", "d", "q", "v", "o", "k", "d", "q", "v", "k", "T0",
    "o", "x0", "q", "k", "v", "o", "q", "d", "x1", "k", "v", "o",
    "R0", "q", "d", "B0", "k", "B1", "q", "v", "v", "k", "o", "q",
    "d", "k", "L0", "o", "v", "k", "v", "q", "d", "k", "k", "o",
    "q", "d", "v", "k", "o", "q",
)


def dot(left, right, left_dim, right_dim):
    return lax.dot_general(
        left, right, (((left_dim,), (right_dim,)), ((), ())), preferred_element_type=F32
    )


class Place:
    def __init__(self):
        dp = lax.axis_index("dp")
        sq = lax.axis_index("seq")
        self.seq = sq
        self.dp = dp
        self.core = lax.rem(dp, 2)
        self.at = {"x": lax.div(dp, 2), "y": lax.rem(sq, 4), "z": lax.div(sq, 4)}

    def shifted(self, axis, step):
        return lax.rem(self.at[axis] + step, 4)

    def neighbour(self, axis, step):
        to = dict(self.at)
        to[axis] = self.shifted(axis, step)
        return (to["x"] * 2 + self.core, to["z"] * 4 + to["y"])

    def sibling(self):
        return (self.dp + 1 - 2 * self.core, self.seq)

    def in_seq(self, index):
        return (self.dp, index)


class Rounds:
    def __init__(self, place, send, recv):
        self.place, self.send, self.recv, self.size = place, send, recv, {}

    def copy(self, index, src, dst, device):
        return pltpu.make_async_remote_copy(
            src_ref=src,
            dst_ref=dst,
            send_sem=self.send.at[index],
            recv_sem=self.recv.at[index],
            device_id=device,
            device_id_type=MESH,
        )

    def start(self, index, src, dst, device):
        self.copy(index, src, dst, device).start()

    def wait(self, index, same_size):
        self.size[index] = same_size
        self.copy(index, same_size, same_size, self.place.sibling()).wait_recv()

    def drain(self, only=None):
        for index in list(self.size) if only is None else only:
            same_size = self.size.pop(index)
            self.copy(index, same_size, same_size, self.place.sibling()).wait_send()


class Locals:
    def __init__(self, sems):
        self.sems, self.used = sems, 0

    def start(self, src, dst):
        copy = pltpu.make_async_copy(src, dst, self.sems.at[self.used])
        self.used += 1
        copy.start()
        return copy


class SumSession:
    def __init__(self, place, rounds, local, kind, orders, width, part, rcore, relay, ra, rb, rc, fin, out):
        self.p, self.r, self.local = place, rounds, local
        self.kind, self.orders, self.width = kind, orders, width
        self.part, self.rcore, self.relay, self.ra, self.rb, self.rc = part, rcore, relay, ra, rb, rc
        self.fin, self.out = fin, out
        self.step_done = 0

    def region(self, i, c, a=None, b=None, half=None):
        if self.kind == "rows":
            row, high, col, wide = 256 * i + 128 * c, 128, 0, self.width
            if a is not None:
                row, high = row + 32 * a, 32
            if half is not None:
                row, high = row + 16 * half, 16
            if b is not None:
                row, high = row + 16 * lax.div(b, 2), 16
                wide = self.width // 2
                col = pl.multiple_of(lax.rem(b, 2) * wide, 128)
        else:
            row, high, col, wide = 640 * c, 640, 256 * i, 256
            if a is not None:
                row, high = row + 160 * a, 160
            if half is not None:
                row, high = row + 80 * half, 80
            if b is not None:
                row, high = row + 80 * lax.div(b, 2), 80
                wide = 128
                col = pl.multiple_of(256 * i + 128 * lax.rem(b, 2), 128)
        return pl.ds(pl.multiple_of(row, 16), high), pl.ds(col, wide)

    def here(self, i, *rest):
        return self.region(i, self.p.core, *rest)

    def axes(self, i):
        return self.orders[i]

    def s0(self):
        for i in range(3):
            self.r.start(0, self.part.at[self.region(i, 1 - self.p.core)], self.rcore.at[i], self.p.sibling())

    def s1(self):
        self.r.wait(0, self.rcore)
        for i in range(3):
            here = self.here(i)
            self.part[here] = self.part[here] + self.rcore[i]
        for i in range(3):
            axis = self.axes(i)[0]
            up, down = self.p.neighbour(axis, 1), self.p.neighbour(axis, 3)
            at = [self.p.shifted(axis, k) for k in range(4)]
            self.r.start(1, self.part.at[self.here(i, at[2], None, 0)], self.relay.at[i, 0], down)
            self.r.start(1, self.part.at[self.here(i, at[2], None, 1)], self.relay.at[i, 1], up)
            self.r.start(2, self.part.at[self.here(i, at[1], None, 0)], self.ra.at[i, 0], up)
            self.r.start(2, self.part.at[self.here(i, at[3], None, 1)], self.ra.at[i, 1], down)

    def s2(self):
        self.r.wait(1, self.relay)
        for i in range(3):
            axis = self.axes(i)[0]
            for half, k in ((0, 3), (1, 1)):
                there = self.here(i, self.p.shifted(axis, k), None, half)
                self.part[there] = self.part[there] + self.relay[i, half]
                self.r.start(2, self.part.at[there], self.ra.at[i, 2 + half], self.p.neighbour(axis, k))

    def s3(self):
        self.r.wait(2, self.ra)
        for i in range(3):
            a = self.p.at[self.axes(i)[0]]
            for half in range(2):
                here = self.here(i, a, None, half)
                total = self.part[here].astype(F32) + self.ra[i, half].astype(F32) + self.ra[i, 2 + half].astype(F32)
                self.part[here] = total.astype(BF16)
        for i in range(3):
            a_axis, b_axis, _ = self.axes(i)
            for k in range(3):
                to = self.p.shifted(b_axis, k + 1)
                self.r.start(
                    3,
                    self.part.at[self.here(i, self.p.at[a_axis], to)],
                    self.rb.at[i, k],
                    self.p.neighbour(b_axis, k + 1),
                )

    def s4(self):
        self.r.wait(3, self.rb)
        for i in range(3):
            a_axis, b_axis, c_axis = self.axes(i)
            total = self.part[self.here(i, self.p.at[a_axis], self.p.at[b_axis])].astype(F32)
            for k in range(3):
                total = total + self.rb[i, k].astype(F32)
            self.rc[i, pl.ds(self.p.at[c_axis], 1)] = total.astype(BF16)[None]
        for i in range(3):
            c_axis = self.axes(i)[2]
            slot = self.rc.at[i, self.p.at[c_axis]]
            for k in range(3):
                self.r.start(4, slot, slot, self.p.neighbour(c_axis, k + 1))

    def s5(self):
        self.r.wait(4, self.rb)
        self.own = []
        for i in range(3):
            total = self.rc[i, 0].astype(F32)
            for k in range(1, 4):
                total = total + self.rc[i, k].astype(F32)
            self.fin[i] = total.astype(BF16)
        for i in range(3):
            a_axis, b_axis, _ = self.axes(i)
            there = self.out.at[self.here(i, self.p.at[a_axis], self.p.at[b_axis])]
            self.own.append(self.local.start(self.fin.at[i], there))
            for k in range(3):
                self.r.start(5, self.fin.at[i], there, self.p.neighbour(b_axis, k + 1))

    def s6(self):
        self.r.wait(5, self.rb)
        for copy in self.own:
            copy.wait()
        for i in range(3):
            axis = self.axes(i)[0]
            there = self.out.at[self.here(i, self.p.at[axis])]
            for k in (1, 3):
                self.r.start(6, there, there, self.p.neighbour(axis, k))

    def s7(self):
        self.r.wait(6, self.ra)
        for i in range(3):
            axis = self.axes(i)[0]
            for half, k in ((0, 3), (1, 1)):
                there = self.out.at[self.here(i, self.p.shifted(axis, k), None, half)]
                self.r.start(7, there, there, self.p.neighbour(axis, 4 - k))
        self.to_sibling(8, (0, 1, 3))

    def to_sibling(self, index, steps):
        for i in range(3):
            for k in steps:
                there = self.out.at[self.here(i, self.p.shifted(self.axes(i)[0], k))]
                self.r.start(index, there, there, self.p.sibling())

    def s8(self):
        self.r.wait(7, self.relay)
        self.to_sibling(9, (2,))

    def s9(self):
        quarter = self.rcore.shape[1] // 4
        self.r.wait(8, self.rcore.at[:, pl.ds(0, 3 * quarter)])
        self.r.wait(9, self.rcore.at[:, pl.ds(0, quarter)])

    def step(self):
        getattr(self, "s%d" % self.step_done)()
        self.step_done += 1


class LatentSession:
    def __init__(self, place, rounds, local, first, other, part, slots, sums, slots2, turned, turned_at, lat, buffers, out):
        self.p, self.r, self.local, self.first, self.other = place, rounds, local, first, other
        self.part, self.slots, self.sums, self.slots2 = part, slots, sums, slots2
        self.turned, self.turned_at, self.lat, self.out = turned, turned_at, lat, out
        self.half, self.rhalf, self.ra, self.rb, self.rc, self.rd, self.fa, self.fb, self.fc, self.fd = buffers
        self.f, self.g = place.at[first], place.at[other]
        self.step_done = 0

    def rows(self, step):
        return pl.ds(pl.multiple_of(320 * self.p.shifted(self.first, step), 64), 320)

    def send(self, step):
        if step > 0:
            self.r.start(0, self.part.at[self.rows(step)], self.slots.at[step - 1], self.p.neighbour(self.first, step))

    def s0(self):
        self.r.wait(0, self.slots)
        total = self.part[self.rows(0)].astype(F32)
        for k in range(3):
            total = total + self.slots[k].astype(F32)
        for k in range(4):
            self.sums[k] = total[80 * k : 80 * k + 80].astype(BF16)
        for k in range(1, 4):
            to = self.p.shifted(self.other, k)
            self.r.start(1, self.sums.at[to], self.slots2.at[k - 1], self.p.neighbour(self.other, k))

    def s1(self):
        self.r.wait(1, self.slots2)
        total = self.sums[self.g].astype(F32)
        for k in range(3):
            total = total + self.slots2[k].astype(F32)
        product = dot(total.astype(BF16), self.lat[...].reshape(LAT, DL), 1, 0).astype(BF16)
        self.half[0] = product[:, :640]
        self.half[1] = product[:, 640:]
        self.r.start(2, self.half.at[1 - self.p.core], self.rhalf, self.p.sibling())
        self.turned[:, self.turned_at : self.turned_at + 80] = total.T

    def s2(self):
        self.r.wait(2, self.rhalf)
        x = self.p.at["x"]
        total = self.half[self.p.core] + self.rhalf[...]
        self.half[self.p.core] = total
        self.rb[pl.ds(x, 1)] = total[0:64, 256:512][None]
        self.rc[pl.ds(x, 1)] = total[0:64, 512:][None]
        self.rd[pl.ds(x, 1)] = total[64:80][None]
        for k in range(1, 4):
            rows = pl.ds(pl.multiple_of(16 * self.p.shifted("x", k), 16), 16)
            self.r.start(
                3, self.half.at[self.p.core, rows, pl.ds(0, 256)], self.ra.at[k - 1], self.p.neighbour("x", k)
            )
        for k in range(1, 4):
            for index, buf in ((4, self.rb), (5, self.rc), (6, self.rd)):
                self.r.start(index, buf.at[x], buf.at[x], self.p.neighbour("x", k))

    def columns(self, start, size):
        return pl.ds(pl.multiple_of(640 * self.p.core + start, 128), size)

    def a_part(self):
        return pl.ds(pl.multiple_of(16 * self.p.at["x"], 16), 16), self.columns(0, 256)

    def b_part(self):
        return pl.ds(0, 64), self.columns(256, 256)

    def c_part(self):
        return pl.ds(0, 64), self.columns(512, 128)

    def d_part(self):
        return pl.ds(64, 16), self.columns(0, 640)

    def same(self, index, *lead):
        rows, cols = ((16, 256), (64, 256), (64, 128), (16, 640))[index]
        return self.out.at[lead + (pl.ds(0, rows), pl.ds(0, cols))]

    def s3(self):
        three = pl.ds(0, 3)
        self.r.wait(3, self.ra)
        total = self.half[self.p.core, self.a_part()[0], 0:256].astype(F32)
        for k in range(3):
            total = total + self.ra[k].astype(F32)
        self.fa[...] = total.astype(BF16)
        for index, buf, fin in ((4, self.rb, self.fb), (5, self.rc, self.fc), (6, self.rd, self.fd)):
            self.r.wait(index, buf.at[three])
            total = buf[0].astype(F32)
            for k in range(1, 4):
                total = total + buf[k].astype(F32)
            fin[...] = total.astype(BF16)
        block = self.out.at[self.f, self.g]
        self.own = []
        for index, fin, part, axis in (
            (7, self.fa, self.a_part(), self.first),
            (9, self.fc, self.c_part(), self.other),
            (10, self.fd, self.d_part(), self.other),
            (8, self.fb, self.b_part(), self.first),
        ):
            there = block.at[part]
            self.own.append(self.local.start(fin, there))
            for k in range(1, 4):
                self.r.start(index, fin, there, self.p.neighbour(axis, k))

    def s4(self):
        three, every = pl.ds(0, 3), slice(None)
        for index in range(4):
            self.r.wait(7 + index, self.same(index, 0, three))
        for copy in self.own:
            copy.wait()
        there = self.out.at[(every, self.g) + self.a_part()]
        for k in range(1, 4):
            self.r.start(11, there, there, self.p.neighbour(self.other, k))
        for index, part in ((13, self.c_part()), (14, self.d_part())):
            there = self.out.at[(self.f, every) + part]
            for k in (1, 3):
                self.r.start(index, there, there, self.p.neighbour(self.first, k))
        there = self.out.at[(every, self.g) + self.b_part()]
        for k in (1, 3):
            self.r.start(12, there, there, self.p.neighbour(self.other, k))

    def s5(self):
        every = slice(None)
        self.r.wait(11, self.same(0, pl.ds(0, 3), every))
        there = self.out.at[(every, every) + self.a_part()]
        for k in (1, 3):
            self.r.start(15, there, there, self.p.neighbour("x", k))

    def x_rows(self, k):
        return pl.ds(pl.multiple_of(16 * self.p.shifted("x", k), 16), 16)

    def to_sibling(self, index, steps):
        every = slice(None)
        for k in steps:
            f, g = self.p.shifted(self.first, k), self.p.shifted(self.other, k)
            for i, where in ((0, (every, g) + self.b_part()), (1, (f, every) + self.c_part()), (2, (f, every) + self.d_part())):
                there = self.out.at[where]
                self.r.start(index + i, there, there, self.p.sibling())

    def a_to_sibling(self, index, steps):
        for k in steps:
            there = self.out.at[:, :, self.x_rows(k), self.columns(0, 256)]
            self.r.start(index, there, there, self.p.sibling())

    def s6(self):
        two, every = pl.ds(0, 2), slice(None)
        self.r.wait(13, self.same(2, two, every))
        self.r.wait(14, self.same(3, two, every))
        for index, part in ((21, self.c_part()), (22, self.d_part())):
            for low, k in ((0, 3), (2, 1)):
                there = self.out.at[(self.p.shifted(self.first, k), pl.ds(low, 2)) + part]
                self.r.start(index, there, there, self.p.neighbour(self.first, 4 - k))
        self.r.wait(12, self.same(1, two, every))
        for low, k in ((0, 3), (2, 1)):
            there = self.out.at[(pl.ds(low, 2), self.p.shifted(self.other, k)) + self.b_part()]
            self.r.start(20, there, there, self.p.neighbour(self.other, 4 - k))
        self.to_sibling(16, (0, 1, 3))

    def s7(self):
        self.r.wait(15, self.out.at[:, :, pl.ds(0, 32), pl.ds(0, 256)])
        for low, k in ((0, 3), (2, 1)):
            there = self.out.at[pl.ds(low, 2), :, self.x_rows(k), self.columns(0, 256)]
            self.r.start(23, there, there, self.p.neighbour("x", 4 - k))
        self.a_to_sibling(19, (0, 1, 3))

    def s8(self):
        for index in (1, 2, 3):
            self.r.wait(19 + index, self.same(index, 0, slice(None)))
        self.to_sibling(24, (2,))

    def s9(self):
        self.r.wait(23, self.same(0, slice(None), slice(None)))
        self.a_to_sibling(27, (2,))

    def s10(self):
        three, every = pl.ds(0, 3), slice(None)
        for index in (1, 2, 3):
            self.r.wait(15 + index, self.same(index, three, every))
            self.r.wait(23 + index, self.same(index, 0, every))
        self.r.wait(19, self.out.at[:, :, pl.ds(0, 48), pl.ds(0, 256)])
        self.r.wait(27, self.same(0, every, every))

    def step(self):
        getattr(self, "s%d" % self.step_done)()
        self.step_done += 1


SUM_ROUNDS = 10
LATENT_ROUNDS = 28
N_LOCAL = 36


def main_kernel(
    lengths,
    gain1_in,
    gain2_in,
    queries,
    cotangent,
    latents,
    q_w,
    k_w,
    v_w,
    o_w,
    u_w,
    d_w,
    block_out,
    query_grad,
    latent_grad,
    g_du,
    g_o,
    g_q,
    g_k,
    g_v,
    qin,
    cin,
    lat,
    wq,
    wk,
    wv,
    wo,
    wu,
    wd,
    first,
    query,
    keys,
    values,
    att,
    mixed,
    resid,
    second,
    act,
    gup,
    gout,
    stats,
    gcol,
    part_du,
    part_q,
    part_k,
    part_v,
    rcore_du,
    rcore_o,
    rcore_q,
    relay_du,
    relay_o,
    relay_q,
    ra_du,
    ra_o,
    ra_q,
    rb_du,
    rb_o,
    rb_q,
    rc_du,
    rc_o,
    rc_q,
    fin_du,
    fin_o,
    fin_q,
    slots_k,
    slots_v,
    sums_k,
    sums_v,
    slots2_k,
    slots2_v,
    *rest,
):
    buffers_k, buffers_v = rest[0:10], rest[10:20]
    (
        turned,
        turned_low,
        rturned,
        gathered_k,
        gathered_v,
        latent_sum,
        gain1,
        gain2,
        du_send,
        du_recv,
        o_send,
        o_recv,
        q_send,
        q_recv,
        k_send,
        k_recv,
        v_send,
        v_recv,
        a_send,
        a_recv,
        local_sem,
    ) = rest[20:]
    p = Place()
    local = Locals(local_sem)
    load_q = [local.start(queries.at[pl.ds(TILE * j, TILE)], qin.at[pl.ds(TILE * j, TILE)]) for j in range(2)]
    z, y = p.at["z"], p.at["y"]
    load_own = local.start(latents, lat.at[z, y])
    load_g = [local.start(gain1_in, gain1), local.start(gain2_in, gain2)]
    load_wq = local.start(q_w, wq)

    barrier = pltpu.get_barrier_semaphore()
    for k in range(1, 16):
        pl.semaphore_signal(barrier, inc=1, device_id=p.in_seq(lax.rem(p.seq + k, 16)), device_id_type=MESH)
    for k in range(1, 4):
        pl.semaphore_signal(barrier, inc=1, device_id=p.neighbour("x", k), device_id_type=MESH)
    pl.semaphore_signal(barrier, inc=1, device_id=p.sibling(), device_id_type=MESH)

    seq = p.seq
    is_long = (seq < 8).astype(jnp.int32)
    lane = lax.broadcasted_iota(jnp.int32, (1, 128), 1)
    for j in range(8):
        item = is_long * lax.div(seq, 2) + (1 - is_long) * (4 + (seq - 8) * 8 + j)
        offset = is_long * (lax.rem(seq, 2) * 1024 + 128 * j)
        stats[0:1, 128 * j : 128 * j + 128] = jnp.where(lane + offset < lengths[0, item], 1.0, 0.0).astype(F32)

    for load in load_g:
        load.wait()
    gcol[0] = jnp.broadcast_to(gain1[...].reshape(1, D), (128, D)).T
    gcol[1] = jnp.broadcast_to(gain2[...].reshape(1, D), (128, D)).T
    col1 = gcol[0][:, 0:1]
    col2 = gcol[1][:, 0:1]
    turned[...] = jnp.zeros_like(turned)

    def normalized(x):
        center = x - jnp.mean(x, axis=0, keepdims=True)
        rstd = lax.rsqrt(jnp.mean(center * center, axis=0, keepdims=True) + EPS)
        return center * rstd, rstd

    tiles = [pl.ds(TILE * j, TILE) for j in range(2)]

    def first_part(j):
        t = tiles[j]
        load_q[j].wait()
        x = qin[t, :].T.astype(F32)
        resid[:, t] = x
        n, _ = normalized(x)
        first[:, t] = (n * col1).astype(BF16)

    load_c = local.start(cotangent, cin)
    load_wd = local.start(d_w, wd)
    load_wk = local.start(k_w, wk)
    load_wv = local.start(v_w, wv)
    load_wo = local.start(o_w, wo)
    load_wu = local.start(u_w, wu)
    first_part(0)
    load_own.wait()
    pl.semaphore_wait(barrier, 19)

    early = Rounds(p, a_send, a_recv)
    left, right = pl.ds(0, 640), pl.ds(640, 640)
    for k in range(1, 4):
        early.start(0, lat.at[z, y, :, left], lat.at[z, y, :, left], p.neighbour("y", k))
        early.start(0, lat.at[z, y, :, right], lat.at[z, y, :, right], p.neighbour("z", k))

    def latents_on():
        early.wait(0, lat.at[0, pl.ds(0, 3)])
        for k in range(1, 4):
            early.start(1, lat.at[z, :, :, left], lat.at[z, :, :, left], p.neighbour("z", k))
            early.start(1, lat.at[:, y, :, right], lat.at[:, y, :, right], p.neighbour("y", k))

    first_part(1)
    load_wq.wait()
    for j, t in enumerate(tiles):
        query[:, t] = (dot(wq[...], first[:, t], 0, 0) * SCALE).astype(BF16)
        if j == 0:
            latents_on()
    load_c.wait()
    load_wd.wait()
    for t in tiles:
        gout[:, t] = (stats[0:1, t] * cin[t, :].T.astype(F32)).astype(BF16)
        gup[:, t] = dot(wd[...], gout[:, t], 1, 0).astype(BF16)

    early.wait(1, lat.at[pl.ds(0, 3)])
    all_latents = lat[...].reshape(LAT, DL)
    load_wk.wait()
    keys[...] = dot(all_latents, wk[...], 1, 0).astype(BF16).T
    load_wv.wait()
    values[...] = dot(all_latents, wv[...], 1, 0).astype(BF16).T
    load_wo.wait()
    load_wu.wait()

    def mix(h):
        r = pl.ds(HEAD * h, HEAD)
        mixed[r, :] = dot(values[r, :], att[pl.ds(LAT * h, LAT), :], 1, 0).astype(BF16)

    for h in range(HEADS):
        r = pl.ds(HEAD * h, HEAD)
        for t in tiles:
            s = dot(keys[r, :], query[r, t], 0, 0)
            e = jnp.exp(s - jnp.max(s, axis=0, keepdims=True))
            att[pl.ds(LAT * h, LAT), t] = (e * (1.0 / jnp.sum(e, axis=0, keepdims=True))).astype(BF16)
        if h > 0:
            mix(h - 1)
    mix(HEADS - 1)
    attn_out = [dot(wo[...], mixed[:, t], 0, 0) for t in tiles]
    for j, t in enumerate(tiles):
        x = resid[:, t] + attn_out[j]
        resid[:, t] = x
        mu = jnp.mean(x, axis=0, keepdims=True)
        center = x - mu
        rstd = lax.rsqrt(jnp.mean(center * center, axis=0, keepdims=True) + EPS)
        stats[1:2, t] = mu
        stats[2:3, t] = rstd
        second[:, t] = (center * rstd * col2).astype(BF16)
        up = dot(wu[...], second[:, t], 0, 0)
        cdf = 0.5 * (1.0 + lax.erf(up * (0.5**0.5)))
        act[:, t] = (up * cdf).astype(BF16)
        slope = cdf + up * (jnp.exp(-0.5 * up * up) * 0.3989422804014327)
        gup[:, t] = (slope * gup[:, t].astype(F32)).astype(BF16)

    part_o = wk.at[:, pl.ds(0, D)]
    du = SumSession(
        p,
        Rounds(p, du_send, du_recv),
        local,
        "rows",
        ORDERS["du"],
        1536,
        part_du,
        rcore_du,
        relay_du,
        ra_du,
        rb_du,
        rc_du,
        fin_du,
        g_du,
    )
    so = SumSession(
        p,
        Rounds(p, o_send, o_recv),
        local,
        "cols",
        ORDERS["o"],
        D,
        part_o,
        rcore_o,
        relay_o,
        ra_o,
        rb_o,
        rc_o,
        fin_o,
        g_o,
    )
    sq = SumSession(
        p,
        Rounds(p, q_send, q_recv),
        local,
        "rows",
        ORDERS["q"],
        DL,
        part_q,
        rcore_q,
        relay_q,
        ra_q,
        rb_q,
        rc_q,
        fin_q,
        g_q,
    )
    sk = LatentSession(
        p,
        Rounds(p, k_send, k_recv),
        local,
        "y",
        "z",
        part_k,
        slots_k,
        sums_k,
        slots2_k,
        turned,
        0,
        lat,
        buffers_k,
        g_k,
    )
    sv = LatentSession(
        p,
        Rounds(p, v_send, v_recv),
        local,
        "z",
        "y",
        part_v,
        slots_v,
        sums_v,
        slots2_v,
        turned,
        128,
        lat,
        buffers_v,
        g_v,
    )
    gal = second
    gm = wv.at[:, pl.ds(0, ROWS)]
    stores = []

    def heads_of(axis, j):
        for i in range(2):
            h = 2 * p.shifted(axis, j) + i
            yield pl.ds(pl.multiple_of(h * HEAD, 32), HEAD), pl.ds(pl.multiple_of(h * LAT, 256), LAT)

    def mlp_back(j):
        t = tiles[j]
        gg = dot(wu[...], gup[:, t], 1, 0) * col2
        rstd = stats[2:3, t]
        n = (resid[:, t] - stats[1:2, t]) * rstd
        mean_gg = jnp.mean(gg, axis=0, keepdims=True)
        mean_ggn = jnp.mean(gg * n, axis=0, keepdims=True)
        gal[:, t] = (gout[:, t].astype(F32) + rstd * (gg - mean_gg - n * mean_ggn)).astype(BF16)

    def mixed_back(j):
        gm[:, tiles[j]] = dot(wo[...], gal[:, tiles[j]], 1, 0).astype(BF16)

    def value_heads(j):
        step = (j + 1) % 4
        for r, l in heads_of("z", step):
            part_v[r, :] = dot(gm[r, :], att[l, :], 1, 1).astype(BF16)
        sv.send(step)

    def key_heads(j):
        step = (j + 1) % 4
        for r, l in heads_of("y", step):
            for t in tiles:
                ga = dot(values[r, :], gm[r, t], 0, 0)
                a = att[l, t].astype(F32)
                att[l, t] = (a * (ga - jnp.sum(ga * a, axis=0, keepdims=True))).astype(BF16)
            part_k[r, :] = dot(query[r, :], att[l, :], 1, 1).astype(BF16)
        sk.send(step)

    def query_back(j):
        for h in range(4 * j, 4 * j + 4):
            r = pl.ds(h * HEAD, HEAD)
            gm[r, :] = dot(keys[r, :], att[pl.ds(h * LAT, LAT), :], 1, 0).astype(BF16)

    def query_weight(j):
        c = pl.ds(640 * j, 640)
        part_q[:, c] = (dot(first[...], gm[c, :], 1, 1) * SCALE).astype(BF16)

    def out_weight(j):
        c = pl.ds(640 * j, 640)
        wk[c, 0:D] = dot(mixed[c, :], gal[...], 1, 1).astype(BF16)

    def query_out(j):
        t = tiles[j]
        gg = dot(wq[...], gm[:, t], 1, 0) * (col1 * SCALE)
        n, rstd = normalized(qin[t, :].T.astype(F32))
        mean_gg = jnp.mean(gg, axis=0, keepdims=True)
        mean_ggn = jnp.mean(gg * n, axis=0, keepdims=True)
        total = gal[:, t].astype(F32) + rstd * (gg - mean_gg - n * mean_ggn)
        qin[t, :] = total.astype(BF16).T
        stores.append(local.start(qin.at[t], query_grad.at[t]))

    def block(j):
        t = tiles[j]
        out = stats[0:1, t] * (resid[:, t] + dot(wd[...], act[:, t], 0, 0))
        cin[t, :] = out.astype(BF16).T
        stores.append(local.start(cin.at[t], block_out.at[t]))

    def turn_send(j):
        turned_low[...] = turned[...].astype(BF16)
        for k in range(1, 16):
            who = lax.rem(seq + k, 16)
            mine = turned_low.at[pl.ds(pl.multiple_of(who * 16, 16), 16)]
            early.start(2, mine, rturned.at[seq], p.in_seq(who))
        rturned[pl.ds(seq, 1)] = turned_low[pl.ds(pl.multiple_of(seq * 16, 16), 16), :][None]

    reload = []

    def load_again(j):
        so.r.drain((0, 1, 2, 3))
        reload.append(local.start(k_w, wk))
        reload.append(local.start(v_w, wv))

    def latent_back(j):
        early.wait(2, rturned.at[pl.ds(0, 15)])
        for i in range(16):
            piece = rturned[i].astype(F32).T
            gathered_k[pl.ds(80 * (4 * (i % 4) + i // 4), 80), :] = piece[0:80, :]
            gathered_v[pl.ds(80 * i, 80), :] = piece[128:208, :]
        for load in reload:
            load.wait()
        latent_sum[...] = dot(gathered_k[...].T.astype(BF16), wk[...], 1, 1) + dot(
            gathered_v[...].T.astype(BF16), wv[...], 1, 1
        )
        stores.append(local.start(latent_sum, latent_grad))

    def down_up(j):
        part_du[:, 0:D] = dot(act[...], gout[...], 1, 1).astype(BF16)
        part_du[:, D:] = dot(second[...], gup[...], 1, 1).astype(BF16)

    parts = {
        "w": down_up,
        "b": mlp_back,
        "m": mixed_back,
        "V": value_heads,
        "K": key_heads,
        "g": query_back,
        "Q": query_weight,
        "O": out_weight,
        "x": query_out,
        "B": block,
        "T": turn_send,
        "R": load_again,
        "L": latent_back,
    }
    sessions = {"d": du, "o": so, "q": sq, "k": sk, "v": sv}
    for item in PLAN:
        if item in sessions:
            sessions[item].step()
        else:
            parts[item[0]](int(item[1]))
    for copy in stores:
        copy.wait()
    early.drain()
    for session in (du, so, sq, sk, sv):
        session.r.drain()
    assert [s.step_done for s in (du, so, sq, sk, sv)] == [10, 10, 10, 11, 11]


def convert_kernel(
    gain1,
    gain2,
    du,
    o,
    q,
    k,
    v,
    u_w,
    q_w,
    block,
    query,
    latent,
    out_q,
    out_k,
    out_v,
    out_o,
    out_u,
    out_d,
    out_block,
    out_query,
    out_latent,
    out_g1,
    out_g2,
):
    high = out_q.shape[0]
    at = pl.ds(pl.multiple_of(pl.program_id(0) * high, 128), high)

    def per_row(product, gain):
        total = jnp.sum(product, axis=1, keepdims=True)
        return (jnp.broadcast_to(total, (high, 128)).T[0:1, :] / gain.reshape(1, high)).reshape(high)

    out_d[...] = du[:, 0:D].astype(F32)
    up = du[:, D:].astype(F32)
    out_u[...] = up
    out_g2[at] = per_row(up * u_w[...].astype(F32), gain2[at])
    value = q[...].astype(F32)
    out_q[...] = value
    out_g1[at] = per_row(value * q_w[...].astype(F32), gain1[at])
    out_o[...] = o[...].astype(F32)
    out_k[...] = k[...].T.astype(F32)
    out_v[...] = v[...].T.astype(F32)
    out_block[...] = block[...]
    out_query[...] = query[...].astype(F32)
    out_latent[...] = latent[...]


def vm(shape, dtype=BF16):
    return pltpu.VMEM(shape, dtype)


def on_device(queries, latents, lengths, q_w, k_w, v_w, o_w, u_w, d_w, gain1, gain2, cotangent):
    any_spec = pl.BlockSpec(memory_space=pl.ANY)
    vmem_spec = pl.BlockSpec(memory_space=pltpu.VMEM)
    dma = pltpu.SemaphoreType.DMA
    sds = jax.ShapeDtypeStruct
    outs = pl.pallas_call(
        main_kernel,
        out_shape=(
            sds((ROWS, D), BF16),
            sds((ROWS, D), BF16),
            sds((16, DL), F32),
            sds((D, 1536), BF16),
            sds((DL, D), BF16),
            sds((D, DL), BF16),
            sds((4, 4, 80, DL), BF16),
            sds((4, 4, 80, DL), BF16),
        ),
        in_specs=[pl.BlockSpec(memory_space=pltpu.SMEM)] + [any_spec] * 11,
        out_specs=(any_spec,) * 8,
        scratch_shapes=[
            vm((ROWS, D)),
            vm((ROWS, D)),
            vm((4, 4, 16, DL)),
            vm((D, DL)),
            vm((DL, DL)),
            vm((DL, DL)),
            vm((DL, D)),
            vm((D, D)),
            vm((D, D)),
            vm((D, ROWS)),
            vm((DL, ROWS)),
            vm((DL, LAT)),
            vm((DL, LAT)),
            vm((HEADS * LAT, ROWS)),
            vm((DL, ROWS)),
            vm((D, ROWS), F32),
            vm((D, ROWS)),
            vm((D, ROWS)),
            vm((D, ROWS)),
            vm((D, ROWS)),
            vm((8, ROWS), F32),
            vm((2, D, 128), F32),
            vm((D, 1536)),
            vm((D, DL)),
            vm((DL, LAT)),
            vm((DL, LAT)),
            vm((3, 128, 1536)),
            vm((3, 640, 256)),
            vm((3, 128, DL)),
            vm((3, 2, 16, 1536)),
            vm((3, 2, 80, 256)),
            vm((3, 2, 16, DL)),
            vm((3, 4, 16, 1536)),
            vm((3, 4, 80, 256)),
            vm((3, 4, 16, DL)),
            vm((3, 3, 16, 768)),
            vm((3, 3, 80, 128)),
            vm((3, 3, 16, 640)),
            vm((3, 4, 16, 768)),
            vm((3, 4, 80, 128)),
            vm((3, 4, 16, 640)),
            vm((3, 16, 768)),
            vm((3, 80, 128)),
            vm((3, 16, 640)),
            vm((3, 320, LAT)),
            vm((3, 320, LAT)),
            vm((4, 80, LAT)),
            vm((4, 80, LAT)),
            vm((3, 80, LAT)),
            vm((3, 80, LAT)),
        ]
        + [
            vm((2, 80, 640)),
            vm((80, 640)),
            vm((3, 16, 256)),
            vm((4, 64, 256)),
            vm((4, 64, 128)),
            vm((4, 16, 640)),
            vm((16, 256)),
            vm((64, 256)),
            vm((64, 128)),
            vm((16, 640)),
        ]
        * 2
        + [
            vm((LAT, 256), F32),
            vm((LAT, 256)),
            vm((16, 16, 256)),
            vm((DL, 16), F32),
            vm((DL, 16), F32),
            vm((16, DL), F32),
            vm((D,), F32),
            vm((D,), F32),
        ]
        + [dma((SUM_ROUNDS,))] * 6
        + [dma((LATENT_ROUNDS,))] * 4
        + [dma((3,)), dma((3,)), dma((N_LOCAL,))],
        compiler_params=pltpu.CompilerParams(
            collective_id=0, has_side_effects=True, vmem_limit_bytes=VMEM_LIMIT
        ),
        name="decoder_block",
    )(lengths, gain1, gain2, queries[0], cotangent[0], latents[0], q_w, k_w, v_w, o_w, u_w, d_w)
    block_out, query_grad, latent_grad, g_du, g_o, g_q, g_k, g_v = outs

    def by_rows(rows, columns):
        return pl.BlockSpec((rows // 2, columns), lambda i: (i, 0))

    by_columns = pl.BlockSpec((DL, DL // 2), lambda i: (0, i))
    whole = pl.BlockSpec((D,), lambda i: (0,))
    latent_spec = pl.BlockSpec((16, DL), lambda i: (0, 0))
    conv = pl.pallas_call(
        convert_kernel,
        out_shape=(
            sds((D, DL), F32),
            sds((DL, DL), F32),
            sds((DL, DL), F32),
            sds((DL, D), F32),
            sds((D, D), F32),
            sds((D, D), F32),
            sds((ROWS, D), BF16),
            sds((ROWS, D), F32),
            sds((16, DL), F32),
            sds((D,), F32),
            sds((D,), F32),
        ),
        grid=(2,),
        in_specs=[whole, whole]
        + [by_rows(*shape) for shape in ((D, 1536), (DL, D), (D, DL))]
        + [by_columns, by_columns]
        + [by_rows(*shape) for shape in ((D, D), (D, DL), (ROWS, D), (ROWS, D))]
        + [latent_spec],
        out_specs=tuple(
            by_rows(*shape)
            for shape in ((D, DL), (DL, DL), (DL, DL), (DL, D), (D, D), (D, D), (ROWS, D), (ROWS, D))
        )
        + (latent_spec, whole, whole),
        compiler_params=pltpu.CompilerParams(vmem_limit_bytes=VMEM_LIMIT),
        name="to_float32",
    )(
        gain1,
        gain2,
        g_du,
        g_o,
        g_q,
        g_k.reshape(DL, DL),
        g_v.reshape(DL, DL),
        u_w,
        q_w,
        block_out,
        query_grad,
        latent_grad,
    )
    q_grad, k_grad, v_grad, o_grad, u_grad, d_grad, block_out, query_grad, latent_grad, g1_grad, g2_grad = conv
    return (
        block_out[None],
        query_grad[None],
        latent_grad[None],
        q_grad,
        k_grad,
        v_grad,
        o_grad,
        u_grad,
        d_grad,
        g1_grad,
        g2_grad,
    )


def solution(mesh):
    rows = P("dp", "seq", None)
    in_specs = (rows, rows, P("dp", None)) + (P(),) * 8 + (rows,)
    out_specs = (rows, rows, rows) + (P(),) * 8
    return jax.shard_map(on_device, mesh=mesh, in_specs=in_specs, out_specs=out_specs, check_vma=False)
```
